128 devices in a mesh: blk: 16 (over z_hi, y, core), pair: 8 (over x, z_lo).
Axes of the slice: x: 4, y: 4, z: 4 (z_hi: 2, z_lo: 2; z = z_hi * 2 + z_lo), core: 2. Of those that a mesh axis runs over, the one named last changes fastest.
Arguments:
- density: float32 [160, 512, 256], P('pair', 'blk'), may hold values from 0.05 to 2
- agg_kernel: float32 [160, 160], replicated, may hold values from 0.00125 to 0.0125
- pair_share: float32 [160, 160], replicated, may hold values from 0 to 1
- pair_target: int32 [160, 160], replicated, may hold values from 0 to 158, as said below
- fragments: float32 [160, 160], replicated, may hold values from 0 to 0.025
- break_rate: float32 [160], replicated, may hold values from 0.05 to 0.4
- courant: float32 [160], replicated, may hold values from 0.2 to 0.9
- block_rows: int32 [16], replicated, may hold values from 1 to 32, 384 in all
- upstream: int32 [16], replicated, may hold values from 0 to 15, as said below
- face_map: int32 [16, 256], P('blk'), may hold values from 0 to 255, each once within a row
Outputs:
- updated: float32 [160, 512, 256], P('pair', 'blk')
The draws below stay inside these ranges and needn't reach their ends.
Inputs may be any that keep to these rules, and one draw needn't show every extreme that they name: `pair_target`: entry (i, j) lies from min(max(i, j), 158) to min(max(i, j) + 3, 158). `upstream`: the links form one cycle through all 16 blocks: every block feeds exactly one block and none feeds itself.
All inputs are finite; a program needn't handle non-finite values.
Results may differ from the reference program's by a relative error of at most 0.00043.
Values may be sent and summed in bfloat16 or wider, within the bound.
A program may use at most 128 MiB of HBM per device.

```python
import math
import jax
import jax.numpy as jnp
import numpy as np
from jax import lax

P_SIZE = 160
CH = 32
CW = 256
NB = 16


def draw_pair_target(key, part):
    pivot_ids = jnp.arange(P_SIZE, dtype=jnp.int32)
    offsets = jax.random.randint(key, (P_SIZE, P_SIZE), 0, 4, dtype=jnp.int32)
    larger = jnp.maximum(pivot_ids[:, None], pivot_ids[None, :])
    offsets = jnp.where(larger == 0, 0, offsets).astype(jnp.int32)
    return jnp.minimum(larger + offsets, P_SIZE - 2).astype(jnp.int32)


def draw_upstream(key, part):
    order = jax.random.permutation(key, NB).astype(jnp.int32)
    linked = jnp.zeros((NB,), jnp.int32).at[order].set(jnp.roll(order, 1))
    return linked.astype(jnp.int32)


def level_of(stream_key, extent, cuts, smallest, top_value):
    def one(axis_at, parts):
        steps = jax.random.uniform(jax.random.fold_in(jax.random.fold_in(stream_key, 6), axis_at), (parts,), jnp.float32, smallest / len(cuts), top_value / len(cuts))
        return jnp.repeat(jnp.exp(steps), extent[axis_at] // parts).reshape((-1,) + (1,) * (len(extent) - axis_at - 1))

    factor_of = one(*cuts[0])
    for cut in cuts[1:]:
        factor_of = factor_of * one(*cut)
    return factor_of


def split_up(count, total, reach, lean):
    weights = [(1 << 20) // math.isqrt(standing ** lean) + 1 for standing in range(2, count + 1)]
    surplus, given = total - reach - (count - 1), [1] * (count - 1)
    while surplus > 0:
        movable = [i for i in range(count - 1) if given[i] < reach]
        mass, remaining = sum([weights[i] for i in movable]), surplus
        for i in movable:
            more = min(reach - given[i], max(1, remaining * weights[i] // mass), surplus)
            given[i] = given[i] + more
            surplus = surplus - more
    return np.array([reach] + given)


def ragged(stream_key, count, total, bound, slope):
    if count == 2:
        one = jax.random.randint(stream_key, (), max(1, total - bound), min(bound, total - 1) + 1)
        return jnp.stack([one, total - one])
    lengths = jnp.asarray(split_up(count, total, bound, slope), jnp.int32)
    couples = (count - 1) // 2
    donor, receiver = lengths[1:1 + 2 * couples:2], lengths[2:2 + 2 * couples:2]
    margin = jnp.minimum(donor - 1, bound - receiver)
    moved = jax.random.randint(jax.random.fold_in(stream_key, 1), (couples,), 0, 1 << 20) % (margin + 1)
    lengths = lengths.at[1:1 + 2 * couples:2].set(donor - moved).at[2:2 + 2 * couples:2].set(receiver + moved)
    return lengths[jax.random.permutation(jax.random.fold_in(stream_key, 2), count)]


def setup_inputs(seed: int = 0) -> dict:
    streams_of = jax.random.split(jax.random.key(seed), 11)
    return {
        "density": jnp.clip(jnp.exp(math.log(2.0) - 3.6888794 * jax.random.uniform(streams_of[0], (P_SIZE, NB * CH, CW), jnp.float32) ** level_of(streams_of[0], (P_SIZE, NB * CH, CW), ((0, 8), (1, 16)), -0.2, 0.2)), 0.05, 2.0),
        "agg_kernel": jnp.clip(jnp.exp(jax.random.uniform(streams_of[1], (P_SIZE, P_SIZE), jnp.float32, math.log(0.00125), math.log(0.0125))), 0.00125, 0.0125),
        "pair_share": jnp.clip(jax.random.uniform(streams_of[2], (P_SIZE, P_SIZE), jnp.float32, 0.0, 1.0), 0.0, 1.0),
        "pair_target": draw_pair_target(jax.random.fold_in(streams_of[10], 71), 0),
        "fragments": jnp.clip(jax.random.uniform(streams_of[4], (P_SIZE, P_SIZE), jnp.float32, 0.0, 0.025), 0.0, 0.025),
        "break_rate": jnp.clip(jnp.exp(jax.random.uniform(streams_of[5], (P_SIZE,), jnp.float32, math.log(0.05), math.log(0.4))), 0.05, 0.4),
        "courant": jnp.clip(jnp.exp(jax.random.uniform(streams_of[6], (P_SIZE,), jnp.float32, math.log(0.2), math.log(0.9))), 0.2, 0.9),
        "block_rows": ragged(streams_of[7], NB, NB * CH * 3 // 4, CH, 2).astype(jnp.int32),
        "upstream": draw_upstream(jax.random.fold_in(streams_of[10], 71), 0),
        "face_map": jax.vmap(lambda own: jax.random.permutation(own, CW))(jax.random.split(streams_of[9], NB)).reshape((NB, CW)).astype(jnp.int32),
    }


def pair_births(vb_flat, agg_kernel, pair_share, pair_target):
    pivot_ids = jnp.arange(P_SIZE, dtype=jnp.int32)
    dense = vb_flat.astype(jnp.float32)

    def one_partner(running, first_id):
        kern_row = agg_kernel[first_id]
        share_row = pair_share[first_id]
        target_row = pair_target[first_id]
        first_hit = (pivot_ids[:, None] == target_row[None, :]).astype(jnp.float32)
        second_hit = (pivot_ids[:, None] == target_row[None, :] + 1).astype(jnp.float32)
        weights = 0.5 * kern_row[None, :] * (share_row[None, :] * first_hit + (1.0 - share_row[None, :]) * second_hit)
        weights = weights.astype(jnp.bfloat16).astype(jnp.float32)
        inner = jnp.dot(weights, dense, preferred_element_type=jnp.float32)
        return running + dense[first_id][None, :] * inner, None

    running, _ = lax.scan(one_partner, jnp.zeros(dense.shape, jnp.float32), pivot_ids)
    return running


def reference(density, agg_kernel, pair_share, pair_target, fragments, break_rate, courant, block_rows, upstream, face_map):
    pivot_ids = jnp.arange(P_SIZE, dtype=jnp.int32)
    smaller = (pivot_ids[:, None] < pivot_ids[None, :]).astype(jnp.float32)
    frag_b = (fragments * break_rate[None, :] * smaller).astype(jnp.bfloat16)
    kern_b = agg_kernel.astype(jnp.bfloat16)
    live = (jnp.arange(CH, dtype=jnp.int32)[None, :] < block_rows[:, None])[None, :, :, None]

    def tendency(field_now):
        flat = field_now.reshape(P_SIZE, NB * CH * CW)
        vb_flat = flat.astype(jnp.bfloat16)
        births = pair_births(vb_flat, agg_kernel, pair_share, pair_target)
        loss = jnp.dot(kern_b, vb_flat, preferred_element_type=jnp.float32)
        gain = jnp.dot(frag_b, vb_flat, preferred_element_type=jnp.float32)
        source = births - flat * loss + gain - break_rate[:, None] * flat
        top_index = jnp.broadcast_to((block_rows - 1).astype(jnp.int32)[None, :, None, None], (P_SIZE, NB, 1, CW))
        tops = jnp.take_along_axis(field_now, top_index, axis=2)[:, :, 0, :]
        arrived = tops[:, upstream, :]
        column_index = jnp.broadcast_to(face_map[None, :, :], (P_SIZE, NB, CW))
        inflow = jnp.take_along_axis(arrived, column_index, axis=2)
        previous = jnp.concatenate([inflow[:, :, None, :], field_now[:, :, :-1, :]], axis=2)
        return -courant[:, None, None, None] * (field_now - previous) + source.reshape(P_SIZE, NB, CH, CW)

    start_field = density.reshape(P_SIZE, NB, CH, CW)
    section = jnp.where(live, start_field + tendency(start_field), 0.0)
    final = jnp.where(live, 0.5 * start_field + 0.5 * (section + tendency(section)), 0.0)
    return final.reshape(P_SIZE, NB * CH, CW)
```

```python
import functools

import jax
import jax.numpy as jnp
from jax import lax
from jax.experimental import pallas as pl
from jax.experimental.pallas import tpu as pltpu
from jax.sharding import PartitionSpec as P

MESH = pl.DeviceIdType.MESH
BANDS = 5
F32 = jnp.float32
BF16 = jnp.bfloat16


def permuted(face, one_hot):
    total = None
    for _ in range(3):
        part = face.astype(BF16)
        face = face - part.astype(F32)
        moved = jnp.dot(part, one_hot, preferred_element_type=F32)
        total = moved if total is None else total + moved
    return total


def step_kernel(
    n_blk, n_pair, own, piv, height, width,
    density, agg, share, target, frag, rate, cour, rows_sm, up_sm, face_map,
    main, add,
    dens_v, v0, sec, out, wb, y_s, faces, faces2, halo_s, halo_r, halo_c, edge_r, top_s, top_p, top_r,
    local_sem, main_send, main_recv, face_send, face_recv, face2_send, face2_recv,
    halo_send, halo_recv, edge_send, edge_recv, top_send, top_recv, out_send, out_recv,
):
    me_b, me_p = lax.axis_index("blk"), lax.axis_index("pair")
    grp, half = me_p // 2, me_p % 2
    pairs = [lax.rem(me_p + d, n_pair) for d in range(n_pair)]
    blks = [lax.rem(me_b + d, n_blk) for d in range(n_blk)]

    def tile_of(ref, p):
        return ref.at[:, pl.ds(pl.multiple_of((p // 2) * 8, 8), 8), pl.ds(pl.multiple_of((p % 2) * 128, 128), 128)]

    loads = [pltpu.make_async_copy(density.at[:, :, pl.ds(t * 128, 128)], dens_v.at[t], local_sem.at[5 + t])
             for t in range(2)]
    for load in loads:
        load.start()
    load_own = pltpu.make_async_copy(tile_of(density, me_p), v0.at[pl.ds(me_p * own, own)], local_sem.at[1])
    load_own.start()

    barrier = pltpu.get_barrier_semaphore()
    for d in range(1, n_pair):
        pl.semaphore_signal(barrier, inc=1, device_id=(me_b, pairs[d]), device_id_type=MESH)
    for d in range(1, n_blk):
        pl.semaphore_signal(barrier, inc=1, device_id=(blks[d], me_p), device_id_type=MESH)
    pl.semaphore_wait(barrier, n_pair + n_blk - 2)

    def to_pair(d, src, dst, send, recv):
        return pltpu.make_async_remote_copy(
            src_ref=src, dst_ref=dst, send_sem=send.at[d], recv_sem=recv.at[d],
            device_id=(me_b, pairs[d]), device_id_type=MESH)

    def to_blk(d, src, dst, send, recv):
        return pltpu.make_async_remote_copy(
            src_ref=src, dst_ref=dst, send_sem=send.at[d], recv_sem=recv.at[d],
            device_id=(blks[d], me_p), device_id_type=MESH)

    main_in = [to_pair(d, tile_of(density, pairs[d]), v0.at[pl.ds(me_p * own, own)], main_send, main_recv)
               for d in range(1, n_pair)]
    for copy in main_in:
        copy.start()

    for load in loads:
        load.wait()
    dens_rows = dens_v.reshape(2 * own * height, 128)
    for t in range(2):
        faces[me_b, :, pl.ds(t * 128, 128)] = dens_rows[
            pl.ds(jnp.maximum(rows_sm[me_b] - 1, 0) + t * own * height, own, stride=height), :]
    faces_out = [to_blk(d, faces.at[me_b], faces.at[me_b], face_send, face_recv) for d in range(1, n_blk)]
    for copy in faces_out:
        copy.start()
    for q in range(1, height // 8):
        for t in range(2):
            halo_s[q, :, pl.ds(t * 128, 128)] = dens_rows[
                pl.ds(8 * q - 1 + t * own * height, own, stride=height), :]

    row_id = lax.broadcasted_iota(jnp.int32, (piv, piv), 0)
    col_id = lax.broadcasted_iota(jnp.int32, (piv, piv), 1)
    kern = agg[...]
    part = share[...]
    low = (0.5 * kern * part).astype(BF16).astype(F32)
    high = (0.5 * kern * (1.0 - part)).astype(BF16).astype(F32)
    offset = (target[...] - jnp.maximum(row_id, col_id)).astype(F32)
    last = []
    for n, (lo, hi, off, keep) in enumerate((
        (low, high, offset, col_id <= row_id),
        (low.T, high.T, offset.T, col_id < row_id),
    )):
        for d in range(BANDS):
            band = jnp.where(off == d, lo, jnp.where(off == d - 1, hi, 0.0))
            wb[pl.ds((n * BANDS + d) * piv, piv), :] = jnp.where(keep, band, 0.0).astype(BF16)
        last.append(pltpu.roll(jnp.where(keep & (off == -1), lo, 0.0)[piv - 8:], 7, 0))
    rate_row = rate[...]
    base = 2 * BANDS * piv
    wb[pl.ds(base, piv), :] = kern.astype(BF16)
    wb[pl.ds(base + 2 * piv, 16), :] = jnp.concatenate(last, axis=0).astype(BF16)
    smaller = (row_id < col_id).astype(F32)
    wb[pl.ds(base + piv, piv), :] = (frag[...] * rate_row * smaller).astype(BF16)
    diag = row_id == col_id
    rate_col = jnp.sum(jnp.where(diag, rate_row, 0.0), axis=1, keepdims=True)
    cour_col = jnp.sum(jnp.where(diag, cour[...], 0.0), axis=1, keepdims=True)

    one_hot = (lax.broadcasted_iota(jnp.int32, (width, width), 0) == face_map[...]).astype(F32).astype(BF16)

    for copy in faces_out:
        copy.wait_recv()
    halo_s[0] = permuted(faces[up_sm[me_b]], one_hot)

    def halo_of(p):
        return halo_s.at[p // 2, :, pl.ds(pl.multiple_of((p % 2) * 128, 128), 128)]

    halos = [to_pair(d, halo_of(pairs[d]), halo_r.at[me_p], halo_send, halo_recv) for d in range(1, n_pair)]
    for copy in halos:
        copy.start()
    halo_own = pltpu.make_async_copy(halo_of(me_p), halo_r.at[me_p], local_sem.at[2])
    halo_own.start()

    live_rows = rows_sm[me_b]
    top_row = live_rows - 1

    def change(v, prev):
        y_s[...] = jnp.dot(wb[...], v.astype(BF16), preferred_element_type=F32)
        vb = v.astype(BF16).astype(F32)
        below = y_s[pl.ds(base + 2 * piv, 8), :] + y_s[pl.ds(base + 2 * piv + 8, 8), :]
        y_s[pl.ds(base + 2 * piv - 8, 8), :] += below * vb[piv - 1:]
        births = None
        for d in reversed(range(BANDS)):
            here = vb * (y_s[pl.ds(d * piv, piv), :] + y_s[pl.ds((BANDS + d) * piv, piv), :])
            births = here if births is None else here + pltpu.roll(births, 1, 0)
        loss = y_s[pl.ds(base, piv), :]
        gain = y_s[pl.ds(base + piv, piv), :]
        source = births - v * loss + gain - rate_col * v
        return v + (source - cour_col * (v - prev))

    v0_rows = v0.reshape(piv * 8, 128)
    out_rows = out.reshape(piv * 8, 128)

    def start_row(s):
        return v0_rows[pl.ds(s, piv, stride=8), :]

    load_own.wait()
    for copy in main_in:
        copy.wait_recv()

    top = None
    edge = to_pair(
        2, sec.at[:, pl.ds(7 * 128, 128)], edge_r, edge_send, edge_recv)
    for it in reversed(range(4)):
        s = 2 * it
        if it == 0:
            halo_own.wait()
            for copy in halos:
                copy.wait_recv()
            for p in range(n_pair):
                halo_c[pl.ds(p * own, own), :] = halo_r[p]
            before = halo_c[...]
        else:
            before = start_row(s - 1)
        first, second = start_row(s), start_row(s + 1)
        now = change(jnp.concatenate([first, second], axis=1), jnp.concatenate([before, first], axis=1))
        for t in range(2):
            row = grp * 8 + s + t
            piece = jnp.where(row < live_rows, now[:, t * 128:(t + 1) * 128], 0.0)
            sec[:, pl.ds((s + t) * 128, 128)] = piece
            mine = jnp.where(row == top_row, piece, 0.0)
            top = mine if top is None else top + mine
        if it == 3:
            edge.start()

    top_s[...] = 0.5 * cour_col * top
    for p in range(n_pair):
        top_p[p] = top_s[pl.ds(p * own, own), :]
    tops = [to_pair(d, top_p.at[pairs[d]], top_r.at[me_p], top_send, top_recv) for d in range(1, n_pair)]
    for copy in tops:
        copy.start()
    top_own = pltpu.make_async_copy(top_p.at[me_p], top_r.at[me_p], local_sem.at[3])
    top_own.start()

    for it in reversed(range(4)):
        s = 2 * it
        if it == 0:
            top_own.wait()
            for copy in tops:
                copy.wait_recv()
            for t in range(2):
                faces2[me_b, :, pl.ds(t * 128, 128)] = (top_r[t] + top_r[t + 2]) + (top_r[t + 4] + top_r[t + 6])
            faces2_out = [to_blk(d, faces2.at[me_b], faces2.at[me_b], face2_send, face2_recv)
                          for d in range(1, n_blk)]
            for copy in faces2_out:
                copy.start()
            edge.wait_recv()
            before = jnp.where(grp > 0, edge_r[...], 0.0)
        else:
            before = sec[:, pl.ds((s - 1) * 128, 128)]
        v = sec[:, pl.ds(s * 128, 256)]
        now = change(v, jnp.concatenate([before, v[:, :128]], axis=1))
        for t in range(2):
            row = grp * 8 + s + t
            piece = 0.5 * start_row(s + t) + 0.5 * now[:, t * 128:(t + 1) * 128]
            out_rows[pl.ds(s + t, piv, stride=8), :] = jnp.where(row < live_rows, piece, 0.0)

    outs = [to_pair(d, out.at[pl.ds(pairs[d] * own, own)], tile_of(main, me_p), out_send, out_recv)
            for d in range(1, n_pair)]
    for copy in outs:
        copy.start()
    out_own = pltpu.make_async_copy(out.at[pl.ds(me_p * own, own)], tile_of(main, me_p), local_sem.at[4])
    out_own.start()

    for copy in faces2_out:
        copy.wait_recv()
    add[...] = permuted(faces2[up_sm[me_b]], one_hot)

    out_own.wait()
    for copy in outs:
        copy.wait_recv()
    for copy in main_in + faces_out + halos + [edge] + tops + faces2_out + outs:
        copy.wait_send()


def shards(n_blk, n_pair, density, agg, share, target, frag, rate, cour, block_rows, upstream, face_map):
    own, height, width = density.shape
    piv = agg.shape[0]
    vmem = pl.BlockSpec(memory_space=pltpu.VMEM)
    smem = pl.BlockSpec(memory_space=pltpu.SMEM)
    hbm = pl.BlockSpec(memory_space=pl.ANY)
    dma = pltpu.SemaphoreType.DMA
    main, add = pl.pallas_call(
        functools.partial(step_kernel, n_blk, n_pair, own, piv, height, width),
        out_shape=(
            jax.ShapeDtypeStruct(density.shape, F32),
            jax.ShapeDtypeStruct((own, width), F32),
        ),
        in_specs=[hbm] + [vmem] * 6 + [smem] * 2 + [vmem],
        out_specs=(hbm, vmem),
        scratch_shapes=[
            pltpu.VMEM((2, own, height, 128), F32),
            pltpu.VMEM((piv, 8, 128), F32),
            pltpu.VMEM((piv, 1024), F32),
            pltpu.VMEM((piv, 8, 128), F32),
            pltpu.VMEM(((2 * BANDS + 2) * piv + 16, piv), BF16),
            pltpu.VMEM(((2 * BANDS + 2) * piv + 16, 256), F32),
            pltpu.VMEM((n_blk, own, width), F32),
            pltpu.VMEM((n_blk, own, width), F32),
            pltpu.VMEM((height // 8, own, width), F32),
            pltpu.VMEM((n_pair, own, 128), F32),
            pltpu.VMEM((piv, 128), F32),
            pltpu.VMEM((piv, 128), F32),
            pltpu.VMEM((piv, 128), F32),
            pltpu.VMEM((n_pair, own, 128), F32),
            pltpu.VMEM((n_pair, own, 128), F32),
            dma((7,)),
            dma((n_pair,)), dma((n_pair,)),
            dma((n_blk,)), dma((n_blk,)),
            dma((n_blk,)), dma((n_blk,)),
            dma((n_pair,)), dma((n_pair,)),
            dma((n_pair,)), dma((n_pair,)),
            dma((n_pair,)), dma((n_pair,)),
            dma((n_pair,)), dma((n_pair,)),
        ],
        compiler_params=pltpu.CompilerParams(
            collective_id=0, has_side_effects=True, vmem_limit_bytes=40 * 1024 * 1024),
    )(density, agg, share, target, frag, rate.reshape(1, piv), cour.reshape(1, piv), block_rows, upstream, face_map)
    bottom = lax.broadcasted_iota(jnp.int32, main.shape, 1) == 0
    return jnp.where(bottom, main + add[:, None, :], main)


def solution(mesh):
    in_specs = (P("pair", "blk", None), P(), P(), P(), P(), P(), P(), P(), P(), P("blk", None))
    out_specs = P("pair", "blk", None)
    return jax.shard_map(
        functools.partial(shards, mesh.shape["blk"], mesh.shape["pair"]),
        mesh=mesh, in_specs=in_specs, out_specs=out_specs, check_vma=False)
```

```python
import functools

import jax
import jax.numpy as jnp
from jax import lax
from jax.experimental import pallas as pl
from jax.experimental.pallas import tpu as pltpu
from jax.sharding import PartitionSpec as P

MESH = pl.DeviceIdType.MESH
BANDS = 5
F32 = jnp.float32
BF16 = jnp.bfloat16


def permuted(face, one_hot):
    total = None
    for _ in range(3):
        part = face.astype(BF16)
        face = face - part.astype(F32)
        moved = jnp.dot(part, one_hot, preferred_element_type=F32)
        total = moved if total is None else total + moved
    return total


def step_kernel(
    n_blk, n_pair, own, piv, height, width,
    density, agg_h, share_h, target_h, frag_h, rate, cour, rows_sm, up_sm, face_map,
    main, add,
    agg, share, target, frag, dens_v, v0, sec, out, wb, y_s, faces, faces2, halo_s, halo_r, halo_c, edge_r, top_s, top_p, top_r,
    local_sem, main_send, main_recv, face_send, face_recv, face2_send, face2_recv,
    halo_send, halo_recv, edge_send, edge_recv, top_send, top_recv, out_send, out_recv,
):
    me_b, me_p = lax.axis_index("blk"), lax.axis_index("pair")
    grp, half = me_p // 2, me_p % 2
    pairs = [lax.rem(me_p + d, n_pair) for d in range(n_pair)]
    blks = [lax.rem(me_b + d, n_blk) for d in range(n_blk)]

    def tile_of(ref, p):
        return ref.at[:, pl.ds(pl.multiple_of((p // 2) * 8, 8), 8), pl.ds(pl.multiple_of((p % 2) * 128, 128), 128)]

    loads = [pltpu.make_async_copy(density.at[:, :, pl.ds(t * 128, 128)], dens_v.at[t], local_sem.at[5 + t])
             for t in range(2)]
    for load in loads:
        load.start()
    load_own = pltpu.make_async_copy(tile_of(density, me_p), v0.at[pl.ds(me_p * own, own)], local_sem.at[1])
    load_own.start()
    tables = [pltpu.make_async_copy(src, dst, local_sem.at[7 + n]) for n, (src, dst) in enumerate(
        ((agg_h, agg), (share_h, share), (target_h, target), (frag_h, frag)))]
    for load in tables:
        load.start()

    barrier = pltpu.get_barrier_semaphore()
    for d in range(1, n_pair):
        pl.semaphore_signal(barrier, inc=1, device_id=(me_b, pairs[d]), device_id_type=MESH)
    for d in range(1, n_blk):
        pl.semaphore_signal(barrier, inc=1, device_id=(blks[d], me_p), device_id_type=MESH)
    pl.semaphore_wait(barrier, n_pair + n_blk - 2)

    def to_pair(d, src, dst, send, recv):
        return pltpu.make_async_remote_copy(
            src_ref=src, dst_ref=dst, send_sem=send.at[d], recv_sem=recv.at[d],
            device_id=(me_b, pairs[d]), device_id_type=MESH)

    def to_blk(d, src, dst, send, recv):
        return pltpu.make_async_remote_copy(
            src_ref=src, dst_ref=dst, send_sem=send.at[d], recv_sem=recv.at[d],
            device_id=(blks[d], me_p), device_id_type=MESH)

    main_in = [to_pair(d, tile_of(density, pairs[d]), v0.at[pl.ds(me_p * own, own)], main_send, main_recv)
               for d in range(1, n_pair)]
    for copy in main_in:
        copy.start()

    for load in loads:
        load.wait()
    dens_rows = dens_v.reshape(2 * own * height, 128)
    for t in range(2):
        faces[me_b, :, pl.ds(t * 128, 128)] = dens_rows[
            pl.ds(jnp.maximum(rows_sm[me_b] - 1, 0) + t * own * height, own, stride=height), :]
    faces_out = [to_blk(d, faces.at[me_b], faces.at[me_b], face_send, face_recv) for d in range(1, n_blk)]
    for copy in faces_out:
        copy.start()
    for q in range(1, height // 8):
        for t in range(2):
            halo_s[q, :, pl.ds(t * 128, 128)] = dens_rows[
                pl.ds(8 * q - 1 + t * own * height, own, stride=height), :]

    for load in tables:
        load.wait()
    row_id = lax.broadcasted_iota(jnp.int32, (piv, piv), 0)
    col_id = lax.broadcasted_iota(jnp.int32, (piv, piv), 1)
    kern = agg[...]
    part = share[...]
    low = (0.5 * kern * part).astype(BF16).astype(F32)
    high = (0.5 * kern * (1.0 - part)).astype(BF16).astype(F32)
    offset = (target[...] - jnp.maximum(row_id, col_id)).astype(F32)
    last = []
    for n, (lo, hi, off, keep) in enumerate((
        (low, high, offset, col_id <= row_id),
        (low.T, high.T, offset.T, col_id < row_id),
    )):
        for d in range(BANDS):
            band = jnp.where(off == d, lo, jnp.where(off == d - 1, hi, 0.0))
            wb[pl.ds((n * BANDS + d) * piv, piv), :] = jnp.where(keep, band, 0.0).astype(BF16)
        last.append(pltpu.roll(jnp.where(keep & (off == -1), lo, 0.0)[piv - 8:], 7, 0))
    rate_row = rate[...]
    base = 2 * BANDS * piv
    wb[pl.ds(base, piv), :] = kern.astype(BF16)
    wb[pl.ds(base + 2 * piv, 16), :] = jnp.concatenate(last, axis=0).astype(BF16)
    smaller = (row_id < col_id).astype(F32)
    wb[pl.ds(base + piv, piv), :] = (frag[...] * rate_row * smaller).astype(BF16)
    diag = row_id == col_id
    rate_col = jnp.sum(jnp.where(diag, rate_row, 0.0), axis=1, keepdims=True)
    cour_col = jnp.sum(jnp.where(diag, cour[...], 0.0), axis=1, keepdims=True)

    one_hot = (lax.broadcasted_iota(jnp.int32, (width, width), 0) == face_map[...]).astype(F32).astype(BF16)

    for copy in faces_out:
        copy.wait_recv()
    halo_s[0] = permuted(faces[up_sm[me_b]], one_hot)

    def halo_of(p):
        return halo_s.at[p // 2, :, pl.ds(pl.multiple_of((p % 2) * 128, 128), 128)]

    halos = [to_pair(d, halo_of(pairs[d]), halo_r.at[me_p], halo_send, halo_recv) for d in range(1, n_pair)]
    for copy in halos:
        copy.start()
    halo_own = pltpu.make_async_copy(halo_of(me_p), halo_r.at[me_p], local_sem.at[2])
    halo_own.start()

    live_rows = rows_sm[me_b]
    top_row = live_rows - 1

    def change(v, prev):
        y_s[...] = jnp.dot(wb[...], v.astype(BF16), preferred_element_type=F32)
        vb = v.astype(BF16).astype(F32)
        below = y_s[pl.ds(base + 2 * piv, 8), :] + y_s[pl.ds(base + 2 * piv + 8, 8), :]
        y_s[pl.ds(base + 2 * piv - 8, 8), :] += below * vb[piv - 1:]
        births = None
        for d in reversed(range(BANDS)):
            here = vb * (y_s[pl.ds(d * piv, piv), :] + y_s[pl.ds((BANDS + d) * piv, piv), :])
            births = here if births is None else here + pltpu.roll(births, 1, 0)
        loss = y_s[pl.ds(base, piv), :]
        gain = y_s[pl.ds(base + piv, piv), :]
        source = births - v * loss + gain - rate_col * v
        return v + (source - cour_col * (v - prev))

    v0_rows = v0.reshape(piv * 8, 128)
    out_rows = out.reshape(piv * 8, 128)

    def start_row(s):
        return v0_rows[pl.ds(s, piv, stride=8), :]

    load_own.wait()
    for copy in main_in:
        copy.wait_recv()

    top = None
    edge = to_pair(
        2, sec.at[:, pl.ds(7 * 128, 128)], edge_r, edge_send, edge_recv)
    for it in reversed(range(4)):
        s = 2 * it
        if it == 0:
            halo_own.wait()
            for copy in halos:
                copy.wait_recv()
            for p in range(n_pair):
                halo_c[pl.ds(p * own, own), :] = halo_r[p]
            before = halo_c[...]
        else:
            before = start_row(s - 1)
        first, second = start_row(s), start_row(s + 1)
        now = change(jnp.concatenate([first, second], axis=1), jnp.concatenate([before, first], axis=1))
        for t in range(2):
            row = grp * 8 + s + t
            piece = jnp.where(row < live_rows, now[:, t * 128:(t + 1) * 128], 0.0)
            sec[:, pl.ds((s + t) * 128, 128)] = piece
            mine = jnp.where(row == top_row, piece, 0.0)
            top = mine if top is None else top + mine
        if it == 3:
            edge.start()

    top_s[...] = 0.5 * cour_col * top
    for p in range(n_pair):
        top_p[p] = top_s[pl.ds(p * own, own), :]
    tops = [to_pair(d, top_p.at[pairs[d]], top_r.at[me_p], top_send, top_recv) for d in range(1, n_pair)]
    for copy in tops:
        copy.start()
    top_own = pltpu.make_async_copy(top_p.at[me_p], top_r.at[me_p], local_sem.at[3])
    top_own.start()

    for it in reversed(range(4)):
        s = 2 * it
        if it == 0:
            top_own.wait()
            for copy in tops:
                copy.wait_recv()
            for t in range(2):
                faces2[me_b, :, pl.ds(t * 128, 128)] = (top_r[t] + top_r[t + 2]) + (top_r[t + 4] + top_r[t + 6])
            faces2_out = [to_blk(d, faces2.at[me_b], faces2.at[me_b], face2_send, face2_recv)
                          for d in range(1, n_blk)]
            for copy in faces2_out:
                copy.start()
            edge.wait_recv()
            before = jnp.where(grp > 0, edge_r[...], 0.0)
        else:
            before = sec[:, pl.ds((s - 1) * 128, 128)]
        v = sec[:, pl.ds(s * 128, 256)]
        now = change(v, jnp.concatenate([before, v[:, :128]], axis=1))
        for t in range(2):
            row = grp * 8 + s + t
            piece = 0.5 * start_row(s + t) + 0.5 * now[:, t * 128:(t + 1) * 128]
            out_rows[pl.ds(s + t, piv, stride=8), :] = jnp.where(row < live_rows, piece, 0.0)

    outs = [to_pair(d, out.at[pl.ds(pairs[d] * own, own)], tile_of(main, me_p), out_send, out_recv)
            for d in range(1, n_pair)]
    for copy in outs:
        copy.start()
    out_own = pltpu.make_async_copy(out.at[pl.ds(me_p * own, own)], tile_of(main, me_p), local_sem.at[4])
    out_own.start()

    for copy in faces2_out:
        copy.wait_recv()
    add[...] = permuted(faces2[up_sm[me_b]], one_hot)

    out_own.wait()
    for copy in outs:
        copy.wait_recv()
    for copy in main_in + faces_out + halos + [edge] + tops + faces2_out + outs:
        copy.wait_send()


def shards(n_blk, n_pair, density, agg, share, target, frag, rate, cour, block_rows, upstream, face_map):
    own, height, width = density.shape
    piv = agg.shape[0]
    vmem = pl.BlockSpec(memory_space=pltpu.VMEM)
    smem = pl.BlockSpec(memory_space=pltpu.SMEM)
    hbm = pl.BlockSpec(memory_space=pltpu.HBM)
    dma = pltpu.SemaphoreType.DMA
    main, add = pl.pallas_call(
        functools.partial(step_kernel, n_blk, n_pair, own, piv, height, width),
        out_shape=(
            jax.ShapeDtypeStruct(density.shape, F32),
            jax.ShapeDtypeStruct((own, width), F32),
        ),
        in_specs=[hbm] * 5 + [vmem] * 2 + [smem] * 2 + [vmem],
        out_specs=(hbm, vmem),
        scratch_shapes=[
            pltpu.VMEM((piv, piv), F32),
            pltpu.VMEM((piv, piv), F32),
            pltpu.VMEM((piv, piv), jnp.int32),
            pltpu.VMEM((piv, piv), F32),
            pltpu.VMEM((2, own, height, 128), F32),
            pltpu.VMEM((piv, 8, 128), F32),
            pltpu.VMEM((piv, 1024), F32),
            pltpu.VMEM((piv, 8, 128), F32),
            pltpu.VMEM(((2 * BANDS + 2) * piv + 16, piv), BF16),
            pltpu.VMEM(((2 * BANDS + 2) * piv + 16, 256), F32),
            pltpu.VMEM((n_blk, own, width), F32),
            pltpu.VMEM((n_blk, own, width), F32),
            pltpu.VMEM((height // 8, own, width), F32),
            pltpu.VMEM((n_pair, own, 128), F32),
            pltpu.VMEM((piv, 128), F32),
            pltpu.VMEM((piv, 128), F32),
            pltpu.VMEM((piv, 128), F32),
            pltpu.VMEM((n_pair, own, 128), F32),
            pltpu.VMEM((n_pair, own, 128), F32),
            dma((11,)),
            dma((n_pair,)), dma((n_pair,)),
            dma((n_blk,)), dma((n_blk,)),
            dma((n_blk,)), dma((n_blk,)),
            dma((n_pair,)), dma((n_pair,)),
            dma((n_pair,)), dma((n_pair,)),
            dma((n_pair,)), dma((n_pair,)),
            dma((n_pair,)), dma((n_pair,)),
        ],
        compiler_params=pltpu.CompilerParams(
            collective_id=0, has_side_effects=True, vmem_limit_bytes=56 * 1024 * 1024),
    )(density, agg, share, target, frag, rate.reshape(1, piv), cour.reshape(1, piv), block_rows, upstream, face_map)
    bottom = lax.broadcasted_iota(jnp.int32, main.shape, 1) == 0
    return jnp.where(bottom, main + add[:, None, :], main)


def solution(mesh):
    in_specs = (P("pair", "blk", None), P(), P(), P(), P(), P(), P(), P(), P(), P("blk", None))
    out_specs = P("pair", "blk", None)
    return jax.shard_map(
        functools.partial(shards, mesh.shape["blk"], mesh.shape["pair"]),
        mesh=mesh, in_specs=in_specs, out_specs=out_specs, check_vma=False)
```

```python
import functools

import jax
import jax.numpy as jnp
from jax import lax
from jax.experimental import pallas as pl
from jax.experimental.pallas import tpu as pltpu
from jax.sharding import PartitionSpec as P

MESH = pl.DeviceIdType.MESH
BANDS = 5
F32 = jnp.float32
BF16 = jnp.bfloat16
I16 = jnp.int16
RING, CORES = 4, 2
MIDDLE = 1.025
STEP = 1.95 / 65534.0


def permuted(face, one_hot):
    total = None
    for _ in range(3):
        part = face.astype(BF16)
        face = face - part.astype(F32)
        moved = jnp.dot(part, one_hot, preferred_element_type=F32)
        total = moved if total is None else total + moved
    return total


def rounded16(x):
    return jnp.round(x).astype(jnp.int32).astype(I16)


def step_kernel(
    n_pair, own, piv, height, width,
    density, agg_h, share_h, target_h, frag_h, rate, cour, rows_sm, up_sm, face_map,
    main,
    agg, share, target, frag, dens_v, enc, got, v0, sec, res, out_f, out_s, out_r, wb, y_s,
    ring, picked, picked_r, ring2, picked2, picked2_r,
    halo_s, halo_r, halo_c, inflow_s, inflow_r, edge_r, top_s, top_p, top_r, scale_p, scale_r,
    local_sem, main_send, main_recv, halo_send, halo_recv, inflow_send, inflow_recv,
    ring_send, ring_recv, pick_send, pick_recv, ring2_send, ring2_recv, pick2_send, pick2_recv,
    edge_send, edge_recv, top_send, top_recv, out_send, out_recv, scale_send, scale_recv,
):
    me_b, me_p = lax.axis_index("blk"), lax.axis_index("pair")
    grp = me_p // 2
    z_hi, y, core = me_b // (RING * CORES), (me_b // CORES) % RING, me_b % CORES
    pairs = [(me_p + d) % n_pair for d in range(n_pair)]

    def block_at(dz, dy, dc):
        return ((z_hi + dz) % 2) * (RING * CORES) + ((y + dy) % RING) * CORES + (core + dc) % CORES

    ring_mates = [block_at(0, d, 0) for d in range(RING)]
    pick_mates = [block_at(q // 2, 0, q % 2) for q in range(4)]

    loads = [pltpu.make_async_copy(density.at[:, :, pl.ds(t * 128, 128)], dens_v.at[t], local_sem.at[t])
             for t in range(2)]
    for load in loads:
        load.start()
    tables = [pltpu.make_async_copy(src, dst, local_sem.at[2 + n]) for n, (src, dst) in enumerate(
        ((agg_h, agg), (share_h, share), (target_h, target), (frag_h, frag)))]
    for load in tables:
        load.start()

    barrier = pltpu.get_barrier_semaphore()
    for p in pairs[1:]:
        pl.semaphore_signal(barrier, inc=1, device_id=(me_b, p), device_id_type=MESH)
    for b in ring_mates[1:] + pick_mates[1:]:
        pl.semaphore_signal(barrier, inc=1, device_id=(b, me_p), device_id_type=MESH)

    def to_pair(d, src, dst, send, recv):
        return pltpu.make_async_remote_copy(
            src_ref=src, dst_ref=dst, send_sem=send.at[d], recv_sem=recv.at[d],
            device_id=(me_b, pairs[d]), device_id_type=MESH)

    def to_block(b, d, src, dst, send, recv):
        return pltpu.make_async_remote_copy(
            src_ref=src, dst_ref=dst, send_sem=send.at[d], recv_sem=recv.at[d],
            device_id=(b, me_p), device_id_type=MESH)

    live_rows = rows_sm[me_b]
    top_row = live_rows - 1
    for load in loads:
        load.wait()
    dens_rows = dens_v.reshape(2 * own * height, 128)
    for t in range(2):
        at = t * own * height
        ring[y, :, pl.ds(t * 128, 128)] = dens_rows[pl.ds(jnp.maximum(top_row, 0) + at, own, stride=height), :]
        halo_s[t] = jnp.zeros((own, 128), F32)
        for q in range(1, height // 8):
            halo_s[2 * q + t] = dens_rows[pl.ds(8 * q - 1 + at, own, stride=height), :]
    for p in range(n_pair):
        tile = dens_v[p % 2, :, pl.ds((p // 2) * 8, 8), :].reshape(own * 8, 128)
        enc[p] = rounded16((tile - MIDDLE) * (1.0 / STEP))

    for load in tables:
        load.wait()
    row_id = lax.broadcasted_iota(jnp.int32, (piv, piv), 0)
    col_id = lax.broadcasted_iota(jnp.int32, (piv, piv), 1)
    kern = agg[...]
    part = share[...]
    low = (0.5 * kern * part).astype(BF16).astype(F32)
    high = (0.5 * kern * (1.0 - part)).astype(BF16).astype(F32)
    offset = (target[...] - jnp.maximum(row_id, col_id)).astype(F32)
    last = []
    for n, (lo, hi, off, keep) in enumerate((
        (low, high, offset, col_id <= row_id),
        (low.T, high.T, offset.T, col_id < row_id),
    )):
        for d in range(BANDS):
            band = jnp.where(off == d, lo, jnp.where(off == d - 1, hi, 0.0))
            wb[pl.ds((n * BANDS + d) * piv, piv), :] = jnp.where(keep, band, 0.0).astype(BF16)
        last.append(pltpu.roll(jnp.where(keep & (off == -1), lo, 0.0)[piv - 8:], 7, 0))
    rate_row = rate[...]
    cour_row = cour[...]
    base = 2 * BANDS * piv
    wb[pl.ds(base, piv), :] = kern.astype(BF16)
    wb[pl.ds(base + 2 * piv, 16), :] = jnp.concatenate(last, axis=0).astype(BF16)
    smaller = (row_id < col_id).astype(F32)
    wb[pl.ds(base + piv, piv), :] = (frag[...] * rate_row * smaller).astype(BF16)
    diag = row_id == col_id
    rate_col = jnp.sum(jnp.where(diag, rate_row, 0.0), axis=1, keepdims=True)
    cour_col = jnp.sum(jnp.where(diag, cour_row, 0.0), axis=1, keepdims=True)
    own_diag = (lax.broadcasted_iota(jnp.int32, (own, piv), 0) + me_p * own
                == lax.broadcasted_iota(jnp.int32, (own, piv), 1))
    own_cour = jnp.sum(jnp.where(own_diag, cour_row, 0.0), axis=1, keepdims=True)
    one_hot = (lax.broadcasted_iota(jnp.int32, (width, width), 0) == face_map[...]).astype(F32).astype(BF16)

    pl.semaphore_wait(barrier, len(pairs) + len(ring_mates) + len(pick_mates) - 3)

    def along_ring(faces, send, recv):
        copies = [to_block(ring_mates[d], d, faces.at[y], faces.at[y], send, recv) for d in range(1, RING)]
        for copy in copies:
            copy.start()
        return copies

    def across(faces, copies, chosen, chosen_r, send, recv):
        for copy in copies:
            copy.wait_recv()
        for q in range(1, 4):
            chosen[q] = faces[(up_sm[pick_mates[q]] // CORES) % RING]
        more = [to_block(pick_mates[q], q, chosen.at[q], chosen_r.at[q], send, recv) for q in range(1, 4)]
        for copy in more:
            copy.start()
        chosen_r[0] = faces[(up_sm[me_b] // CORES) % RING]
        return more

    def arrived(copies, chosen_r):
        for copy in copies:
            copy.wait_recv()
        u = up_sm[me_b]
        q = ((u // (RING * CORES) + z_hi) % 2) * 2 + (u + core) % 2
        return permuted(chosen_r[q], one_hot)

    ring_out = along_ring(ring, ring_send, ring_recv)
    main_in = [to_pair(d, enc.at[pairs[d]], got.at[me_p], main_send, main_recv) for d in range(1, n_pair)]
    halos = [to_pair(d, halo_s.at[pairs[d]], halo_r.at[me_p], halo_send, halo_recv) for d in range(1, n_pair)]
    for copy in main_in + halos:
        copy.start()
    got_own = pltpu.make_async_copy(enc.at[me_p], got.at[me_p], local_sem.at[6])
    got_own.start()
    halo_own = pltpu.make_async_copy(halo_s.at[me_p], halo_r.at[me_p], local_sem.at[7])
    halo_own.start()

    pick_out = across(ring, ring_out, picked, picked_r, pick_send, pick_recv)
    inflow = arrived(pick_out, picked_r)
    for t in range(2):
        inflow_s[t] = inflow[:, t * 128:(t + 1) * 128]

    def inflow_copy(t, source):
        return pltpu.make_async_remote_copy(
            src_ref=inflow_s.at[t], dst_ref=inflow_r.at[source], send_sem=inflow_send.at[t],
            recv_sem=inflow_recv.at[source], device_id=(me_b, t), device_id_type=MESH)

    for t in range(2):
        @pl.when(me_p != t)
        def _():
            inflow_copy(t, me_p).start()

        @pl.when(me_p == t)
        def _():
            inflow_r[t] = inflow_s[t]

    def change(v, prev):
        y_s[...] = jnp.dot(wb[...], v.astype(BF16), preferred_element_type=F32)
        vb = v.astype(BF16).astype(F32)
        below = y_s[pl.ds(base + 2 * piv, 8), :] + y_s[pl.ds(base + 2 * piv + 8, 8), :]
        y_s[pl.ds(base + 2 * piv - 8, 8), :] += below * vb[piv - 1:]
        births = None
        for d in reversed(range(BANDS)):
            here = vb * (y_s[pl.ds(d * piv, piv), :] + y_s[pl.ds((BANDS + d) * piv, piv), :])
            births = here if births is None else here + pltpu.roll(births, 1, 0)
        loss = y_s[pl.ds(base, piv), :]
        gain = y_s[pl.ds(base + piv, piv), :]
        source = births - v * loss + gain - rate_col * v
        return v + (source - cour_col * (v - prev))

    def start_row(s):
        return v0[pl.ds(s, piv, stride=8), :]

    got_own.wait()
    for copy in main_in:
        copy.wait_recv()
    for p in range(n_pair):
        v0[pl.ds(p * own * 8, own * 8), :] = got[p].astype(jnp.int32).astype(F32) * STEP + MIDDLE
    halo_own.wait()
    for copy in halos:
        copy.wait_recv()
    for p in range(n_pair):
        halo_c[pl.ds(p * own, own), :] = halo_r[p]

    top = None
    edge = to_pair(2, sec.at[:, pl.ds(7 * 128, 128)], edge_r, edge_send, edge_recv)
    for it in reversed(range(4)):
        s = 2 * it
        before = halo_c[...] if it == 0 else start_row(s - 1)
        first, second = start_row(s), start_row(s + 1)
        now = change(jnp.concatenate([first, second], axis=1), jnp.concatenate([before, first], axis=1))
        for t in range(2):
            row = grp * 8 + s + t
            piece = jnp.where(row < live_rows, now[:, t * 128:(t + 1) * 128], 0.0)
            sec[:, pl.ds((s + t) * 128, 128)] = piece
            mine = jnp.where(row == top_row, piece, 0.0)
            top = mine if top is None else top + mine
        if it == 3:
            edge.start()

    top_s[...] = top
    for p in range(n_pair):
        top_p[p] = top_s[pl.ds(p * own, own), :]
    tops = [to_pair(d, top_p.at[pairs[d]], top_r.at[me_p], top_send, top_recv) for d in range(1, n_pair)]
    for copy in tops:
        copy.start()
    top_own = pltpu.make_async_copy(top_p.at[me_p], top_r.at[me_p], local_sem.at[8])
    top_own.start()

    biggest = None
    for it in reversed(range(4)):
        s = 2 * it
        if it == 0:
            @pl.when(grp == 0)
            def _():
                for q in range(n_pair):
                    @pl.when(me_p != q)
                    def _():
                        inflow_copy(0, q).wait_recv()

                for p in range(n_pair):
                    halo_c[pl.ds(p * own, own), :] = inflow_r[p]
                sec[:, :128] += cour_col * halo_c[...]

            edge.wait_recv()
            before = jnp.where(grp > 0, edge_r[...], 0.0)
        else:
            before = sec[:, pl.ds((s - 1) * 128, 128)]
        v = sec[:, pl.ds(s * 128, 256)]
        now = change(v, jnp.concatenate([before, v[:, :128]], axis=1))
        for t in range(2):
            row = grp * 8 + s + t
            piece = 0.5 * start_row(s + t) + 0.5 * now[:, t * 128:(t + 1) * 128]
            piece = jnp.where(row < live_rows, piece, 0.0)
            res[:, pl.ds((s + t) * 128, 128)] = piece
            size = jnp.abs(piece)
            biggest = size if biggest is None else jnp.maximum(biggest, size)

    biggest = jnp.max(biggest, axis=1, keepdims=True)
    finer = jnp.where(biggest > 0.0, 32767.0 / biggest, 0.0)
    for s in range(8):
        out_f[pl.ds(s, piv, stride=8), :] = res[:, pl.ds(s * 128, 128)] * finer
    for p in range(n_pair):
        out_s[p] = rounded16(out_f[pl.ds(p * own * 8, own * 8), :])
    outs = [to_pair(d, out_s.at[pairs[d]], out_r.at[me_p], out_send, out_recv) for d in range(1, n_pair)]
    for copy in outs:
        copy.start()
    top_s[...] = jnp.broadcast_to(biggest * (1.0 / 32767.0), (piv, 128))
    for p in range(n_pair):
        scale_p[p] = top_s[pl.ds(p * own, own), :]
    scales = [to_pair(d, scale_p.at[pairs[d]], scale_r.at[me_p], scale_send, scale_recv) for d in range(1, n_pair)]
    for copy in scales:
        copy.start()
    out_own = [pltpu.make_async_copy(out_s.at[me_p], out_r.at[me_p], local_sem.at[9]),
               pltpu.make_async_copy(scale_p.at[me_p], scale_r.at[me_p], local_sem.at[10])]
    for copy in out_own:
        copy.start()

    top_own.wait()
    for copy in tops:
        copy.wait_recv()
    for t in range(2):
        face = (top_r[t] + top_r[t + 2]) + (top_r[t + 4] + top_r[t + 6])
        ring2[y, :, pl.ds(t * 128, 128)] = face + jnp.where(top_row == 0, own_cour * inflow_s[t], 0.0)
    ring2_out = along_ring(ring2, ring2_send, ring2_recv)
    pick2_out = across(ring2, ring2_out, picked2, picked2_r, pick2_send, pick2_recv)
    add = 0.5 * own_cour * arrived(pick2_out, picked2_r)

    for copy in out_own:
        copy.wait()
    for copy in outs + scales:
        copy.wait_recv()
    bottom = lax.broadcasted_iota(jnp.int32, (own, 8, 128), 1) == 0
    for p in range(n_pair):
        tile = out_r[p].astype(jnp.int32).astype(F32).reshape(own, 8, 128) * scale_r[p][:, None, :]
        if p < 2:
            tile = tile + jnp.where(bottom, add[:, p * 128:(p + 1) * 128][:, None, :], 0.0)
        main[:, pl.ds((p // 2) * 8, 8), pl.ds((p % 2) * 128, 128)] = tile

    for copy in (ring_out + main_in + halos + pick_out + [edge] + tops + outs + scales + ring2_out + pick2_out):
        copy.wait_send()
    for t in range(2):
        @pl.when(me_p != t)
        def _():
            inflow_copy(t, me_p).wait_send()


def shards(n_pair, density, agg, share, target, frag, rate, cour, block_rows, upstream, face_map):
    own, height, width = density.shape
    piv = agg.shape[0]
    vmem = pl.BlockSpec(memory_space=pltpu.VMEM)
    smem = pl.BlockSpec(memory_space=pltpu.SMEM)
    hbm = pl.BlockSpec(memory_space=pltpu.HBM)
    dma = pltpu.SemaphoreType.DMA
    weight_rows = (2 * BANDS + 2) * piv + 16
    return pl.pallas_call(
        functools.partial(step_kernel, n_pair, own, piv, height, width),
        out_shape=jax.ShapeDtypeStruct(density.shape, F32),
        in_specs=[hbm] * 5 + [vmem] * 2 + [smem] * 2 + [vmem],
        out_specs=vmem,
        scratch_shapes=[
            pltpu.VMEM((piv, piv), F32),
            pltpu.VMEM((piv, piv), F32),
            pltpu.VMEM((piv, piv), jnp.int32),
            pltpu.VMEM((piv, piv), F32),
            pltpu.VMEM((2, own, height, 128), F32),
            pltpu.VMEM((n_pair, own * 8, 128), I16),
            pltpu.VMEM((n_pair, own * 8, 128), I16),
            pltpu.VMEM((piv * 8, 128), F32),
            pltpu.VMEM((piv, 1024), F32),
            pltpu.VMEM((piv, 1024), F32),
            pltpu.VMEM((piv * 8, 128), F32),
            pltpu.VMEM((n_pair, own * 8, 128), I16),
            pltpu.VMEM((n_pair, own * 8, 128), I16),
            pltpu.VMEM((weight_rows, piv), BF16),
            pltpu.VMEM((weight_rows, 256), F32),
            pltpu.VMEM((RING, own, width), F32),
            pltpu.VMEM((4, own, width), F32),
            pltpu.VMEM((4, own, width), F32),
            pltpu.VMEM((RING, own, width), F32),
            pltpu.VMEM((4, own, width), F32),
            pltpu.VMEM((4, own, width), F32),
            pltpu.VMEM((n_pair, own, 128), F32),
            pltpu.VMEM((n_pair, own, 128), F32),
            pltpu.VMEM((piv, 128), F32),
            pltpu.VMEM((2, own, 128), F32),
            pltpu.VMEM((n_pair, own, 128), F32),
            pltpu.VMEM((piv, 128), F32),
            pltpu.VMEM((piv, 128), F32),
            pltpu.VMEM((n_pair, own, 128), F32),
            pltpu.VMEM((n_pair, own, 128), F32),
            pltpu.VMEM((n_pair, own, 128), F32),
            pltpu.VMEM((n_pair, own, 128), F32),
            dma((11,)),
            dma((n_pair,)), dma((n_pair,)),
            dma((n_pair,)), dma((n_pair,)),
            dma((2,)), dma((n_pair,)),
            dma((RING,)), dma((RING,)),
            dma((4,)), dma((4,)),
            dma((RING,)), dma((RING,)),
            dma((4,)), dma((4,)),
            dma((n_pair,)), dma((n_pair,)),
            dma((n_pair,)), dma((n_pair,)),
            dma((n_pair,)), dma((n_pair,)),
            dma((n_pair,)), dma((n_pair,)),
        ],
        compiler_params=pltpu.CompilerParams(
            collective_id=0, has_side_effects=True, vmem_limit_bytes=56 * 1024 * 1024),
    )(density, agg, share, target, frag, rate.reshape(1, piv), cour.reshape(1, piv), block_rows, upstream, face_map)


def solution(mesh):
    in_specs = (P("pair", "blk", None), P(), P(), P(), P(), P(), P(), P(), P(), P("blk", None))
    out_specs = P("pair", "blk", None)
    return jax.shard_map(
        functools.partial(shards, mesh.shape["pair"]),
        mesh=mesh, in_specs=in_specs, out_specs=out_specs, check_vma=False)
```

```python
import functools

import jax
import jax.numpy as jnp
from jax import lax
from jax.experimental import pallas as pl
from jax.experimental.pallas import tpu as pltpu
from jax.sharding import PartitionSpec as P

MESH = pl.DeviceIdType.MESH
BANDS = 5
F32 = jnp.float32
BF16 = jnp.bfloat16
I16 = jnp.int16
RING, CORES = 4, 2
ORDER = (4, 3, 5, 2, 6, 1, 7)
MIDDLE = 1.025
STEP = 1.95 / 65534.0


def permuted(face, one_hot):
    total = None
    for _ in range(3):
        part = face.astype(BF16)
        face = face - part.astype(F32)
        moved = jnp.dot(part, one_hot, preferred_element_type=F32)
        total = moved if total is None else total + moved
    return total


def rounded16(x):
    return jnp.round(x).astype(jnp.int32).astype(I16)


def step_kernel(
    n_pair, own, piv, height, width,
    density, agg_h, share_h, target_h, frag_h, rate, cour, rows_sm, up_sm, face_map,
    main, add_0, add_1,
    agg, share, target, frag, dens_v, enc, got, v0, sec, res, out_f, out_s, out_r, main_v, wb, y_s,
    ring, picked, picked_r, ring2, picked2, picked2_r,
    halo_f, halo_c, inflow_s, inflow_r, late_s, late_p, late_r, edge_r, top_s, top_p, top_r, scale_p, scale_r,
    local_sem, main_send, main_recv, inflow_send, inflow_recv, late_send, late_recv,
    ring_send, ring_recv, pick_send, pick_recv, ring2_send, ring2_recv, pick2_send, pick2_recv,
    edge_send, edge_recv, top_send, top_recv, out_send, out_recv, scale_send, scale_recv,
):
    me_b, me_p = lax.axis_index("blk"), lax.axis_index("pair")
    grp = me_p // 2
    z_hi, y, core = me_b // (RING * CORES), (me_b // CORES) % RING, me_b % CORES
    pairs = [(me_p + d) % n_pair for d in range(n_pair)]

    def block_at(dz, dy, dc):
        return ((z_hi + dz) % 2) * (RING * CORES) + ((y + dy) % RING) * CORES + (core + dc) % CORES

    ring_mates = [block_at(0, d, 0) for d in range(RING)]
    pick_mates = [block_at(q // 2, 0, q % 2) for q in range(4)]

    barrier = pltpu.get_barrier_semaphore()
    for p in pairs[1:]:
        pl.semaphore_signal(barrier, inc=1, device_id=(me_b, p), device_id_type=MESH)
    for b in ring_mates[1:] + pick_mates[1:]:
        pl.semaphore_signal(barrier, inc=1, device_id=(b, me_p), device_id_type=MESH)

    loads = [pltpu.make_async_copy(density.at[:, :, pl.ds(t * 128, 128)], dens_v.at[t], local_sem.at[t])
             for t in range(2)]
    for load in loads:
        load.start()
    tables = [pltpu.make_async_copy(src, dst, local_sem.at[2 + n]) for n, (src, dst) in enumerate(
        ((agg_h, agg), (share_h, share), (target_h, target), (frag_h, frag)))]
    for load in tables:
        load.start()

    def to_pair(d, src, dst, send, recv):
        return pltpu.make_async_remote_copy(
            src_ref=src, dst_ref=dst, send_sem=send.at[d], recv_sem=recv.at[d],
            device_id=(me_b, pairs[d]), device_id_type=MESH)

    def to_block(b, d, src, dst, send, recv):
        return pltpu.make_async_remote_copy(
            src_ref=src, dst_ref=dst, send_sem=send.at[d], recv_sem=recv.at[d],
            device_id=(b, me_p), device_id_type=MESH)

    def along_ring(faces, send, recv):
        copies = [to_block(ring_mates[d], d, faces.at[y], faces.at[y], send, recv) for d in range(1, RING)]
        for copy in copies:
            copy.start()
        return copies

    def across(faces, copies, chosen, chosen_r, send, recv):
        for copy in copies:
            copy.wait_recv()
        for q in range(1, 4):
            chosen[q] = faces[(up_sm[pick_mates[q]] // CORES) % RING]
        more = [to_block(pick_mates[q], q, chosen.at[q], chosen_r.at[q], send, recv) for q in range(1, 4)]
        for copy in more:
            copy.start()
        chosen_r[0] = faces[(up_sm[me_b] // CORES) % RING]
        return more

    def arrived(copies, chosen_r):
        for copy in copies:
            copy.wait_recv()
        u = up_sm[me_b]
        q = ((u // (RING * CORES) + z_hi) % 2) * 2 + (u + core) % 2
        return permuted(chosen_r[q], one_hot)

    live_rows = rows_sm[me_b]
    top_row = live_rows - 1
    halo_f[...] = jnp.zeros(halo_f.shape, F32)
    for load in loads:
        load.wait()
    dens_rows = dens_v.reshape(2 * own * height, 128)
    for t in range(2):
        ring[y, :, pl.ds(t * 128, 128)] = dens_rows[
            pl.ds(jnp.maximum(top_row, 0) + t * own * height, own, stride=height), :]
    pl.semaphore_wait(barrier, len(pairs) + len(ring_mates) + len(pick_mates) - 3)
    ring_out = along_ring(ring, ring_send, ring_recv)

    main_in = []
    for d in ORDER + (0,):
        p = pairs[d]
        tile = dens_v[p % 2, :, pl.ds(pl.multiple_of((p // 2) * 8, 8), 8), :].reshape(own * 8, 128)
        under = jnp.maximum((p // 2) * 8 - 1, 0) + (p % 2) * own * height
        halo_f[pl.ds(0, own), :] = dens_rows[pl.ds(under, own, stride=height), :]
        goal = enc.at[d] if d else got.at[me_p]
        goal[pl.ds(0, own * 8), :] = rounded16((tile - MIDDLE) * (1.0 / STEP))
        goal[pl.ds(own * 8, 32), :] = rounded16((halo_f[...] - MIDDLE) * (1.0 / STEP))
        if d:
            main_in.append(to_pair(d, enc.at[d], got.at[me_p], main_send, main_recv))
            main_in[-1].start()

    for load in tables:
        load.wait()
    row_id = lax.broadcasted_iota(jnp.int32, (piv, piv), 0)
    col_id = lax.broadcasted_iota(jnp.int32, (piv, piv), 1)
    kern = agg[...]
    part = share[...]
    low = (0.5 * kern * part).astype(BF16).astype(F32)
    high = (0.5 * kern * (1.0 - part)).astype(BF16).astype(F32)
    offset = (target[...] - jnp.maximum(row_id, col_id)).astype(F32)
    last = []
    for n, (lo, hi, off, keep) in enumerate((
        (low, high, offset, col_id <= row_id),
        (low.T, high.T, offset.T, col_id < row_id),
    )):
        for d in range(BANDS):
            band = jnp.where(off == d, lo, jnp.where(off == d - 1, hi, 0.0))
            wb[pl.ds((n * BANDS + d) * piv, piv), :] = jnp.where(keep, band, 0.0).astype(BF16)
        last.append(pltpu.roll(jnp.where(keep & (off == -1), lo, 0.0)[piv - 8:], 7, 0))
    rate_row = rate[...]
    cour_row = cour[...]
    base = 2 * BANDS * piv
    wb[pl.ds(base, piv), :] = kern.astype(BF16)
    wb[pl.ds(base + 2 * piv, 16), :] = jnp.concatenate(last, axis=0).astype(BF16)
    smaller = (row_id < col_id).astype(F32)
    wb[pl.ds(base + piv, piv), :] = (frag[...] * rate_row * smaller).astype(BF16)
    diag = row_id == col_id
    rate_col = jnp.sum(jnp.where(diag, rate_row, 0.0), axis=1, keepdims=True)
    cour_col = jnp.sum(jnp.where(diag, cour_row, 0.0), axis=1, keepdims=True)
    own_diag = (lax.broadcasted_iota(jnp.int32, (own, piv), 0) + me_p * own
                == lax.broadcasted_iota(jnp.int32, (own, piv), 1))
    own_cour = jnp.sum(jnp.where(own_diag, cour_row, 0.0), axis=1, keepdims=True)
    one_hot = (lax.broadcasted_iota(jnp.int32, (width, width), 0) == face_map[...]).astype(F32).astype(BF16)

    pick_out = across(ring, ring_out, picked, picked_r, pick_send, pick_recv)

    def change(v, prev):
        y_s[...] = jnp.dot(wb[...], v.astype(BF16), preferred_element_type=F32)
        vb = v.astype(BF16).astype(F32)
        below = y_s[pl.ds(base + 2 * piv, 8), :] + y_s[pl.ds(base + 2 * piv + 8, 8), :]
        y_s[pl.ds(base + 2 * piv - 8, 8), :] += below * vb[piv - 1:]
        births = None
        for d in reversed(range(BANDS)):
            here = vb * (y_s[pl.ds(d * piv, piv), :] + y_s[pl.ds((BANDS + d) * piv, piv), :])
            births = here if births is None else here + pltpu.roll(births, 1, 0)
        loss = y_s[pl.ds(base, piv), :]
        gain = y_s[pl.ds(base + piv, piv), :]
        source = births - v * loss + gain - rate_col * v
        return v + (source - cour_col * (v - prev))

    def start_row(s):
        return v0[pl.ds(s, piv, stride=8), :]

    for copy in main_in:
        copy.wait_recv()
    for p in range(n_pair):
        v0[pl.ds(p * own * 8, own * 8), :] = (
            got[p, pl.ds(0, own * 8), :].astype(jnp.int32).astype(F32) * STEP + MIDDLE)
        under = got[p, pl.ds(own * 8, 32), :].astype(jnp.int32).astype(F32) * STEP + MIDDLE
        halo_c[pl.ds(p * own, own), :] = jnp.where(grp > 0, under[:own], 0.0)

    top = None
    edge = to_pair(2, sec.at[:, pl.ds(7 * 128, 128)], edge_r, edge_send, edge_recv)
    for it in reversed(range(4)):
        s = 2 * it
        before = halo_c[...] if it == 0 else start_row(s - 1)
        first, second = start_row(s), start_row(s + 1)
        now = change(jnp.concatenate([first, second], axis=1), jnp.concatenate([before, first], axis=1))
        for t in range(2):
            row = grp * 8 + s + t
            piece = jnp.where(row < live_rows, now[:, t * 128:(t + 1) * 128], 0.0)
            sec[:, pl.ds((s + t) * 128, 128)] = piece
            mine = jnp.where(row == top_row, piece, 0.0)
            top = mine if top is None else top + mine
        if it == 3:
            edge.start()

    top_s[...] = top
    for p in range(n_pair):
        top_p[p] = top_s[pl.ds(p * own, own), :]
    tops = [to_pair(d, top_p.at[pairs[d]], top_r.at[me_p], top_send, top_recv) for d in range(1, n_pair)]
    for copy in tops:
        copy.start()
    top_own = pltpu.make_async_copy(top_p.at[me_p], top_r.at[me_p], local_sem.at[8])
    top_own.start()

    inflow = arrived(pick_out, picked_r)
    for t in range(2):
        inflow_s[t] = inflow[:, t * 128:(t + 1) * 128]

    def inflow_copy(t, source):
        return pltpu.make_async_remote_copy(
            src_ref=inflow_s.at[t], dst_ref=inflow_r.at[source], send_sem=inflow_send.at[t],
            recv_sem=inflow_recv.at[source], device_id=(me_b, t), device_id_type=MESH)

    for t in range(2):
        @pl.when(me_p != t)
        def _():
            inflow_copy(t, me_p).start()

        @pl.when(me_p == t)
        def _():
            inflow_r[t] = inflow_s[t]

    def final_rows(it, before):
        v = sec[:, pl.ds(it * 256, 256)]
        now = change(v, jnp.concatenate([before, v[:, :128]], axis=1))
        return [0.5 * start_row(2 * it + t) + 0.5 * now[:, t * 128:(t + 1) * 128] for t in range(2)]

    biggest = None
    for it in reversed(range(4)):
        if it == 0:
            edge.wait_recv()
            before = edge_r[...]
        else:
            before = sec[:, pl.ds((2 * it - 1) * 128, 128)]
        for t, piece in enumerate(final_rows(it, before)):
            row = grp * 8 + 2 * it + t
            piece = jnp.where((row < live_rows) & (row >= 2), piece, 0.0)
            res[:, pl.ds((2 * it + t) * 128, 128)] = piece
            size = jnp.abs(piece)
            biggest = size if biggest is None else jnp.maximum(biggest, size)

    biggest = jnp.max(biggest, axis=1, keepdims=True)
    finer = jnp.where(biggest > 0.0, 32767.0 / biggest, 0.0)
    for s in range(8):
        out_f[pl.ds(s, piv, stride=8), :] = res[:, pl.ds(s * 128, 128)] * finer
    for p in range(n_pair):
        out_s[p] = rounded16(out_f[pl.ds(p * own * 8, own * 8), :])
    outs = [to_pair(d, out_s.at[pairs[d]], out_r.at[me_p], out_send, out_recv) for d in range(1, n_pair)]
    for copy in outs:
        copy.start()
    top_s[...] = jnp.broadcast_to(biggest * (1.0 / 32767.0), (piv, 128))
    for p in range(n_pair):
        scale_p[p] = top_s[pl.ds(p * own, own), :]
    scales = [to_pair(d, scale_p.at[pairs[d]], scale_r.at[me_p], scale_send, scale_recv) for d in range(1, n_pair)]
    for copy in scales:
        copy.start()
    out_own = [pltpu.make_async_copy(out_s.at[me_p], out_r.at[me_p], local_sem.at[9]),
               pltpu.make_async_copy(scale_p.at[me_p], scale_r.at[me_p], local_sem.at[10])]
    for copy in out_own:
        copy.start()

    top_own.wait()
    for copy in tops:
        copy.wait_recv()
    for t in range(2):
        face = (top_r[t] + top_r[t + 2]) + (top_r[t + 4] + top_r[t + 6])
        ring2[y, :, pl.ds(t * 128, 128)] = face + jnp.where(top_row == 0, own_cour * inflow_s[t], 0.0)
    ring2_out = along_ring(ring2, ring2_send, ring2_recv)

    def late_copy(p, source):
        return pltpu.make_async_remote_copy(
            src_ref=late_p.at[p], dst_ref=late_r.at[source], send_sem=late_send.at[p],
            recv_sem=late_recv.at[source], device_id=(me_b, p), device_id_type=MESH)

    @pl.when(grp == 0)
    def _():
        for q in range(n_pair):
            @pl.when(me_p != q)
            def _():
                inflow_copy(0, q).wait_recv()

        for p in range(n_pair):
            halo_c[pl.ds(p * own, own), :] = inflow_r[p]
        sec[:, :128] += cour_col * halo_c[...]
        for t, piece in enumerate(final_rows(0, jnp.zeros((piv, 128), F32))):
            late_s[:, pl.ds(t * 128, 128)] = jnp.where(t < live_rows, piece, 0.0)
        for p in range(n_pair):
            late_p[p] = late_s[pl.ds(p * own, own), :]
        for p in range(n_pair):
            @pl.when(me_p != p)
            def _():
                late_copy(p, me_p).start()

            @pl.when(me_p == p)
            def _():
                late_r[min(p, 1)] = late_p[p]

    pick2_out = across(ring2, ring2_out, picked2, picked2_r, pick2_send, pick2_recv)

    for copy in out_own:
        copy.wait()
    for copy in outs + scales:
        copy.wait_recv()
    for p in range(n_pair):
        tile = out_r[p].astype(jnp.int32).astype(F32).reshape(own, 8, 128) * scale_r[p][:, None, :]
        main_v[:, pl.ds((p // 2) * 8, 8), pl.ds((p % 2) * 128, 128)] = tile
    store = pltpu.make_async_copy(main_v, main, local_sem.at[6])
    store.start()

    for q in range(2):
        @pl.when(me_p != q)
        def _():
            late_copy(0, q).wait_recv()
    for t, add in enumerate((add_0, add_1)):
        for q in range(2):
            add[:, pl.ds(q * 128, 128)] = late_r[q, :, pl.ds(t * 128, 128)]
    add_0[...] += 0.5 * own_cour * arrived(pick2_out, picked2_r)

    store.wait()
    for copy in (ring_out + main_in + pick_out + [edge] + tops + outs + scales + ring2_out + pick2_out):
        copy.wait_send()
    for t in range(2):
        @pl.when(me_p != t)
        def _():
            inflow_copy(t, me_p).wait_send()

    @pl.when(grp == 0)
    def _():
        for p in range(n_pair):
            @pl.when(me_p != p)
            def _():
                late_copy(p, me_p).wait_send()


def shards(n_pair, density, agg, share, target, frag, rate, cour, block_rows, upstream, face_map):
    own, height, width = density.shape
    piv = agg.shape[0]
    vmem = pl.BlockSpec(memory_space=pltpu.VMEM)
    smem = pl.BlockSpec(memory_space=pltpu.SMEM)
    hbm = pl.BlockSpec(memory_space=pltpu.HBM)
    dma = pltpu.SemaphoreType.DMA
    weight_rows = (2 * BANDS + 2) * piv + 16
    main, add_0, add_1 = pl.pallas_call(
        functools.partial(step_kernel, n_pair, own, piv, height, width),
        out_shape=(
            jax.ShapeDtypeStruct(density.shape, F32),
            jax.ShapeDtypeStruct((own, width), F32),
            jax.ShapeDtypeStruct((own, width), F32),
        ),
        in_specs=[hbm] * 5 + [vmem] * 2 + [smem] * 2 + [vmem],
        out_specs=(hbm, vmem, vmem),
        scratch_shapes=[
            pltpu.VMEM((piv, piv), F32),
            pltpu.VMEM((piv, piv), F32),
            pltpu.VMEM((piv, piv), jnp.int32),
            pltpu.VMEM((piv, piv), F32),
            pltpu.VMEM((2, own, height, 128), F32),
            pltpu.VMEM((n_pair, own * 8 + 32, 128), I16),
            pltpu.VMEM((n_pair, own * 8 + 32, 128), I16),
            pltpu.VMEM((piv * 8, 128), F32),
            pltpu.VMEM((piv, 1024), F32),
            pltpu.VMEM((piv, 1024), F32),
            pltpu.VMEM((piv * 8, 128), F32),
            pltpu.VMEM((n_pair, own * 8, 128), I16),
            pltpu.VMEM((n_pair, own * 8, 128), I16),
            pltpu.VMEM((own, height, width), F32),
            pltpu.VMEM((weight_rows, piv), BF16),
            pltpu.VMEM((weight_rows, 256), F32),
            pltpu.VMEM((RING, own, width), F32),
            pltpu.VMEM((4, own, width), F32),
            pltpu.VMEM((4, own, width), F32),
            pltpu.VMEM((RING, own, width), F32),
            pltpu.VMEM((4, own, width), F32),
            pltpu.VMEM((4, own, width), F32),
            pltpu.VMEM((32, 128), F32),
            pltpu.VMEM((piv, 128), F32),
            pltpu.VMEM((2, own, 128), F32),
            pltpu.VMEM((n_pair, own, 128), F32),
            pltpu.VMEM((piv, 256), F32),
            pltpu.VMEM((n_pair, own, 256), F32),
            pltpu.VMEM((2, own, 256), F32),
            pltpu.VMEM((piv, 128), F32),
            pltpu.VMEM((piv, 128), F32),
            pltpu.VMEM((n_pair, own, 128), F32),
            pltpu.VMEM((n_pair, own, 128), F32),
            pltpu.VMEM((n_pair, own, 128), F32),
            pltpu.VMEM((n_pair, own, 128), F32),
            dma((11,)),
            dma((n_pair,)), dma((n_pair,)),
            dma((2,)), dma((n_pair,)),
            dma((n_pair,)), dma((2,)),
            dma((RING,)), dma((RING,)),
            dma((4,)), dma((4,)),
            dma((RING,)), dma((RING,)),
            dma((4,)), dma((4,)),
            dma((n_pair,)), dma((n_pair,)),
            dma((n_pair,)), dma((n_pair,)),
            dma((n_pair,)), dma((n_pair,)),
            dma((n_pair,)), dma((n_pair,)),
        ],
        compiler_params=pltpu.CompilerParams(
            collective_id=0, has_side_effects=True, vmem_limit_bytes=56 * 1024 * 1024),
    )(density, agg, share, target, frag, rate.reshape(1, piv), cour.reshape(1, piv), block_rows, upstream, face_map)
    row = lax.broadcasted_iota(jnp.int32, main.shape, 1)
    return main + jnp.where(row == 0, add_0[:, None, :], jnp.where(row == 1, add_1[:, None, :], 0.0))


def solution(mesh):
    in_specs = (P("pair", "blk", None), P(), P(), P(), P(), P(), P(), P(), P(), P("blk", None))
    out_specs = P("pair", "blk", None)
    return jax.shard_map(
        functools.partial(shards, mesh.shape["pair"]),
        mesh=mesh, in_specs=in_specs, out_specs=out_specs, check_vma=False)
```

```python
import functools

import jax
import jax.numpy as jnp
from jax import lax
from jax.experimental import pallas as pl
from jax.experimental.pallas import tpu as pltpu
from jax.sharding import PartitionSpec as P

MESH = pl.DeviceIdType.MESH
BANDS = 5
F32 = jnp.float32
BF16 = jnp.bfloat16
I16 = jnp.int16
RING, CORES = 4, 2
ORDER = (4, 3, 5, 2, 6, 1, 7)
MIDDLE = 1.025
STEP = 1.95 / 65534.0


def permuted(face, one_hot):
    total = None
    for _ in range(3):
        part = face.astype(BF16)
        face = face - part.astype(F32)
        moved = jnp.dot(part, one_hot, preferred_element_type=F32)
        total = moved if total is None else total + moved
    return total


def rounded16(x):
    return jnp.round(x).astype(jnp.int32).astype(I16)


def step_kernel(
    n_pair, own, piv, height, width,
    density, agg_h, share_h, target_h, frag_h, rate, cour, rows_sm, up_sm, face_map,
    main, add_0, add_1,
    agg, share, target, frag, dens_v, enc, got, v0, sec, res, out_f, out_s, out_r, main_v, wb, y_s,
    ring, picked, picked_r, ring2, picked2, picked2_r,
    halo_f, halo_c, inflow_s, inflow_r, face, terms_s, late_s, late_p, late_r, edge_r, wide_s, scale_p, scale_r,
    local_sem, main_send, main_recv, inflow_send, inflow_recv, late_send, late_recv,
    ring_send, ring_recv, pick_send, pick_recv, ring2_send, ring2_recv, pick2_send, pick2_recv,
    edge_send, edge_recv, out_send, out_recv, scale_send, scale_recv,
):
    me_b, me_p = lax.axis_index("blk"), lax.axis_index("pair")
    grp, half = me_p // 2, me_p % 2
    z_hi, y, core = me_b // (RING * CORES), (me_b // CORES) % RING, me_b % CORES
    pairs = [(me_p + d) % n_pair for d in range(n_pair)]

    def block_at(dz, dy, dc):
        return ((z_hi + dz) % 2) * (RING * CORES) + ((y + dy) % RING) * CORES + (core + dc) % CORES

    ring_mates = [block_at(0, d, 0) for d in range(RING)]
    pick_mates = [block_at(q // 2, 0, q % 2) for q in range(4)]

    barrier = pltpu.get_barrier_semaphore()
    for p in pairs[1:]:
        pl.semaphore_signal(barrier, inc=1, device_id=(me_b, p), device_id_type=MESH)
    for b in ring_mates[1:] + pick_mates[1:]:
        pl.semaphore_signal(barrier, inc=1, device_id=(b, me_p), device_id_type=MESH)

    loads = [pltpu.make_async_copy(density.at[:, :, pl.ds(t * 128, 128)], dens_v.at[t], local_sem.at[t])
             for t in range(2)]
    for load in loads:
        load.start()
    tables = [pltpu.make_async_copy(src, dst, local_sem.at[2 + n]) for n, (src, dst) in enumerate(
        ((agg_h, agg), (share_h, share), (target_h, target), (frag_h, frag)))]
    for load in tables:
        load.start()

    def to_pair(d, src, dst, send, recv):
        return pltpu.make_async_remote_copy(
            src_ref=src, dst_ref=dst, send_sem=send.at[d], recv_sem=recv.at[d],
            device_id=(me_b, pairs[d]), device_id_type=MESH)

    def to_block(b, d, src, dst, send, recv):
        return pltpu.make_async_remote_copy(
            src_ref=src, dst_ref=dst, send_sem=send.at[d], recv_sem=recv.at[d],
            device_id=(b, me_p), device_id_type=MESH)

    def along_ring(faces, send, recv):
        copies = [to_block(ring_mates[d], d, faces.at[y], faces.at[y], send, recv) for d in range(1, RING)]
        for copy in copies:
            copy.start()
        return copies

    def across(faces, copies, chosen, chosen_r, send, recv):
        for copy in copies:
            copy.wait_recv()
        for q in range(1, 4):
            chosen[q] = faces[(up_sm[pick_mates[q]] // CORES) % RING]
        more = [to_block(pick_mates[q], q, chosen.at[q], chosen_r.at[q], send, recv) for q in range(1, 4)]
        for copy in more:
            copy.start()
        chosen_r[0] = faces[(up_sm[me_b] // CORES) % RING]
        return more

    def arrived(copies, chosen_r):
        for copy in copies:
            copy.wait_recv()
        u = up_sm[me_b]
        q = ((u // (RING * CORES) + z_hi) % 2) * 2 + (u + core) % 2
        return permuted(chosen_r[q], one_hot)

    live_rows = rows_sm[me_b]
    top_row = live_rows - 1
    halo_f[...] = jnp.zeros(halo_f.shape, F32)
    for load in loads:
        load.wait()
    dens_rows = dens_v.reshape(2 * own * height, 128)
    for t in range(2):
        ring[y, :, pl.ds(t * 128, 128)] = dens_rows[
            pl.ds(jnp.maximum(top_row, 0) + t * own * height, own, stride=height), :]
    pl.semaphore_wait(barrier, len(pairs) + len(ring_mates) + len(pick_mates) - 3)
    ring_out = along_ring(ring, ring_send, ring_recv)

    main_in = []
    for d in ORDER + (0,):
        p = pairs[d]
        tile = dens_v[p % 2, :, pl.ds(pl.multiple_of((p // 2) * 8, 8), 8), :].reshape(own * 8, 128)
        under = jnp.maximum((p // 2) * 8 - 1, 0) + (p % 2) * own * height
        halo_f[pl.ds(0, own), :] = dens_rows[pl.ds(under, own, stride=height), :]
        goal = enc.at[d] if d else got.at[me_p]
        goal[pl.ds(0, own * 8), :] = rounded16((tile - MIDDLE) * (1.0 / STEP))
        goal[pl.ds(own * 8, 32), :] = rounded16((halo_f[...] - MIDDLE) * (1.0 / STEP))
        if d:
            main_in.append(to_pair(d, enc.at[d], got.at[me_p], main_send, main_recv))
            main_in[-1].start()

    for load in tables:
        load.wait()
    row_id = lax.broadcasted_iota(jnp.int32, (piv, piv), 0)
    col_id = lax.broadcasted_iota(jnp.int32, (piv, piv), 1)
    kern = agg[...]
    part = share[...]
    low = (0.5 * kern * part).astype(BF16).astype(F32)
    high = (0.5 * kern * (1.0 - part)).astype(BF16).astype(F32)
    offset = (target[...] - jnp.maximum(row_id, col_id)).astype(F32)
    last = []
    for n, (lo, hi, off, keep) in enumerate((
        (low, high, offset, col_id <= row_id),
        (low.T, high.T, offset.T, col_id < row_id),
    )):
        for d in range(BANDS):
            band = jnp.where(off == d, lo, jnp.where(off == d - 1, hi, 0.0))
            wb[pl.ds((n * BANDS + d) * piv, piv), :] = jnp.where(keep, band, 0.0).astype(BF16)
        last.append(pltpu.roll(jnp.where(keep & (off == -1), lo, 0.0)[piv - 8:], 7, 0))
    rate_row = rate[...]
    cour_row = cour[...]
    base = 2 * BANDS * piv
    wb[pl.ds(base, piv), :] = kern.astype(BF16)
    wb[pl.ds(base + 2 * piv, 16), :] = jnp.concatenate(last, axis=0).astype(BF16)
    smaller = (row_id < col_id).astype(F32)
    wb[pl.ds(base + piv, piv), :] = (frag[...] * rate_row * smaller).astype(BF16)
    diag = row_id == col_id
    rate_col = jnp.sum(jnp.where(diag, rate_row, 0.0), axis=1, keepdims=True)
    cour_col = jnp.sum(jnp.where(diag, cour_row, 0.0), axis=1, keepdims=True)
    own_diag = (lax.broadcasted_iota(jnp.int32, (own, piv), 0) + me_p * own
                == lax.broadcasted_iota(jnp.int32, (own, piv), 1))
    own_cour = jnp.sum(jnp.where(own_diag, cour_row, 0.0), axis=1, keepdims=True)
    own_rate = jnp.sum(jnp.where(own_diag, rate_row, 0.0), axis=1, keepdims=True)
    one_hot = (lax.broadcasted_iota(jnp.int32, (width, width), 0) == face_map[...]).astype(F32).astype(BF16)

    pick_out = across(ring, ring_out, picked, picked_r, pick_send, pick_recv)

    def mixed(v):
        y_s[...] = jnp.dot(wb[...], v.astype(BF16), preferred_element_type=F32)
        vb = v.astype(BF16).astype(F32)
        below = y_s[pl.ds(base + 2 * piv, 8), :] + y_s[pl.ds(base + 2 * piv + 8, 8), :]
        y_s[pl.ds(base + 2 * piv - 8, 8), :] += below * vb[piv - 1:]
        births = None
        for d in reversed(range(BANDS)):
            here = vb * (y_s[pl.ds(d * piv, piv), :] + y_s[pl.ds((BANDS + d) * piv, piv), :])
            births = here if births is None else here + pltpu.roll(births, 1, 0)
        return births - v * y_s[pl.ds(base, piv), :] + y_s[pl.ds(base + piv, piv), :]

    def change(v, prev):
        return v + (mixed(v) - rate_col * v - cour_col * (v - prev))

    def start_row(s):
        return v0[pl.ds(s, piv, stride=8), :]

    for copy in main_in:
        copy.wait_recv()
    for p in range(n_pair):
        v0[pl.ds(p * own * 8, own * 8), :] = (
            got[p, pl.ds(0, own * 8), :].astype(jnp.int32).astype(F32) * STEP + MIDDLE)
        under = got[p, pl.ds(own * 8, 32), :].astype(jnp.int32).astype(F32) * STEP + MIDDLE
        halo_c[pl.ds(p * own, own), :] = jnp.where(grp > 0, under[:own], 0.0)

    edge = to_pair(2, sec.at[:, pl.ds(7 * 128, 128)], edge_r, edge_send, edge_recv)
    for it in reversed(range(4)):
        s = 2 * it
        before = halo_c[...] if it == 0 else start_row(s - 1)
        first, second = start_row(s), start_row(s + 1)
        now = change(jnp.concatenate([first, second], axis=1), jnp.concatenate([before, first], axis=1))
        for t in range(2):
            row = grp * 8 + s + t
            piece = jnp.where(row < live_rows, now[:, t * 128:(t + 1) * 128], 0.0)
            sec[:, pl.ds((s + t) * 128, 128)] = piece
        if it == 3:
            edge.start()

    inflow = arrived(pick_out, picked_r)
    inflow_s[...] = inflow
    inflows = [to_pair(d, inflow_s, inflow_r.at[me_p], inflow_send, inflow_recv) for d in range(1, n_pair)]
    for copy in inflows:
        copy.start()
    inflow_r[me_p] = inflow

    for t in range(2):
        cols = pl.ds(t * 128, 128)
        v = ring[y, :, cols]
        under = dens_rows[pl.ds(jnp.maximum(top_row - 1, 0) + t * own * height, own, stride=height), :]
        prev = jnp.where(top_row == 0, inflow[:, t * 128:(t + 1) * 128], under)
        ring2[y, :, cols] = v - own_cour * (v - prev) - own_rate * v
    ring2_out = along_ring(ring2, ring2_send, ring2_recv)

    def final_rows(it, before):
        v = sec[:, pl.ds(it * 256, 256)]
        now = change(v, jnp.concatenate([before, v[:, :128]], axis=1))
        return [0.5 * start_row(2 * it + t) + 0.5 * now[:, t * 128:(t + 1) * 128] for t in range(2)]

    biggest = None
    for it in reversed(range(4)):
        if it == 0:
            edge.wait_recv()
            before = edge_r[...]
        else:
            before = sec[:, pl.ds((2 * it - 1) * 128, 128)]
        for t, piece in enumerate(final_rows(it, before)):
            row = grp * 8 + 2 * it + t
            piece = jnp.where((row < live_rows) & (row >= 2), piece, 0.0)
            res[:, pl.ds((2 * it + t) * 128, 128)] = piece
            size = jnp.abs(piece)
            biggest = size if biggest is None else jnp.maximum(biggest, size)

    biggest = jnp.max(biggest, axis=1, keepdims=True)
    finer = jnp.where(biggest > 0.0, 32767.0 / biggest, 0.0)
    for s in range(8):
        out_f[pl.ds(s, piv, stride=8), :] = res[:, pl.ds(s * 128, 128)] * finer
    for p in range(n_pair):
        out_s[p] = rounded16(out_f[pl.ds(p * own * 8, own * 8), :])
    outs = [to_pair(d, out_s.at[pairs[d]], out_r.at[me_p], out_send, out_recv) for d in range(1, n_pair)]
    for copy in outs:
        copy.start()
    wide_s[...] = jnp.broadcast_to(biggest * (1.0 / 32767.0), (piv, 128))
    for p in range(n_pair):
        scale_p[p] = wide_s[pl.ds(p * own, own), :]
    scales = [to_pair(d, scale_p.at[pairs[d]], scale_r.at[me_p], scale_send, scale_recv) for d in range(1, n_pair)]
    for copy in scales:
        copy.start()
    out_own = [pltpu.make_async_copy(out_s.at[me_p], out_r.at[me_p], local_sem.at[9]),
               pltpu.make_async_copy(scale_p.at[me_p], scale_r.at[me_p], local_sem.at[10])]
    for copy in out_own:
        copy.start()

    pick2_out = across(ring2, ring2_out, picked2, picked2_r, pick2_send, pick2_recv)
    for copy in inflows:
        copy.wait_recv()
    for p in range(n_pair):
        face[pl.ds(p * own, own), :] = inflow_r[p]

    def late_copy(p, source):
        return pltpu.make_async_remote_copy(
            src_ref=late_p.at[p], dst_ref=late_r.at[source], send_sem=late_send.at[p],
            recv_sem=late_recv.at[source], device_id=(me_b, p), device_id_type=MESH)

    @pl.when(grp == 0)
    def _():
        sec[:, :128] += cour_col * jnp.where(half == 0, face[:, :128], face[:, 128:])
        for t, piece in enumerate(final_rows(0, jnp.zeros((piv, 128), F32))):
            late_s[:, pl.ds(t * 128, 128)] = jnp.where(t < live_rows, piece, 0.0)
        for p in range(n_pair):
            late_p[p] = late_s[pl.ds(p * own, own), :]
        for p in range(n_pair):
            @pl.when(me_p != p)
            def _():
                late_copy(p, me_p).start()

            @pl.when(me_p == p)
            def _():
                late_r[min(p, 1)] = late_p[p]

    terms = mixed(face[...])
    for t in range(2):
        terms_s[pl.ds(t, piv, stride=8), :] = terms[:, t * 128:(t + 1) * 128]

    for copy in out_own:
        copy.wait()
    for copy in outs + scales:
        copy.wait_recv()
    for p in range(n_pair):
        tile = out_r[p].astype(jnp.int32).astype(F32).reshape(own, 8, 128) * scale_r[p][:, None, :]
        main_v[:, pl.ds((p // 2) * 8, 8), pl.ds((p % 2) * 128, 128)] = tile
    store = pltpu.make_async_copy(main_v, main, local_sem.at[6])
    store.start()

    for q in range(2):
        @pl.when(me_p != q)
        def _():
            late_copy(0, q).wait_recv()
    for t, add in enumerate((add_0, add_1)):
        for q in range(2):
            add[:, pl.ds(q * 128, 128)] = late_r[q, :, pl.ds(t * 128, 128)]
    linear = arrived(pick2_out, picked2_r)
    for t in range(2):
        cols = slice(t * 128, (t + 1) * 128)
        top = linear[:, cols] + terms_s[pl.ds(me_p * own * 8 + t, own, stride=8), :]
        add_0[:, cols] += 0.5 * own_cour * top

    store.wait()
    for copy in (ring_out + main_in + pick_out + inflows + [edge] + outs + scales + ring2_out + pick2_out):
        copy.wait_send()

    @pl.when(grp == 0)
    def _():
        for p in range(n_pair):
            @pl.when(me_p != p)
            def _():
                late_copy(p, me_p).wait_send()


def shards(n_pair, density, agg, share, target, frag, rate, cour, block_rows, upstream, face_map):
    own, height, width = density.shape
    piv = agg.shape[0]
    vmem = pl.BlockSpec(memory_space=pltpu.VMEM)
    smem = pl.BlockSpec(memory_space=pltpu.SMEM)
    hbm = pl.BlockSpec(memory_space=pltpu.HBM)
    dma = pltpu.SemaphoreType.DMA
    weight_rows = (2 * BANDS + 2) * piv + 16
    main, add_0, add_1 = pl.pallas_call(
        functools.partial(step_kernel, n_pair, own, piv, height, width),
        out_shape=(
            jax.ShapeDtypeStruct(density.shape, F32),
            jax.ShapeDtypeStruct((own, width), F32),
            jax.ShapeDtypeStruct((own, width), F32),
        ),
        in_specs=[hbm] * 5 + [vmem] * 2 + [smem] * 2 + [vmem],
        out_specs=(hbm, vmem, vmem),
        scratch_shapes=[
            pltpu.VMEM((piv, piv), F32),
            pltpu.VMEM((piv, piv), F32),
            pltpu.VMEM((piv, piv), jnp.int32),
            pltpu.VMEM((piv, piv), F32),
            pltpu.VMEM((2, own, height, 128), F32),
            pltpu.VMEM((n_pair, own * 8 + 32, 128), I16),
            pltpu.VMEM((n_pair, own * 8 + 32, 128), I16),
            pltpu.VMEM((piv * 8, 128), F32),
            pltpu.VMEM((piv, 1024), F32),
            pltpu.VMEM((piv, 1024), F32),
            pltpu.VMEM((piv * 8, 128), F32),
            pltpu.VMEM((n_pair, own * 8, 128), I16),
            pltpu.VMEM((n_pair, own * 8, 128), I16),
            pltpu.VMEM((own, height, width), F32),
            pltpu.VMEM((weight_rows, piv), BF16),
            pltpu.VMEM((weight_rows, 256), F32),
            pltpu.VMEM((RING, own, width), F32),
            pltpu.VMEM((4, own, width), F32),
            pltpu.VMEM((4, own, width), F32),
            pltpu.VMEM((RING, own, width), F32),
            pltpu.VMEM((4, own, width), F32),
            pltpu.VMEM((4, own, width), F32),
            pltpu.VMEM((32, 128), F32),
            pltpu.VMEM((piv, 128), F32),
            pltpu.VMEM((own, width), F32),
            pltpu.VMEM((n_pair, own, width), F32),
            pltpu.VMEM((piv, width), F32),
            pltpu.VMEM((piv * 8, 128), F32),
            pltpu.VMEM((piv, 256), F32),
            pltpu.VMEM((n_pair, own, 256), F32),
            pltpu.VMEM((2, own, 256), F32),
            pltpu.VMEM((piv, 128), F32),
            pltpu.VMEM((piv, 128), F32),
            pltpu.VMEM((n_pair, own, 128), F32),
            pltpu.VMEM((n_pair, own, 128), F32),
            dma((11,)),
            dma((n_pair,)), dma((n_pair,)),
            dma((n_pair,)), dma((n_pair,)),
            dma((n_pair,)), dma((2,)),
            dma((RING,)), dma((RING,)),
            dma((4,)), dma((4,)),
            dma((RING,)), dma((RING,)),
            dma((4,)), dma((4,)),
            dma((n_pair,)), dma((n_pair,)),
            dma((n_pair,)), dma((n_pair,)),
            dma((n_pair,)), dma((n_pair,)),
        ],
        compiler_params=pltpu.CompilerParams(
            collective_id=0, has_side_effects=True, vmem_limit_bytes=56 * 1024 * 1024),
    )(density, agg, share, target, frag, rate.reshape(1, piv), cour.reshape(1, piv), block_rows, upstream, face_map)
    row = lax.broadcasted_iota(jnp.int32, main.shape, 1)
    return main + jnp.where(row == 0, add_0[:, None, :], jnp.where(row == 1, add_1[:, None, :], 0.0))


def solution(mesh):
    in_specs = (P("pair", "blk", None), P(), P(), P(), P(), P(), P(), P(), P(), P("blk", None))
    out_specs = P("pair", "blk", None)
    return jax.shard_map(
        functools.partial(shards, mesh.shape["pair"]),
        mesh=mesh, in_specs=in_specs, out_specs=out_specs, check_vma=False)
```

```python
import functools

import jax
import jax.numpy as jnp
from jax import lax
from jax.experimental import pallas as pl
from jax.experimental.pallas import tpu as pltpu
from jax.sharding import PartitionSpec as P

MESH = pl.DeviceIdType.MESH
BANDS = 5
F32 = jnp.float32
BF16 = jnp.bfloat16
I16 = jnp.int16
RING, CORES = 4, 2
ORDER = (4, 3, 5, 2, 6, 1, 7)
MIDDLE = 1.025
STEP = 1.95 / 65534.0
LEAST = 32768.0 / 65536.0


def permuted(face, one_hot):
    total = None
    for _ in range(3):
        part = face.astype(BF16)
        face = face - part.astype(F32)
        moved = jnp.dot(part, one_hot, preferred_element_type=F32)
        total = moved if total is None else total + moved
    return total


def rounded16(x):
    return jnp.round(x).astype(jnp.int32).astype(I16)


def step_kernel(
    n_pair, own, piv, height, width,
    density, agg_h, share_h, target_h, frag_h, rate_h, cour_h, rows_h, up_h, map_h,
    main, add_0, add_1,
    agg, share, target, frag, rate, cour, rows_sm, up_sm, face_map, dens_v, enc, got, v0, sec, res, out_f, out_s, out_r, main_v, wb, y_s,
    ring, picked, picked_r, ring2, picked2, picked2_r,
    halo_f, halo_c, inflow_s, inflow_r, face, terms_s, late_s, late_p, late_r, edge_r, wide_s,
    local_sem, main_send, main_recv, inflow_send, inflow_recv, late_send, late_recv,
    ring_send, ring_recv, pick_send, pick_recv, ring2_send, ring2_recv, pick2_send, pick2_recv,
    edge_send, edge_recv, out_send, out_recv,
):
    me_b, me_p = lax.axis_index("blk"), lax.axis_index("pair")
    grp, half = me_p // 2, me_p % 2
    z_hi, y, core = me_b // (RING * CORES), (me_b // CORES) % RING, me_b % CORES
    pairs = [(me_p + d) % n_pair for d in range(n_pair)]

    def block_at(dz, dy, dc):
        return ((z_hi + dz) % 2) * (RING * CORES) + ((y + dy) % RING) * CORES + (core + dc) % CORES

    ring_mates = [block_at(0, d, 0) for d in range(RING)]
    pick_mates = [block_at(q // 2, 0, q % 2) for q in range(4)]

    barrier = pltpu.get_barrier_semaphore()
    for p in pairs[1:]:
        pl.semaphore_signal(barrier, inc=1, device_id=(me_b, p), device_id_type=MESH)
    for b in ring_mates[1:] + pick_mates[1:]:
        pl.semaphore_signal(barrier, inc=1, device_id=(b, me_p), device_id_type=MESH)

    loads = [pltpu.make_async_copy(density.at[:, :, pl.ds(t * 128, 128)], dens_v.at[t], local_sem.at[t])
             for t in range(2)]
    for load in loads:
        load.start()
    scalars = [pltpu.make_async_copy(rows_h, rows_sm, local_sem.at[11]),
               pltpu.make_async_copy(up_h, up_sm, local_sem.at[12])]
    for load in scalars:
        load.start()
    tables = [pltpu.make_async_copy(src, dst, local_sem.at[2 + n]) for n, (src, dst) in enumerate(
        ((agg_h, agg), (share_h, share), (target_h, target), (frag_h, frag),
         (rate_h, rate), (cour_h, cour), (map_h, face_map)))]
    for load in tables:
        load.start()

    def to_pair(d, src, dst, send, recv):
        return pltpu.make_async_remote_copy(
            src_ref=src, dst_ref=dst, send_sem=send.at[d], recv_sem=recv.at[d],
            device_id=(me_b, pairs[d]), device_id_type=MESH)

    def to_block(b, d, src, dst, send, recv):
        return pltpu.make_async_remote_copy(
            src_ref=src, dst_ref=dst, send_sem=send.at[d], recv_sem=recv.at[d],
            device_id=(b, me_p), device_id_type=MESH)

    def along_ring(faces, send, recv):
        copies = [to_block(ring_mates[d], d, faces.at[y], faces.at[y], send, recv) for d in range(1, RING)]
        for copy in copies:
            copy.start()
        return copies

    def across(faces, copies, chosen, chosen_r, send, recv):
        for copy in copies:
            copy.wait_recv()
        for q in range(1, 4):
            chosen[q] = faces[(up_sm[pick_mates[q]] // CORES) % RING]
        more = [to_block(pick_mates[q], q, chosen.at[q], chosen_r.at[q], send, recv) for q in range(1, 4)]
        for copy in more:
            copy.start()
        chosen_r[0] = faces[(up_sm[me_b] // CORES) % RING]
        return more

    def arrived(copies, chosen_r):
        for copy in copies:
            copy.wait_recv()
        u = up_sm[me_b]
        q = ((u // (RING * CORES) + z_hi) % 2) * 2 + (u + core) % 2
        return permuted(chosen_r[q], one_hot)

    halo_f[...] = jnp.zeros(halo_f.shape, F32)
    for load in scalars:
        load.wait()
    live_rows = rows_sm[me_b]
    top_row = live_rows - 1
    for load in loads:
        load.wait()
    dens_rows = dens_v.reshape(2 * own * height, 128)
    for t in range(2):
        ring[y, :, pl.ds(t * 128, 128)] = dens_rows[
            pl.ds(jnp.maximum(top_row, 0) + t * own * height, own, stride=height), :]
    pl.semaphore_wait(barrier, len(pairs) + len(ring_mates) + len(pick_mates) - 3)
    ring_out = along_ring(ring, ring_send, ring_recv)

    main_in = []
    for d in ORDER + (0,):
        p = pairs[d]
        tile = dens_v[p % 2, :, pl.ds(pl.multiple_of((p // 2) * 8, 8), 8), :].reshape(own * 8, 128)
        under = jnp.maximum((p // 2) * 8 - 1, 0) + (p % 2) * own * height
        halo_f[pl.ds(0, own), :] = dens_rows[pl.ds(under, own, stride=height), :]
        goal = enc.at[d] if d else got.at[me_p]
        goal[pl.ds(0, own * 8), :] = rounded16((tile - MIDDLE) * (1.0 / STEP))
        goal[pl.ds(own * 8, 32), :] = rounded16((halo_f[...] - MIDDLE) * (1.0 / STEP))
        if d:
            main_in.append(to_pair(d, enc.at[d], got.at[me_p], main_send, main_recv))
            main_in[-1].start()

    for load in tables:
        load.wait()
    row_id = lax.broadcasted_iota(jnp.int32, (piv, piv), 0)
    col_id = lax.broadcasted_iota(jnp.int32, (piv, piv), 1)
    kern = agg[...]
    part = share[...]
    low = (0.5 * kern * part).astype(BF16).astype(F32)
    high = (0.5 * kern * (1.0 - part)).astype(BF16).astype(F32)
    offset = (target[...] - jnp.maximum(row_id, col_id)).astype(F32)
    last = []
    for n, (lo, hi, off, keep) in enumerate((
        (low, high, offset, col_id <= row_id),
        (low.T, high.T, offset.T, col_id < row_id),
    )):
        for d in range(BANDS):
            band = jnp.where(off == d, lo, jnp.where(off == d - 1, hi, 0.0))
            wb[pl.ds((n * BANDS + d) * piv, piv), :] = jnp.where(keep, band, 0.0).astype(BF16)
        last.append(pltpu.roll(jnp.where(keep & (off == -1), lo, 0.0)[piv - 8:], 7, 0))
    rate_row = rate[...]
    cour_row = cour[...]
    base = 2 * BANDS * piv
    wb[pl.ds(base, piv), :] = kern.astype(BF16)
    wb[pl.ds(base + 2 * piv, 16), :] = jnp.concatenate(last, axis=0).astype(BF16)
    smaller = (row_id < col_id).astype(F32)
    wb[pl.ds(base + piv, piv), :] = (frag[...] * rate_row * smaller).astype(BF16)
    diag = row_id == col_id
    rate_col = jnp.sum(jnp.where(diag, rate_row, 0.0), axis=1, keepdims=True)
    cour_col = jnp.sum(jnp.where(diag, cour_row, 0.0), axis=1, keepdims=True)
    own_diag = (lax.broadcasted_iota(jnp.int32, (own, piv), 0) + me_p * own
                == lax.broadcasted_iota(jnp.int32, (own, piv), 1))
    own_cour = jnp.sum(jnp.where(own_diag, cour_row, 0.0), axis=1, keepdims=True)
    own_rate = jnp.sum(jnp.where(own_diag, rate_row, 0.0), axis=1, keepdims=True)
    one_hot = (lax.broadcasted_iota(jnp.int32, (width, width), 0) == face_map[...]).astype(F32).astype(BF16)

    pick_out = across(ring, ring_out, picked, picked_r, pick_send, pick_recv)

    def mixed(v):
        y_s[...] = jnp.dot(wb[...], v.astype(BF16), preferred_element_type=F32)
        vb = v.astype(BF16).astype(F32)
        below = y_s[pl.ds(base + 2 * piv, 8), :] + y_s[pl.ds(base + 2 * piv + 8, 8), :]
        y_s[pl.ds(base + 2 * piv - 8, 8), :] += below * vb[piv - 1:]
        births = None
        for d in reversed(range(BANDS)):
            here = vb * (y_s[pl.ds(d * piv, piv), :] + y_s[pl.ds((BANDS + d) * piv, piv), :])
            births = here if births is None else here + pltpu.roll(births, 1, 0)
        return births - v * y_s[pl.ds(base, piv), :] + y_s[pl.ds(base + piv, piv), :]

    def change(v, prev):
        return v + (mixed(v) - rate_col * v - cour_col * (v - prev))

    def start_row(s):
        return v0[pl.ds(s, piv, stride=8), :]

    for copy in main_in:
        copy.wait_recv()
    for p in range(n_pair):
        v0[pl.ds(p * own * 8, own * 8), :] = (
            got[p, pl.ds(0, own * 8), :].astype(jnp.int32).astype(F32) * STEP + MIDDLE)
        under = got[p, pl.ds(own * 8, 32), :].astype(jnp.int32).astype(F32) * STEP + MIDDLE
        halo_c[pl.ds(p * own, own), :] = jnp.where(grp > 0, under[:own], 0.0)

    edge = to_pair(2, sec.at[:, pl.ds(7 * 128, 128)], edge_r, edge_send, edge_recv)
    for it in reversed(range(4)):
        s = 2 * it
        before = halo_c[...] if it == 0 else start_row(s - 1)
        first, second = start_row(s), start_row(s + 1)
        now = change(jnp.concatenate([first, second], axis=1), jnp.concatenate([before, first], axis=1))
        for t in range(2):
            row = grp * 8 + s + t
            piece = jnp.where(row < live_rows, now[:, t * 128:(t + 1) * 128], 0.0)
            sec[:, pl.ds((s + t) * 128, 128)] = piece
        if it == 3:
            edge.start()

    inflow = arrived(pick_out, picked_r)
    inflow_s[...] = inflow
    inflows = [to_pair(d, inflow_s, inflow_r.at[me_p], inflow_send, inflow_recv) for d in range(1, n_pair)]
    for copy in inflows:
        copy.start()
    inflow_r[me_p] = inflow

    for t in range(2):
        cols = pl.ds(t * 128, 128)
        v = ring[y, :, cols]
        under = dens_rows[pl.ds(jnp.maximum(top_row - 1, 0) + t * own * height, own, stride=height), :]
        prev = jnp.where(top_row == 0, inflow[:, t * 128:(t + 1) * 128], under)
        ring2[y, :, cols] = v - own_cour * (v - prev) - own_rate * v
    ring2_out = along_ring(ring2, ring2_send, ring2_recv)

    def final_rows(it, before):
        v = sec[:, pl.ds(it * 256, 256)]
        now = change(v, jnp.concatenate([before, v[:, :128]], axis=1))
        return [0.5 * start_row(2 * it + t) + 0.5 * now[:, t * 128:(t + 1) * 128] for t in range(2)]

    biggest = None
    for it in reversed(range(4)):
        if it == 0:
            edge.wait_recv()
            before = edge_r[...]
        else:
            before = sec[:, pl.ds((2 * it - 1) * 128, 128)]
        for t, piece in enumerate(final_rows(it, before)):
            row = grp * 8 + 2 * it + t
            piece = jnp.where((row < live_rows) & (row >= 2), piece, 0.0)
            res[:, pl.ds((2 * it + t) * 128, 128)] = piece
            size = jnp.abs(piece)
            biggest = size if biggest is None else jnp.maximum(biggest, size)

    pick2_out = across(ring2, ring2_out, picked2, picked2_r, pick2_send, pick2_recv)

    biggest = jnp.max(biggest, axis=1, keepdims=True)
    finer = jnp.where(biggest > 0.0, 32767.0 / biggest, 0.0)
    for s in range(8):
        out_f[pl.ds(s, piv, stride=8), :] = res[:, pl.ds(s * 128, 128)] * finer
    lane = lax.broadcasted_iota(jnp.int32, (piv, 128), 1)
    wide_s[pl.ds(piv, 16), :] = jnp.zeros((16, 128), F32)
    first = jnp.floor(biggest * LEAST)
    rest = (biggest * LEAST - first) * 32768.0
    second = jnp.floor(rest)
    third = jnp.floor((rest - second) * 32768.0)
    wide_s[pl.ds(0, piv), :] = jnp.where(lane == 0, first, jnp.where(lane == 1, second, jnp.where(lane == 2, third, 0.0)))
    for p in range(n_pair):
        out_s[p, pl.ds(0, own * 8), :] = rounded16(out_f[pl.ds(p * own * 8, own * 8), :])
        out_s[p, pl.ds(own * 8, 32), :] = rounded16(wide_s[pl.ds(p * own, 32), :])
    outs = [to_pair(d, out_s.at[pairs[d]], out_r.at[me_p], out_send, out_recv) for d in ORDER]
    for copy in outs:
        copy.start()
    out_own = pltpu.make_async_copy(out_s.at[me_p], out_r.at[me_p], local_sem.at[9])
    out_own.start()

    for copy in inflows:
        copy.wait_recv()
    for p in range(n_pair):
        face[pl.ds(p * own, own), :] = inflow_r[p]

    def late_copy(p, source):
        return pltpu.make_async_remote_copy(
            src_ref=late_p.at[p], dst_ref=late_r.at[source], send_sem=late_send.at[p],
            recv_sem=late_recv.at[source], device_id=(me_b, p), device_id_type=MESH)

    @pl.when(grp == 0)
    def _():
        sec[:, :128] += cour_col * jnp.where(half == 0, face[:, :128], face[:, 128:])
        for t, piece in enumerate(final_rows(0, jnp.zeros((piv, 128), F32))):
            late_s[:, pl.ds(t * 128, 128)] = jnp.where(t < live_rows, piece, 0.0)
        for p in range(n_pair):
            late_p[p] = late_s[pl.ds(p * own, own), :]
        for p in range(n_pair):
            @pl.when(me_p != p)
            def _():
                late_copy(p, me_p).start()

            @pl.when(me_p == p)
            def _():
                late_r[min(p, 1)] = late_p[p]

    terms = mixed(face[...])
    for t in range(2):
        terms_s[pl.ds(t, piv, stride=8), :] = terms[:, t * 128:(t + 1) * 128]

    digit = lax.broadcasted_iota(jnp.int32, (own, 128), 1)
    digit_size = jnp.where(
        digit == 0, 1.0, jnp.where(digit == 1, 1.0 / 32768.0, jnp.where(digit == 2, 1.0 / 32768.0 ** 2, 0.0))
    ) * (1.0 / (LEAST * 32767.0))
    out_own.wait()
    for copy in outs:
        copy.wait_recv()
    for p in range(n_pair):
        digits = out_r[p, pl.ds(own * 8, 32), :].astype(jnp.int32).astype(F32)[:own]
        scale = jnp.sum(digits * digit_size, axis=1, keepdims=True)
        tile = out_r[p, pl.ds(0, own * 8), :].astype(jnp.int32).astype(F32).reshape(own, 8, 128) * scale[:, :, None]
        main_v[:, pl.ds((p // 2) * 8, 8), pl.ds((p % 2) * 128, 128)] = tile
    store = pltpu.make_async_copy(main_v, main, local_sem.at[10])
    store.start()

    for q in range(2):
        @pl.when(me_p != q)
        def _():
            late_copy(0, q).wait_recv()
    for t, add in enumerate((add_0, add_1)):
        for q in range(2):
            add[:, pl.ds(q * 128, 128)] = late_r[q, :, pl.ds(t * 128, 128)]
    linear = arrived(pick2_out, picked2_r)
    for t in range(2):
        cols = slice(t * 128, (t + 1) * 128)
        top = linear[:, cols] + terms_s[pl.ds(me_p * own * 8 + t, own, stride=8), :]
        add_0[:, cols] += 0.5 * own_cour * top

    store.wait()
    for copy in (ring_out + main_in + pick_out + inflows + [edge] + outs + ring2_out + pick2_out):
        copy.wait_send()

    @pl.when(grp == 0)
    def _():
        for p in range(n_pair):
            @pl.when(me_p != p)
            def _():
                late_copy(p, me_p).wait_send()


def shards(n_pair, density, agg, share, target, frag, rate, cour, block_rows, upstream, face_map):
    own, height, width = density.shape
    piv = agg.shape[0]
    vmem = pl.BlockSpec(memory_space=pltpu.VMEM)
    hbm = pl.BlockSpec(memory_space=pltpu.HBM)
    dma = pltpu.SemaphoreType.DMA
    weight_rows = (2 * BANDS + 2) * piv + 16
    main, add_0, add_1 = pl.pallas_call(
        functools.partial(step_kernel, n_pair, own, piv, height, width),
        out_shape=(
            jax.ShapeDtypeStruct(density.shape, F32),
            jax.ShapeDtypeStruct((own, width), F32),
            jax.ShapeDtypeStruct((own, width), F32),
        ),
        in_specs=[hbm] * 10,
        out_specs=(hbm, vmem, vmem),
        scratch_shapes=[
            pltpu.VMEM((piv, piv), F32),
            pltpu.VMEM((piv, piv), F32),
            pltpu.VMEM((piv, piv), jnp.int32),
            pltpu.VMEM((piv, piv), F32),
            pltpu.VMEM((1, piv), F32),
            pltpu.VMEM((1, piv), F32),
            pltpu.SMEM(block_rows.shape, jnp.int32),
            pltpu.SMEM(upstream.shape, jnp.int32),
            pltpu.VMEM(face_map.shape, jnp.int32),
            pltpu.VMEM((2, own, height, 128), F32),
            pltpu.VMEM((n_pair, own * 8 + 32, 128), I16),
            pltpu.VMEM((n_pair, own * 8 + 32, 128), I16),
            pltpu.VMEM((piv * 8, 128), F32),
            pltpu.VMEM((piv, 1024), F32),
            pltpu.VMEM((piv, 1024), F32),
            pltpu.VMEM((piv * 8, 128), F32),
            pltpu.VMEM((n_pair, own * 8 + 32, 128), I16),
            pltpu.VMEM((n_pair, own * 8 + 32, 128), I16),
            pltpu.VMEM((own, height, width), F32),
            pltpu.VMEM((weight_rows, piv), BF16),
            pltpu.VMEM((weight_rows, 256), F32),
            pltpu.VMEM((RING, own, width), F32),
            pltpu.VMEM((4, own, width), F32),
            pltpu.VMEM((4, own, width), F32),
            pltpu.VMEM((RING, own, width), F32),
            pltpu.VMEM((4, own, width), F32),
            pltpu.VMEM((4, own, width), F32),
            pltpu.VMEM((32, 128), F32),
            pltpu.VMEM((piv, 128), F32),
            pltpu.VMEM((own, width), F32),
            pltpu.VMEM((n_pair, own, width), F32),
            pltpu.VMEM((piv, width), F32),
            pltpu.VMEM((piv * 8, 128), F32),
            pltpu.VMEM((piv, 256), F32),
            pltpu.VMEM((n_pair, own, 256), F32),
            pltpu.VMEM((2, own, 256), F32),
            pltpu.VMEM((piv, 128), F32),
            pltpu.VMEM((piv + 16, 128), F32),
            dma((13,)),
            dma((n_pair,)), dma((n_pair,)),
            dma((n_pair,)), dma((n_pair,)),
            dma((n_pair,)), dma((2,)),
            dma((RING,)), dma((RING,)),
            dma((4,)), dma((4,)),
            dma((RING,)), dma((RING,)),
            dma((4,)), dma((4,)),
            dma((n_pair,)), dma((n_pair,)),
            dma((n_pair,)), dma((n_pair,)),
        ],
        compiler_params=pltpu.CompilerParams(
            collective_id=0, has_side_effects=True, vmem_limit_bytes=56 * 1024 * 1024),
    )(density, agg, share, target, frag, rate.reshape(1, piv), cour.reshape(1, piv), block_rows, upstream, face_map)
    row = lax.broadcasted_iota(jnp.int32, main.shape, 1)
    return main + jnp.where(row == 0, add_0[:, None, :], jnp.where(row == 1, add_1[:, None, :], 0.0))


def solution(mesh):
    in_specs = (P("pair", "blk", None), P(), P(), P(), P(), P(), P(), P(), P(), P("blk", None))
    out_specs = P("pair", "blk", None)
    return jax.shard_map(
        functools.partial(shards, mesh.shape["pair"]),
        mesh=mesh, in_specs=in_specs, out_specs=out_specs, check_vma=False)
```

```python
import functools

import jax
import jax.numpy as jnp
from jax import lax
from jax.experimental import pallas as pl
from jax.experimental.pallas import tpu as pltpu
from jax.sharding import PartitionSpec as P

MESH = pl.DeviceIdType.MESH
BANDS = 5
F32 = jnp.float32
BF16 = jnp.bfloat16
I16 = jnp.int16
RING, CORES = 4, 2
ORDER = (4, 3, 5, 2, 6, 1, 7)
MIDDLE = 1.025
STEP = 1.95 / 65534.0
LEAST = 32768.0 / 65536.0


def permuted(face, one_hot):
    total = None
    for _ in range(3):
        part = face.astype(BF16)
        face = face - part.astype(F32)
        moved = jnp.dot(part, one_hot, preferred_element_type=F32)
        total = moved if total is None else total + moved
    return total


def rounded16(x):
    return jnp.round(x).astype(jnp.int32).astype(I16)


def step_kernel(
    n_pair, own, piv, height, width,
    density, agg_h, share_h, target_h, frag_h, rate_h, cour_h, rows_h, up_h, map_h,
    main, add_0, add_1,
    agg, share, target, frag, rate, cour, rows_sm, up_sm, face_map, dens_v, enc, got, v0, sec, res, out_f, out_s, out_r, wb, y_s,
    ring, picked, picked_r, ring2, picked2, picked2_r,
    halo_f, halo_c, inflow_s, inflow_r, face, terms_s, late_s, late_p, late_r, edge, wide_s,
    local_sem, main_send, main_recv, inflow_send, inflow_recv, late_send, late_recv,
    ring_send, ring_recv, pick_send, pick_recv, ring2_send, ring2_recv, pick2_send, pick2_recv,
    out_send, out_recv,
):
    me_b, me_p = lax.axis_index("blk"), lax.axis_index("pair")
    grp, half = me_p // 2, me_p % 2
    z_hi, y, core = me_b // (RING * CORES), (me_b // CORES) % RING, me_b % CORES
    pairs = [(me_p + d) % n_pair for d in range(n_pair)]

    def block_at(dz, dy, dc):
        return ((z_hi + dz) % 2) * (RING * CORES) + ((y + dy) % RING) * CORES + (core + dc) % CORES

    ring_mates = [block_at(0, d, 0) for d in range(RING)]
    pick_mates = [block_at(q // 2, 0, q % 2) for q in range(4)]

    barrier = pltpu.get_barrier_semaphore()
    for p in pairs[1:]:
        pl.semaphore_signal(barrier, inc=1, device_id=(me_b, p), device_id_type=MESH)
    for b in ring_mates[1:] + pick_mates[1:]:
        pl.semaphore_signal(barrier, inc=1, device_id=(b, me_p), device_id_type=MESH)

    loads = [pltpu.make_async_copy(density.at[:, :, pl.ds(t * 128, 128)], dens_v.at[t], local_sem.at[t])
             for t in range(2)]
    for load in loads:
        load.start()
    scalars = [pltpu.make_async_copy(rows_h, rows_sm, local_sem.at[11]),
               pltpu.make_async_copy(up_h, up_sm, local_sem.at[12])]
    for load in scalars:
        load.start()
    tables = [pltpu.make_async_copy(src, dst, local_sem.at[2 + n]) for n, (src, dst) in enumerate(
        ((agg_h, agg), (share_h, share), (target_h, target), (frag_h, frag),
         (rate_h, rate), (cour_h, cour), (map_h, face_map)))]
    for load in tables:
        load.start()

    def to_pair(d, src, dst, send, recv):
        return pltpu.make_async_remote_copy(
            src_ref=src, dst_ref=dst, send_sem=send.at[d], recv_sem=recv.at[d],
            device_id=(me_b, pairs[d]), device_id_type=MESH)

    def to_block(b, d, src, dst, send, recv):
        return pltpu.make_async_remote_copy(
            src_ref=src, dst_ref=dst, send_sem=send.at[d], recv_sem=recv.at[d],
            device_id=(b, me_p), device_id_type=MESH)

    def along_ring(faces, send, recv):
        copies = [to_block(ring_mates[d], d, faces.at[y], faces.at[y], send, recv) for d in range(1, RING)]
        for copy in copies:
            copy.start()
        return copies

    def across(faces, copies, chosen, chosen_r, send, recv):
        for copy in copies:
            copy.wait_recv()
        for q in range(1, 4):
            chosen[q] = faces[(up_sm[pick_mates[q]] // CORES) % RING]
        more = [to_block(pick_mates[q], q, chosen.at[q], chosen_r.at[q], send, recv) for q in range(1, 4)]
        for copy in more:
            copy.start()
        chosen_r[0] = faces[(up_sm[me_b] // CORES) % RING]
        return more

    def arrived(copies, chosen_r):
        for copy in copies:
            copy.wait_recv()
        u = up_sm[me_b]
        q = ((u // (RING * CORES) + z_hi) % 2) * 2 + (u + core) % 2
        return permuted(chosen_r[q], one_hot)

    halo_f[...] = jnp.zeros(halo_f.shape, F32)
    for load in scalars:
        load.wait()
    live_rows = rows_sm[me_b]
    top_row = live_rows - 1
    for load in loads:
        load.wait()
    dens_rows = dens_v.reshape(2 * own * height, 128)
    for t in range(2):
        ring[y, :, pl.ds(t * 128, 128)] = dens_rows[
            pl.ds(jnp.maximum(top_row, 0) + t * own * height, own, stride=height), :]
    pl.semaphore_wait(barrier, len(pairs) + len(ring_mates) + len(pick_mates) - 3)
    ring_out = along_ring(ring, ring_send, ring_recv)

    main_in = []
    for d in ORDER + (0,):
        p = pairs[d]
        tile = dens_v[p % 2, :, pl.ds(pl.multiple_of((p // 2) * 8, 8), 8), :].reshape(own * 8, 128)
        for n in range(2):
            under = jnp.maximum((p // 2) * 8 - 1 - n, 0) + (p % 2) * own * height
            halo_f[pl.ds(n * own, own), :] = dens_rows[pl.ds(under, own, stride=height), :]
        goal = enc.at[d] if d else got.at[me_p]
        goal[pl.ds(0, own * 8), :] = rounded16((tile - MIDDLE) * (1.0 / STEP))
        goal[pl.ds(own * 8, 48), :] = rounded16((halo_f[...] - MIDDLE) * (1.0 / STEP))
        if d:
            main_in.append(to_pair(d, enc.at[d], got.at[me_p], main_send, main_recv))
            main_in[-1].start()

    for load in tables:
        load.wait()
    row_id = lax.broadcasted_iota(jnp.int32, (piv, piv), 0)
    col_id = lax.broadcasted_iota(jnp.int32, (piv, piv), 1)
    kern = agg[...]
    part = share[...]
    low = (0.5 * kern * part).astype(BF16).astype(F32)
    high = (0.5 * kern * (1.0 - part)).astype(BF16).astype(F32)
    offset = (target[...] - jnp.maximum(row_id, col_id)).astype(F32)
    triangles = ((low, high, offset, col_id <= row_id), (low.T, high.T, offset.T, col_id < row_id))
    for d in range(BANDS):
        pair = [jnp.where(keep, jnp.where(off == d, lo, jnp.where(off == d - 1, hi, 0.0)), 0.0)
                for lo, hi, off, keep in triangles]
        wb[pl.ds(d * piv, piv), :] = (pair[0] + pair[1]).astype(BF16)
    pair = [jnp.where(keep & (off == -1), lo, 0.0)[piv - 8:] for lo, hi, off, keep in triangles]
    last = pltpu.roll(pair[0] + pair[1], 7, 0)
    rate_row = rate[...]
    cour_row = cour[...]
    base = BANDS * piv
    wb[pl.ds(base, piv), :] = kern.astype(BF16)
    wb[pl.ds(base + 2 * piv, 16), :] = jnp.concatenate([last, jnp.zeros_like(last)], axis=0).astype(BF16)
    smaller = (row_id < col_id).astype(F32)
    wb[pl.ds(base + piv, piv), :] = (frag[...] * rate_row * smaller).astype(BF16)
    diag = row_id == col_id
    rate_col = jnp.sum(jnp.where(diag, rate_row, 0.0), axis=1, keepdims=True)
    cour_col = jnp.sum(jnp.where(diag, cour_row, 0.0), axis=1, keepdims=True)
    own_diag = (lax.broadcasted_iota(jnp.int32, (own, piv), 0) + me_p * own
                == lax.broadcasted_iota(jnp.int32, (own, piv), 1))
    own_cour = jnp.sum(jnp.where(own_diag, cour_row, 0.0), axis=1, keepdims=True)
    own_rate = jnp.sum(jnp.where(own_diag, rate_row, 0.0), axis=1, keepdims=True)
    one_hot = (lax.broadcasted_iota(jnp.int32, (width, width), 0) == face_map[...]).astype(F32).astype(BF16)

    pick_out = across(ring, ring_out, picked, picked_r, pick_send, pick_recv)

    def mixed(v):
        y_s[:, :v.shape[1]] = jnp.dot(wb[...], v.astype(BF16), preferred_element_type=F32)
        vb = v.astype(BF16).astype(F32)
        cols = slice(0, v.shape[1])
        y_s[pl.ds(base + 2 * piv - 8, 8), cols] += y_s[pl.ds(base + 2 * piv, 8), cols] * vb[piv - 1:]
        births = None
        for d in reversed(range(BANDS)):
            here = vb * y_s[pl.ds(d * piv, piv), cols]
            births = here if births is None else here + pltpu.roll(births, 1, 0)
        return births - v * y_s[pl.ds(base, piv), cols] + y_s[pl.ds(base + piv, piv), cols]

    def change(v, prev):
        return v + (mixed(v) - rate_col * v - cour_col * (v - prev))

    def start_row(s):
        return v0[pl.ds(s, piv, stride=8), :]

    def first_inflow():
        inflow = arrived(pick_out, picked_r)
        inflow_s[...] = inflow
        inflows = [to_pair(d, inflow_s, inflow_r.at[me_p], inflow_send, inflow_recv) for d in range(1, n_pair)]
        for copy in inflows:
            copy.start()
        inflow_r[me_p] = inflow

        for t in range(2):
            cols = pl.ds(t * 128, 128)
            v = ring[y, :, cols]
            under = dens_rows[pl.ds(jnp.maximum(top_row - 1, 0) + t * own * height, own, stride=height), :]
            prev = jnp.where(top_row == 0, inflow[:, t * 128:(t + 1) * 128], under)
            ring2[y, :, cols] = v - own_cour * (v - prev) - own_rate * v
        ring2_out = along_ring(ring2, ring2_send, ring2_recv)
        return inflow, inflows, ring2_out

    for copy in main_in:
        copy.wait_recv()
    for p in range(n_pair):
        v0[pl.ds(p * own * 8, own * 8), :] = (
            got[p, pl.ds(0, own * 8), :].astype(jnp.int32).astype(F32) * STEP + MIDDLE)
        halo_f[...] = got[p, pl.ds(own * 8, 48), :].astype(jnp.int32).astype(F32) * STEP + MIDDLE
        for n in range(2):
            halo_c[n, pl.ds(p * own, own), :] = jnp.where(grp > 0, halo_f[pl.ds(n * own, own), :], 0.0)

    for it in reversed(range(4)):
        s = 2 * it
        before = halo_c[0] if it == 0 else start_row(s - 1)
        first, second = start_row(s), start_row(s + 1)
        now = change(jnp.concatenate([first, second], axis=1), jnp.concatenate([before, first], axis=1))
        for t in range(2):
            row = grp * 8 + s + t
            piece = jnp.where(row < live_rows, now[:, t * 128:(t + 1) * 128], 0.0)
            sec[:, pl.ds((s + t) * 128, 128)] = piece
        if it == 2:
            inflow, inflows, ring2_out = first_inflow()
    edge[...] = change(halo_c[0], halo_c[1])

    def final_rows(it, before):
        v = sec[:, pl.ds(it * 256, 256)]
        now = change(v, jnp.concatenate([before, v[:, :128]], axis=1))
        return [0.5 * start_row(2 * it + t) + 0.5 * now[:, t * 128:(t + 1) * 128] for t in range(2)]

    biggest = None
    for it in reversed(range(4)):
        if it == 0:
            before = edge[...]
        else:
            before = sec[:, pl.ds((2 * it - 1) * 128, 128)]
        for t, piece in enumerate(final_rows(it, before)):
            row = grp * 8 + 2 * it + t
            piece = jnp.where((row < live_rows) & (row >= 2), piece, 0.0)
            res[:, pl.ds((2 * it + t) * 128, 128)] = piece
            size = jnp.abs(piece)
            biggest = size if biggest is None else jnp.maximum(biggest, size)

    pick2_out = across(ring2, ring2_out, picked2, picked2_r, pick2_send, pick2_recv)

    biggest = jnp.max(biggest, axis=1, keepdims=True)
    finer = jnp.where(biggest > 0.0, 32767.0 / biggest, 0.0)
    for s in range(8):
        out_f[pl.ds(s, piv, stride=8), :] = res[:, pl.ds(s * 128, 128)] * finer
    lane = lax.broadcasted_iota(jnp.int32, (piv, 128), 1)
    wide_s[pl.ds(piv, 16), :] = jnp.zeros((16, 128), F32)
    first = jnp.floor(biggest * LEAST)
    rest = (biggest * LEAST - first) * 32768.0
    second = jnp.floor(rest)
    third = jnp.floor((rest - second) * 32768.0)
    wide_s[pl.ds(0, piv), :] = jnp.where(lane == 0, first, jnp.where(lane == 1, second, jnp.where(lane == 2, third, 0.0)))
    for p in range(n_pair):
        out_s[p, pl.ds(0, own * 8), :] = rounded16(out_f[pl.ds(p * own * 8, own * 8), :])
        out_s[p, pl.ds(own * 8, 32), :] = rounded16(wide_s[pl.ds(p * own, 32), :])
    outs = [to_pair(d, out_s.at[pairs[d]], out_r.at[me_p], out_send, out_recv) for d in ORDER]
    for copy in outs:
        copy.start()
    out_own = pltpu.make_async_copy(out_s.at[me_p], out_r.at[me_p], local_sem.at[9])
    out_own.start()

    for copy in inflows:
        copy.wait_recv()
    for p in range(n_pair):
        face[pl.ds(p * own, own), :] = inflow_r[p]

    def late_copy(p, source):
        return pltpu.make_async_remote_copy(
            src_ref=late_p.at[p], dst_ref=late_r.at[source], send_sem=late_send.at[p],
            recv_sem=late_recv.at[source], device_id=(me_b, p), device_id_type=MESH)

    @pl.when(grp == 0)
    def _():
        sec[:, :128] += cour_col * jnp.where(half == 0, face[:, :128], face[:, 128:])
        for t, piece in enumerate(final_rows(0, jnp.zeros((piv, 128), F32))):
            late_s[:, pl.ds(t * 128, 128)] = jnp.where(t < live_rows, piece, 0.0)
        for p in range(n_pair):
            late_p[p] = late_s[pl.ds(p * own, own), :]
        for p in range(n_pair):
            @pl.when(me_p != p)
            def _():
                late_copy(p, me_p).start()

            @pl.when(me_p == p)
            def _():
                late_r[min(p, 1)] = late_p[p]

    terms = mixed(face[...])
    for t in range(2):
        terms_s[pl.ds(t, piv, stride=8), :] = terms[:, t * 128:(t + 1) * 128]

    digit = lax.broadcasted_iota(jnp.int32, (own, 128), 1)
    digit_size = jnp.where(
        digit == 0, 1.0, jnp.where(digit == 1, 1.0 / 32768.0, jnp.where(digit == 2, 1.0 / 32768.0 ** 2, 0.0))
    ) * (1.0 / (LEAST * 32767.0))
    out_own.wait()
    for copy in outs:
        copy.wait_recv()
    for p in range(n_pair):
        digits = out_r[p, pl.ds(own * 8, 32), :].astype(jnp.int32).astype(F32)[:own]
        scale = jnp.sum(digits * digit_size, axis=1, keepdims=True)
        tile = out_r[p, pl.ds(0, own * 8), :].astype(jnp.int32).astype(F32).reshape(own, 8, 128) * scale[:, :, None]
        main[:, pl.ds((p // 2) * 8, 8), pl.ds((p % 2) * 128, 128)] = tile

    for q in range(2):
        @pl.when(me_p != q)
        def _():
            late_copy(0, q).wait_recv()
    for t, add in enumerate((add_0, add_1)):
        for q in range(2):
            add[:, pl.ds(q * 128, 128)] = late_r[q, :, pl.ds(t * 128, 128)]
    linear = arrived(pick2_out, picked2_r)
    for t in range(2):
        cols = slice(t * 128, (t + 1) * 128)
        top = linear[:, cols] + terms_s[pl.ds(me_p * own * 8 + t, own, stride=8), :]
        add_0[:, cols] += 0.5 * own_cour * top

    for copy in (ring_out + main_in + pick_out + inflows + outs + ring2_out + pick2_out):
        copy.wait_send()

    @pl.when(grp == 0)
    def _():
        for p in range(n_pair):
            @pl.when(me_p != p)
            def _():
                late_copy(p, me_p).wait_send()


def shards(n_pair, density, agg, share, target, frag, rate, cour, block_rows, upstream, face_map):
    own, height, width = density.shape
    piv = agg.shape[0]
    vmem = pl.BlockSpec(memory_space=pltpu.VMEM)
    hbm = pl.BlockSpec(memory_space=pltpu.HBM)
    dma = pltpu.SemaphoreType.DMA
    weight_rows = (BANDS + 2) * piv + 16
    main, add_0, add_1 = pl.pallas_call(
        functools.partial(step_kernel, n_pair, own, piv, height, width),
        out_shape=(
            jax.ShapeDtypeStruct(density.shape, F32),
            jax.ShapeDtypeStruct((own, width), F32),
            jax.ShapeDtypeStruct((own, width), F32),
        ),
        in_specs=[hbm] * 10,
        out_specs=(vmem, vmem, vmem),
        scratch_shapes=[
            pltpu.VMEM((piv, piv), F32),
            pltpu.VMEM((piv, piv), F32),
            pltpu.VMEM((piv, piv), jnp.int32),
            pltpu.VMEM((piv, piv), F32),
            pltpu.VMEM((1, piv), F32),
            pltpu.VMEM((1, piv), F32),
            pltpu.SMEM(block_rows.shape, jnp.int32),
            pltpu.SMEM(upstream.shape, jnp.int32),
            pltpu.VMEM(face_map.shape, jnp.int32),
            pltpu.VMEM((2, own, height, 128), F32),
            pltpu.VMEM((n_pair, own * 8 + 48, 128), I16),
            pltpu.VMEM((n_pair, own * 8 + 48, 128), I16),
            pltpu.VMEM((piv * 8, 128), F32),
            pltpu.VMEM((piv, 1024), F32),
            pltpu.VMEM((piv, 1024), F32),
            pltpu.VMEM((piv * 8, 128), F32),
            pltpu.VMEM((n_pair, own * 8 + 32, 128), I16),
            pltpu.VMEM((n_pair, own * 8 + 32, 128), I16),
            pltpu.VMEM((weight_rows, piv), BF16),
            pltpu.VMEM((weight_rows, 256), F32),
            pltpu.VMEM((RING, own, width), F32),
            pltpu.VMEM((4, own, width), F32),
            pltpu.VMEM((4, own, width), F32),
            pltpu.VMEM((RING, own, width), F32),
            pltpu.VMEM((4, own, width), F32),
            pltpu.VMEM((4, own, width), F32),
            pltpu.VMEM((48, 128), F32),
            pltpu.VMEM((2, piv, 128), F32),
            pltpu.VMEM((own, width), F32),
            pltpu.VMEM((n_pair, own, width), F32),
            pltpu.VMEM((piv, width), F32),
            pltpu.VMEM((piv * 8, 128), F32),
            pltpu.VMEM((piv, 256), F32),
            pltpu.VMEM((n_pair, own, 256), F32),
            pltpu.VMEM((2, own, 256), F32),
            pltpu.VMEM((piv, 128), F32),
            pltpu.VMEM((piv + 16, 128), F32),
            dma((13,)),
            dma((n_pair,)), dma((n_pair,)),
            dma((n_pair,)), dma((n_pair,)),
            dma((n_pair,)), dma((2,)),
            dma((RING,)), dma((RING,)),
            dma((4,)), dma((4,)),
            dma((RING,)), dma((RING,)),
            dma((4,)), dma((4,)),
            dma((n_pair,)), dma((n_pair,)),
        ],
        compiler_params=pltpu.CompilerParams(
            collective_id=0, has_side_effects=True, vmem_limit_bytes=56 * 1024 * 1024),
    )(density, agg, share, target, frag, rate.reshape(1, piv), cour.reshape(1, piv), block_rows, upstream, face_map)
    row = lax.broadcasted_iota(jnp.int32, main.shape, 1)
    return main + jnp.where(row == 0, add_0[:, None, :], jnp.where(row == 1, add_1[:, None, :], 0.0))


def solution(mesh):
    in_specs = (P("pair", "blk", None), P(), P(), P(), P(), P(), P(), P(), P(), P("blk", None))
    out_specs = P("pair", "blk", None)
    return jax.shard_map(
        functools.partial(shards, mesh.shape["pair"]),
        mesh=mesh, in_specs=in_specs, out_specs=out_specs, check_vma=False)
```

```python
import functools

import jax
import jax.numpy as jnp
from jax import lax
from jax.experimental import pallas as pl
from jax.experimental.pallas import tpu as pltpu
from jax.sharding import PartitionSpec as P

MESH = pl.DeviceIdType.MESH
BANDS = 5
F32 = jnp.float32
BF16 = jnp.bfloat16
I16 = jnp.int16
RING, CORES = 4, 2
ORDER = (4, 3, 5, 2, 6, 1, 7)
MIDDLE = 1.025
STEP = 1.95 / 65534.0
LEAST = 32768.0 / 65536.0


def permuted(face, one_hot):
    total = None
    for _ in range(3):
        part = face.astype(BF16)
        face = face - part.astype(F32)
        moved = jnp.dot(part, one_hot, preferred_element_type=F32)
        total = moved if total is None else total + moved
    return total


def rounded16(x):
    return jnp.round(x).astype(jnp.int32).astype(I16)


def step_kernel(
    n_pair, own, piv, height, width,
    density, agg_h, share_h, target_h, frag_h, rate_h, cour_h, rows_h, up_h, map_h,
    main, add_0, add_1,
    agg, share, target, frag, rate, cour, rows_sm, up_sm, face_map, dens_v, enc, got, v0, sec, res, out_f, out_s, out_r, wb, y_s,
    ring, picked, picked_r, ring2, picked2, picked2_r,
    halo_f, halo_c, inflow_s, inflow_r, face, terms_s, late_s, late_p, late_r, edge, wide_s,
    local_sem, main_send, main_recv, inflow_send, inflow_recv, late_send, late_recv,
    ring_send, ring_recv, pick_send, pick_recv, ring2_send, ring2_recv, pick2_send, pick2_recv,
    out_send, out_recv,
):
    me_b, me_p = lax.axis_index("blk"), lax.axis_index("pair")
    grp, half = me_p // 2, me_p % 2
    z_hi, y, core = me_b // (RING * CORES), (me_b // CORES) % RING, me_b % CORES
    pairs = [(me_p + d) % n_pair for d in range(n_pair)]

    def block_at(dz, dy, dc):
        return ((z_hi + dz) % 2) * (RING * CORES) + ((y + dy) % RING) * CORES + (core + dc) % CORES

    ring_mates = [block_at(0, d, 0) for d in range(RING)]
    pick_mates = [block_at(q // 2, 0, q % 2) for q in range(4)]

    barrier = pltpu.get_barrier_semaphore()
    for p in pairs[1:]:
        pl.semaphore_signal(barrier, inc=1, device_id=(me_b, p), device_id_type=MESH)
    for b in ring_mates[1:] + pick_mates[1:]:
        pl.semaphore_signal(barrier, inc=1, device_id=(b, me_p), device_id_type=MESH)

    loads = [pltpu.make_async_copy(density.at[:, :, pl.ds(t * 128, 128)], dens_v.at[t], local_sem.at[t])
             for t in range(2)]
    for load in loads:
        load.start()
    scalars = [pltpu.make_async_copy(rows_h, rows_sm, local_sem.at[11]),
               pltpu.make_async_copy(up_h, up_sm, local_sem.at[12])]
    for load in scalars:
        load.start()
    tables = [pltpu.make_async_copy(src, dst, local_sem.at[2 + n]) for n, (src, dst) in enumerate(
        ((agg_h, agg), (share_h, share), (target_h, target), (frag_h, frag),
         (rate_h, rate), (cour_h, cour), (map_h, face_map)))]
    for load in tables:
        load.start()

    def to_pair(d, src, dst, send, recv):
        return pltpu.make_async_remote_copy(
            src_ref=src, dst_ref=dst, send_sem=send.at[d], recv_sem=recv.at[d],
            device_id=(me_b, pairs[d]), device_id_type=MESH)

    def to_block(b, d, src, dst, send, recv):
        return pltpu.make_async_remote_copy(
            src_ref=src, dst_ref=dst, send_sem=send.at[d], recv_sem=recv.at[d],
            device_id=(b, me_p), device_id_type=MESH)

    def along_ring(faces, send, recv):
        copies = [to_block(ring_mates[d], d, faces.at[y], faces.at[y], send, recv) for d in range(1, RING)]
        for copy in copies:
            copy.start()
        return copies

    def across(faces, copies, chosen, chosen_r, send, recv):
        for copy in copies:
            copy.wait_recv()
        for q in range(1, 4):
            chosen[q] = faces[(up_sm[pick_mates[q]] // CORES) % RING]
        more = [to_block(pick_mates[q], q, chosen.at[q], chosen_r.at[q], send, recv) for q in range(1, 4)]
        for copy in more:
            copy.start()
        chosen_r[0] = faces[(up_sm[me_b] // CORES) % RING]
        return more

    def arrived(copies, chosen_r):
        for copy in copies:
            copy.wait_recv()
        u = up_sm[me_b]
        q = ((u // (RING * CORES) + z_hi) % 2) * 2 + (u + core) % 2
        return permuted(chosen_r[q], one_hot)

    halo_f[...] = jnp.zeros(halo_f.shape, F32)
    for load in scalars:
        load.wait()
    live_rows = rows_sm[me_b]
    top_row = live_rows - 1
    for load in loads:
        load.wait()
    dens_rows = dens_v.reshape(2 * own * height, 128)
    for t in range(2):
        ring[y, :, pl.ds(t * 128, 128)] = dens_rows[
            pl.ds(jnp.maximum(top_row, 0) + t * own * height, own, stride=height), :]
    pl.semaphore_wait(barrier, len(pairs) + len(ring_mates) + len(pick_mates) - 3)
    ring_out = along_ring(ring, ring_send, ring_recv)

    main_in = []
    for d in ORDER + (0,):
        p = pairs[d]
        tile = dens_v[p % 2, :, pl.ds(pl.multiple_of((p // 2) * 8, 8), 8), :].reshape(own * 8, 128)
        for n in range(2):
            under = jnp.maximum((p // 2) * 8 - 1 - n, 0) + (p % 2) * own * height
            halo_f[pl.ds(n * own, own), :] = dens_rows[pl.ds(under, own, stride=height), :]
        goal = enc.at[d] if d else got.at[me_p]
        goal[pl.ds(0, own * 8), :] = rounded16((tile - MIDDLE) * (1.0 / STEP))
        goal[pl.ds(own * 8, 48), :] = rounded16((halo_f[...] - MIDDLE) * (1.0 / STEP))
        if d:
            main_in.append(to_pair(d, enc.at[d], got.at[me_p], main_send, main_recv))
            main_in[-1].start()

    for load in tables:
        load.wait()
    row_id = lax.broadcasted_iota(jnp.int32, (piv, piv), 0)
    col_id = lax.broadcasted_iota(jnp.int32, (piv, piv), 1)
    kern = agg[...]
    part = share[...]
    low = (0.5 * kern * part).astype(BF16).astype(F32)
    high = (0.5 * kern * (1.0 - part)).astype(BF16).astype(F32)
    offset = (target[...] - jnp.maximum(row_id, col_id)).astype(F32)
    triangles = ((low, high, offset, col_id <= row_id), (low.T, high.T, offset.T, col_id < row_id))
    for d in range(BANDS):
        pair = [jnp.where(keep, jnp.where(off == d, lo, jnp.where(off == d - 1, hi, 0.0)), 0.0)
                for lo, hi, off, keep in triangles]
        wb[pl.ds(d * piv, piv), :] = (pair[0] + pair[1]).astype(BF16)
    pair = [jnp.where(keep & (off == -1), lo, 0.0)[piv - 8:] for lo, hi, off, keep in triangles]
    last = pltpu.roll(pair[0] + pair[1], 7, 0)
    rate_row = rate[...]
    cour_row = cour[...]
    base = BANDS * piv
    wb[pl.ds(base, piv), :] = kern.astype(BF16)
    wb[pl.ds(base + 2 * piv, 16), :] = jnp.concatenate([last, jnp.zeros_like(last)], axis=0).astype(BF16)
    smaller = (row_id < col_id).astype(F32)
    wb[pl.ds(base + piv, piv), :] = (frag[...] * rate_row * smaller).astype(BF16)
    diag = row_id == col_id
    rate_col = jnp.sum(jnp.where(diag, rate_row, 0.0), axis=1, keepdims=True)
    cour_col = jnp.sum(jnp.where(diag, cour_row, 0.0), axis=1, keepdims=True)
    own_diag = (lax.broadcasted_iota(jnp.int32, (own, piv), 0) + me_p * own
                == lax.broadcasted_iota(jnp.int32, (own, piv), 1))
    own_cour = jnp.sum(jnp.where(own_diag, cour_row, 0.0), axis=1, keepdims=True)
    own_rate = jnp.sum(jnp.where(own_diag, rate_row, 0.0), axis=1, keepdims=True)
    one_hot = (lax.broadcasted_iota(jnp.int32, (width, width), 0) == face_map[...]).astype(F32).astype(BF16)

    pick_out = across(ring, ring_out, picked, picked_r, pick_send, pick_recv)

    def mixed(v):
        y_s[:, :v.shape[1]] = jnp.dot(wb[...], v.astype(BF16), preferred_element_type=F32)
        vb = v.astype(BF16).astype(F32)
        cols = slice(0, v.shape[1])
        y_s[pl.ds(base + 2 * piv - 8, 8), cols] += y_s[pl.ds(base + 2 * piv, 8), cols] * vb[piv - 1:]
        births = None
        for d in reversed(range(BANDS)):
            here = vb * y_s[pl.ds(d * piv, piv), cols]
            births = here if births is None else here + pltpu.roll(births, 1, 0)
        return births - v * y_s[pl.ds(base, piv), cols] + y_s[pl.ds(base + piv, piv), cols]

    def change(v, prev):
        return v + (mixed(v) - rate_col * v - cour_col * (v - prev))

    def start_row(s):
        return v0[pl.ds(s, piv, stride=8), :]

    def first_inflow():
        inflow = arrived(pick_out, picked_r)
        inflow_s[...] = inflow
        inflows = [to_pair(d, inflow_s, inflow_r.at[me_p], inflow_send, inflow_recv) for d in range(1, n_pair)]
        for copy in inflows:
            copy.start()
        inflow_r[me_p] = inflow

        for t in range(2):
            cols = pl.ds(t * 128, 128)
            v = ring[y, :, cols]
            under = dens_rows[pl.ds(jnp.maximum(top_row - 1, 0) + t * own * height, own, stride=height), :]
            prev = jnp.where(top_row == 0, inflow[:, t * 128:(t + 1) * 128], under)
            ring2[y, :, cols] = v - own_cour * (v - prev) - own_rate * v
        ring2_out = along_ring(ring2, ring2_send, ring2_recv)
        return inflow, inflows, ring2_out

    for copy in main_in:
        copy.wait_recv()
    for p in range(n_pair):
        v0[pl.ds(p * own * 8, own * 8), :] = (
            got[p, pl.ds(0, own * 8), :].astype(jnp.int32).astype(F32) * STEP + MIDDLE)
        halo_f[...] = got[p, pl.ds(own * 8, 48), :].astype(jnp.int32).astype(F32) * STEP + MIDDLE
        for n in range(2):
            halo_c[n, pl.ds(p * own, own), :] = jnp.where(grp > 0, halo_f[pl.ds(n * own, own), :], 0.0)

    for it in reversed(range(4)):
        s = 2 * it
        before = halo_c[0] if it == 0 else start_row(s - 1)
        first, second = start_row(s), start_row(s + 1)
        now = change(jnp.concatenate([first, second], axis=1), jnp.concatenate([before, first], axis=1))
        for t in range(2):
            row = grp * 8 + s + t
            piece = jnp.where(row < live_rows, now[:, t * 128:(t + 1) * 128], 0.0)
            sec[:, pl.ds((s + t) * 128, 128)] = piece
        if it == 2:
            inflow, inflows, ring2_out = first_inflow()
    edge[...] = change(halo_c[0], halo_c[1])

    def final_rows(it, before):
        v = sec[:, pl.ds(it * 256, 256)]
        now = change(v, jnp.concatenate([before, v[:, :128]], axis=1))
        return [0.5 * start_row(2 * it + t) + 0.5 * now[:, t * 128:(t + 1) * 128] for t in range(2)]

    biggest = None
    for it in reversed(range(4)):
        if it == 0:
            before = edge[...]
        else:
            before = sec[:, pl.ds((2 * it - 1) * 128, 128)]
        for t, piece in enumerate(final_rows(it, before)):
            row = grp * 8 + 2 * it + t
            piece = jnp.where((row < live_rows) & (row >= 2), piece, 0.0)
            res[:, pl.ds((2 * it + t) * 128, 128)] = piece
            size = jnp.abs(piece)
            biggest = size if biggest is None else jnp.maximum(biggest, size)

    pick2_out = across(ring2, ring2_out, picked2, picked2_r, pick2_send, pick2_recv)

    biggest = jnp.max(biggest, axis=1, keepdims=True)
    finer = jnp.where(biggest > 0.0, 32767.0 / biggest, 0.0)
    for s in range(8):
        out_f[pl.ds(s, piv, stride=8), :] = res[:, pl.ds(s * 128, 128)] * finer
    lane = lax.broadcasted_iota(jnp.int32, (piv, 128), 1)
    wide_s[pl.ds(piv, 16), :] = jnp.zeros((16, 128), F32)
    first = jnp.floor(biggest * LEAST)
    rest = (biggest * LEAST - first) * 32768.0
    second = jnp.floor(rest)
    third = jnp.floor((rest - second) * 32768.0)
    wide_s[pl.ds(0, piv), :] = jnp.where(lane == 0, first, jnp.where(lane == 1, second, jnp.where(lane == 2, third, 0.0)))
    for p in range(n_pair):
        out_s[p, pl.ds(0, own * 8), :] = rounded16(out_f[pl.ds(p * own * 8, own * 8), :])
        out_s[p, pl.ds(own * 8, 32), :] = rounded16(wide_s[pl.ds(p * own, 32), :])
    outs = [to_pair(d, out_s.at[pairs[d]], out_r.at[me_p], out_send, out_recv) for d in ORDER]
    for copy in outs:
        copy.start()
    out_own = pltpu.make_async_copy(out_s.at[me_p], out_r.at[me_p], local_sem.at[9])
    out_own.start()

    for copy in inflows:
        copy.wait_recv()
    for p in range(n_pair):
        face[pl.ds(p * own, own), :] = inflow_r[p]

    def late_copy(p, source):
        return pltpu.make_async_remote_copy(
            src_ref=late_p.at[p], dst_ref=late_r.at[source], send_sem=late_send.at[p],
            recv_sem=late_recv.at[source], device_id=(me_b, p), device_id_type=MESH)

    @pl.when(grp == 0)
    def _():
        sec[:, :128] += cour_col * jnp.where(half == 0, face[:, :128], face[:, 128:])
        for t, piece in enumerate(final_rows(0, jnp.zeros((piv, 128), F32))):
            late_s[:, pl.ds(t * 128, 128)] = jnp.where(t < live_rows, piece, 0.0)
        for p in range(n_pair):
            late_p[p] = late_s[pl.ds(p * own, own), :]
        for p in range(n_pair):
            @pl.when(me_p != p)
            def _():
                late_copy(p, me_p).start()

            @pl.when(me_p == p)
            def _():
                late_r[min(p, 1)] = late_p[p]

    terms = mixed(face[...])
    for t in range(2):
        terms_s[pl.ds(t, piv, stride=8), :] = terms[:, t * 128:(t + 1) * 128]

    digit = lax.broadcasted_iota(jnp.int32, (own, 128), 1)
    digit_size = jnp.where(
        digit == 0, 1.0, jnp.where(digit == 1, 1.0 / 32768.0, jnp.where(digit == 2, 1.0 / 32768.0 ** 2, 0.0))
    ) * (1.0 / (LEAST * 32767.0))
    out_own.wait()
    for copy in outs:
        copy.wait_recv()
    for p in range(n_pair):
        digits = out_r[p, pl.ds(own * 8, 32), :].astype(jnp.int32).astype(F32)[:own]
        scale = jnp.sum(digits * digit_size, axis=1, keepdims=True)
        tile = out_r[p, pl.ds(0, own * 8), :].astype(jnp.int32).astype(F32).reshape(own, 8, 128) * scale[:, :, None]
        main[:, pl.ds((p // 2) * 8, 8), pl.ds((p % 2) * 128, 128)] = tile

    for q in range(2):
        @pl.when(me_p != q)
        def _():
            late_copy(0, q).wait_recv()
    for t, add in enumerate((add_0, add_1)):
        for q in range(2):
            add[:, pl.ds(q * 128, 128)] = late_r[q, :, pl.ds(t * 128, 128)]
    linear = arrived(pick2_out, picked2_r)
    for t in range(2):
        cols = slice(t * 128, (t + 1) * 128)
        top = linear[:, cols] + terms_s[pl.ds(me_p * own * 8 + t, own, stride=8), :]
        add_0[:, cols] += 0.5 * own_cour * top

    for copy in (ring_out + main_in + pick_out + inflows + outs + ring2_out + pick2_out):
        copy.wait_send()

    @pl.when(grp == 0)
    def _():
        for p in range(n_pair):
            @pl.when(me_p != p)
            def _():
                late_copy(p, me_p).wait_send()


def shards(n_pair, density, agg, share, target, frag, rate, cour, block_rows, upstream, face_map):
    own, height, width = density.shape
    piv = agg.shape[0]
    vmem = pl.BlockSpec(memory_space=pltpu.VMEM)
    hbm = pl.BlockSpec(memory_space=pltpu.HBM)
    dma = pltpu.SemaphoreType.DMA
    weight_rows = (BANDS + 2) * piv + 16
    main, add_0, add_1 = pl.pallas_call(
        functools.partial(step_kernel, n_pair, own, piv, height, width),
        out_shape=(
            pltpu.VMEM(density.shape, F32),
            pltpu.VMEM((own, width), F32),
            pltpu.VMEM((own, width), F32),
        ),
        in_specs=[hbm] * 10,
        out_specs=(vmem, vmem, vmem),
        scratch_shapes=[
            pltpu.VMEM((piv, piv), F32),
            pltpu.VMEM((piv, piv), F32),
            pltpu.VMEM((piv, piv), jnp.int32),
            pltpu.VMEM((piv, piv), F32),
            pltpu.VMEM((1, piv), F32),
            pltpu.VMEM((1, piv), F32),
            pltpu.SMEM(block_rows.shape, jnp.int32),
            pltpu.SMEM(upstream.shape, jnp.int32),
            pltpu.VMEM(face_map.shape, jnp.int32),
            pltpu.VMEM((2, own, height, 128), F32),
            pltpu.VMEM((n_pair, own * 8 + 48, 128), I16),
            pltpu.VMEM((n_pair, own * 8 + 48, 128), I16),
            pltpu.VMEM((piv * 8, 128), F32),
            pltpu.VMEM((piv, 1024), F32),
            pltpu.VMEM((piv, 1024), F32),
            pltpu.VMEM((piv * 8, 128), F32),
            pltpu.VMEM((n_pair, own * 8 + 32, 128), I16),
            pltpu.VMEM((n_pair, own * 8 + 32, 128), I16),
            pltpu.VMEM((weight_rows, piv), BF16),
            pltpu.VMEM((weight_rows, 256), F32),
            pltpu.VMEM((RING, own, width), F32),
            pltpu.VMEM((4, own, width), F32),
            pltpu.VMEM((4, own, width), F32),
            pltpu.VMEM((RING, own, width), F32),
            pltpu.VMEM((4, own, width), F32),
            pltpu.VMEM((4, own, width), F32),
            pltpu.VMEM((48, 128), F32),
            pltpu.VMEM((2, piv, 128), F32),
            pltpu.VMEM((own, width), F32),
            pltpu.VMEM((n_pair, own, width), F32),
            pltpu.VMEM((piv, width), F32),
            pltpu.VMEM((piv * 8, 128), F32),
            pltpu.VMEM((piv, 256), F32),
            pltpu.VMEM((n_pair, own, 256), F32),
            pltpu.VMEM((2, own, 256), F32),
            pltpu.VMEM((piv, 128), F32),
            pltpu.VMEM((piv + 16, 128), F32),
            dma((13,)),
            dma((n_pair,)), dma((n_pair,)),
            dma((n_pair,)), dma((n_pair,)),
            dma((n_pair,)), dma((2,)),
            dma((RING,)), dma((RING,)),
            dma((4,)), dma((4,)),
            dma((RING,)), dma((RING,)),
            dma((4,)), dma((4,)),
            dma((n_pair,)), dma((n_pair,)),
        ],
        compiler_params=pltpu.CompilerParams(
            collective_id=0, has_side_effects=True, vmem_limit_bytes=56 * 1024 * 1024),
    )(density, agg, share, target, frag, rate.reshape(1, piv), cour.reshape(1, piv), block_rows, upstream, face_map)
    row = lax.broadcasted_iota(jnp.int32, main.shape, 1)
    return main + jnp.where(row == 0, add_0[:, None, :], jnp.where(row == 1, add_1[:, None, :], 0.0))


def solution(mesh):
    in_specs = (P("pair", "blk", None), P(), P(), P(), P(), P(), P(), P(), P(), P("blk", None))
    out_specs = P("pair", "blk", None)
    return jax.shard_map(
        functools.partial(shards, mesh.shape["pair"]),
        mesh=mesh, in_specs=in_specs, out_specs=out_specs, check_vma=False)
```

```python
import functools

import jax
import jax.numpy as jnp
from jax import lax
from jax.experimental import pallas as pl
from jax.experimental.pallas import tpu as pltpu
from jax.sharding import PartitionSpec as P

MESH = pl.DeviceIdType.MESH
BANDS = 5
F32 = jnp.float32
BF16 = jnp.bfloat16
I16 = jnp.int16
RING, CORES = 4, 2
ORDER = (4, 3, 5, 2, 6, 1, 7)
MIDDLE = 1.025
STEP = 1.95 / 65534.0
LEAST = 32768.0 / 65536.0


def permuted(face, one_hot):
    total = None
    for _ in range(3):
        part = face.astype(BF16)
        face = face - part.astype(F32)
        moved = jnp.dot(part, one_hot, preferred_element_type=F32)
        total = moved if total is None else total + moved
    return total


def rounded16(x):
    return jnp.round(x).astype(jnp.int32).astype(I16)


def step_kernel(
    n_pair, own, piv, height, width,
    density, agg_h, share_h, target_h, frag_h, rate_h, cour_h, rows_h, up_h, map_h,
    main, add_0, add_1,
    agg, share, target, frag, rate, cour, rows_sm, up_sm, face_map, dens_v, enc, got, v0, sec, res, out_f, out_s, out_r, wb, y_s,
    ring, picked, picked_r, stage,
    halo_f, halo_c, inflow_s, inflow_r, face, terms_s, late_s, late_p, late_r, edge, wide_s,
    local_sem, main_send, main_recv, inflow_send, inflow_recv, late_send, late_recv,
    ring_send, ring_recv, pick_send, pick_recv,
    out_send, out_recv,
):
    me_b, me_p = lax.axis_index("blk"), lax.axis_index("pair")
    grp, half = me_p // 2, me_p % 2
    z_hi, y, core = me_b // (RING * CORES), (me_b // CORES) % RING, me_b % CORES
    pairs = [(me_p + d) % n_pair for d in range(n_pair)]

    def block_at(dz, dy, dc):
        return ((z_hi + dz) % 2) * (RING * CORES) + ((y + dy) % RING) * CORES + (core + dc) % CORES

    ring_mates = [block_at(0, d, 0) for d in range(RING)]
    pick_mates = [block_at(q // 2, 0, q % 2) for q in range(4)]

    barrier = pltpu.get_barrier_semaphore()
    for p in pairs[1:]:
        pl.semaphore_signal(barrier, inc=1, device_id=(me_b, p), device_id_type=MESH)
    for b in ring_mates[1:] + pick_mates[1:]:
        pl.semaphore_signal(barrier, inc=1, device_id=(b, me_p), device_id_type=MESH)

    loads = [pltpu.make_async_copy(density.at[:, :, pl.ds(t * 128, 128)], dens_v.at[t], local_sem.at[t])
             for t in range(2)]
    for load in loads:
        load.start()
    scalars = [pltpu.make_async_copy(rows_h, rows_sm, local_sem.at[11]),
               pltpu.make_async_copy(up_h, up_sm, local_sem.at[12])]
    map_load = pltpu.make_async_copy(map_h, face_map, local_sem.at[8])
    for load in scalars + [map_load]:
        load.start()
    tables = [pltpu.make_async_copy(src, dst, local_sem.at[2 + n]) for n, (src, dst) in enumerate(
        ((agg_h, agg), (share_h, share), (target_h, target), (frag_h, frag),
         (rate_h, rate), (cour_h, cour)))]
    for load in tables:
        load.start()

    def to_pair(d, src, dst, send, recv):
        return pltpu.make_async_remote_copy(
            src_ref=src, dst_ref=dst, send_sem=send.at[d], recv_sem=recv.at[d],
            device_id=(me_b, pairs[d]), device_id_type=MESH)

    def to_block(b, d, src, dst, send, recv):
        return pltpu.make_async_remote_copy(
            src_ref=src, dst_ref=dst, send_sem=send.at[d], recv_sem=recv.at[d],
            device_id=(b, me_p), device_id_type=MESH)

    def ring_slot(b):
        return (b // CORES) % RING

    halo_f[...] = jnp.zeros(halo_f.shape, F32)
    stage[...] = jnp.zeros(stage.shape, F32)
    for load in scalars:
        load.wait()
    live_rows = rows_sm[me_b]
    map_load.wait()
    stage[pl.ds(44, 1), :] = face_map[...].astype(F32)
    for load in loads:
        load.wait()
    dens_rows = dens_v.reshape(2 * own * height, 128)
    for n in range(2):
        for t in range(2):
            here = jnp.maximum(live_rows - 1 - n, 0) + t * own * height
            stage[pl.ds(24 * n, own), pl.ds(t * 128, 128)] = (
                dens_rows[pl.ds(here, own, stride=height), :] - MIDDLE) * (1.0 / STEP)
    ring[y] = rounded16(stage[...])
    pl.semaphore_wait(barrier, len(pairs) + len(ring_mates) + len(pick_mates) - 3)
    ring_out = [to_block(ring_mates[d], d, ring.at[y], ring.at[y], ring_send, ring_recv) for d in range(1, RING)]
    for copy in ring_out:
        copy.start()

    main_in = []
    for d in ORDER + (0,):
        p = pairs[d]
        tile = dens_v[p % 2, :, pl.ds(pl.multiple_of((p // 2) * 8, 8), 8), :].reshape(own * 8, 128)
        for n in range(2):
            under = jnp.maximum((p // 2) * 8 - 1 - n, 0) + (p % 2) * own * height
            halo_f[pl.ds(n * own, own), :] = dens_rows[pl.ds(under, own, stride=height), :]
        goal = enc.at[d] if d else got.at[me_p]
        goal[pl.ds(0, own * 8), :] = rounded16((tile - MIDDLE) * (1.0 / STEP))
        goal[pl.ds(own * 8, 48), :] = rounded16((halo_f[...] - MIDDLE) * (1.0 / STEP))
        if d:
            main_in.append(to_pair(d, enc.at[d], got.at[me_p], main_send, main_recv))
            main_in[-1].start()

    for load in tables:
        load.wait()
    row_id = lax.broadcasted_iota(jnp.int32, (piv, piv), 0)
    col_id = lax.broadcasted_iota(jnp.int32, (piv, piv), 1)
    kern = agg[...]
    part = share[...]
    low = (0.5 * kern * part).astype(BF16).astype(F32)
    high = (0.5 * kern * (1.0 - part)).astype(BF16).astype(F32)
    offset = (target[...] - jnp.maximum(row_id, col_id)).astype(F32)
    triangles = ((low, high, offset, col_id <= row_id), (low.T, high.T, offset.T, col_id < row_id))
    for d in range(BANDS):
        pair = [jnp.where(keep, jnp.where(off == d, lo, jnp.where(off == d - 1, hi, 0.0)), 0.0)
                for lo, hi, off, keep in triangles]
        wb[pl.ds(d * piv, piv), :] = (pair[0] + pair[1]).astype(BF16)
    pair = [jnp.where(keep & (off == -1), lo, 0.0)[piv - 8:] for lo, hi, off, keep in triangles]
    last = pltpu.roll(pair[0] + pair[1], 7, 0)
    rate_row = rate[...]
    cour_row = cour[...]
    base = BANDS * piv
    wb[pl.ds(base, piv), :] = kern.astype(BF16)
    wb[pl.ds(base + 2 * piv, 16), :] = jnp.concatenate([last, jnp.zeros_like(last)], axis=0).astype(BF16)
    smaller = (row_id < col_id).astype(F32)
    wb[pl.ds(base + piv, piv), :] = (frag[...] * rate_row * smaller).astype(BF16)
    diag = row_id == col_id
    rate_col = jnp.sum(jnp.where(diag, rate_row, 0.0), axis=1, keepdims=True)
    cour_col = jnp.sum(jnp.where(diag, cour_row, 0.0), axis=1, keepdims=True)
    own_diag = (lax.broadcasted_iota(jnp.int32, (own, piv), 0) + me_p * own
                == lax.broadcasted_iota(jnp.int32, (own, piv), 1))
    own_cour = jnp.sum(jnp.where(own_diag, cour_row, 0.0), axis=1, keepdims=True)
    own_rate = jnp.sum(jnp.where(own_diag, rate_row, 0.0), axis=1, keepdims=True)
    one_hot = (lax.broadcasted_iota(jnp.int32, (width, width), 0) == face_map[...]).astype(F32).astype(BF16)

    for copy in ring_out:
        copy.wait_recv()
    for q in range(4):
        feeder = up_sm[pick_mates[q]]
        goal = picked.at[q] if q else picked_r.at[0]
        goal[pl.ds(0, 48), :] = ring[ring_slot(feeder)]
        goal[pl.ds(48, 32), :] = ring[ring_slot(up_sm[feeder]), pl.ds(0, 32), :]
    pick_out = [to_block(pick_mates[q], q, picked.at[q], picked_r.at[q], pick_send, pick_recv) for q in range(1, 4)]
    for copy in pick_out:
        copy.start()

    def mixed(v):
        y_s[:, :v.shape[1]] = jnp.dot(wb[...], v.astype(BF16), preferred_element_type=F32)
        vb = v.astype(BF16).astype(F32)
        cols = slice(0, v.shape[1])
        y_s[pl.ds(base + 2 * piv - 8, 8), cols] += y_s[pl.ds(base + 2 * piv, 8), cols] * vb[piv - 1:]
        births = None
        for d in reversed(range(BANDS)):
            here = vb * y_s[pl.ds(d * piv, piv), cols]
            births = here if births is None else here + pltpu.roll(births, 1, 0)
        return births - v * y_s[pl.ds(base, piv), cols] + y_s[pl.ds(base + piv, piv), cols]

    def change(v, prev):
        return v + (mixed(v) - rate_col * v - cour_col * (v - prev))

    def start_row(s):
        return v0[pl.ds(s, piv, stride=8), :]

    def pick_slot(b):
        return ((b // (RING * CORES) + z_hi) % 2) * 2 + (b + core) % CORES

    def first_inflow():
        for copy in pick_out:
            copy.wait_recv()
        feeder = up_sm[me_b]
        stage[...] = picked_r[pick_slot(feeder), pl.ds(0, 48), :].astype(jnp.int32).astype(F32)
        inflow = permuted(stage[pl.ds(0, 24), :], one_hot)[:own] * STEP + MIDDLE
        inflow_s[...] = inflow
        inflows = [to_pair(d, inflow_s, inflow_r.at[me_p], inflow_send, inflow_recv) for d in ORDER]
        for copy in inflows:
            copy.start()
        inflow_r[me_p] = inflow

        feeder_hot = (lax.broadcasted_iota(jnp.int32, (width, width), 0).astype(F32) == stage[pl.ds(44, 1), :])
        fed = picked_r[pick_slot(up_sm[feeder]), pl.ds(48, 32), :].astype(jnp.int32).astype(F32)
        fed = permuted(fed, feeder_hot.astype(F32).astype(BF16))
        prev = jnp.where(rows_sm[feeder] == 1, fed[:24], stage[pl.ds(24, 24), :])
        prev = permuted(prev, one_hot)[:own] * STEP + MIDDLE
        return inflows, inflow - own_cour * (inflow - prev) - own_rate * inflow

    for copy in main_in:
        copy.wait_recv()
    for p in range(n_pair):
        v0[pl.ds(p * own * 8, own * 8), :] = (
            got[p, pl.ds(0, own * 8), :].astype(jnp.int32).astype(F32) * STEP + MIDDLE)
        halo_f[...] = got[p, pl.ds(own * 8, 48), :].astype(jnp.int32).astype(F32) * STEP + MIDDLE
        for n in range(2):
            halo_c[n, pl.ds(p * own, own), :] = jnp.where(grp > 0, halo_f[pl.ds(n * own, own), :], 0.0)

    for it in reversed(range(4)):
        s = 2 * it
        before = halo_c[0] if it == 0 else start_row(s - 1)
        first, second = start_row(s), start_row(s + 1)
        now = change(jnp.concatenate([first, second], axis=1), jnp.concatenate([before, first], axis=1))
        for t in range(2):
            row = grp * 8 + s + t
            piece = jnp.where(row < live_rows, now[:, t * 128:(t + 1) * 128], 0.0)
            sec[:, pl.ds((s + t) * 128, 128)] = piece
    edge[...] = change(halo_c[0], halo_c[1])

    def final_rows(it, before):
        v = sec[:, pl.ds(it * 256, 256)]
        now = change(v, jnp.concatenate([before, v[:, :128]], axis=1))
        return [0.5 * start_row(2 * it + t) + 0.5 * now[:, t * 128:(t + 1) * 128] for t in range(2)]

    biggest = None
    for it in reversed(range(4)):
        if it == 0:
            before = edge[...]
        else:
            before = sec[:, pl.ds((2 * it - 1) * 128, 128)]
        for t, piece in enumerate(final_rows(it, before)):
            row = grp * 8 + 2 * it + t
            piece = jnp.where((row < live_rows) & (row >= 2), piece, 0.0)
            res[:, pl.ds((2 * it + t) * 128, 128)] = piece
            size = jnp.abs(piece)
            biggest = size if biggest is None else jnp.maximum(biggest, size)

    biggest = jnp.max(biggest, axis=1, keepdims=True)
    finer = jnp.where(biggest > 0.0, 32767.0 / biggest, 0.0)
    for s in range(8):
        out_f[pl.ds(s, piv, stride=8), :] = res[:, pl.ds(s * 128, 128)] * finer
    lane = lax.broadcasted_iota(jnp.int32, (piv, 128), 1)
    wide_s[pl.ds(piv, 16), :] = jnp.zeros((16, 128), F32)
    first = jnp.floor(biggest * LEAST)
    rest = (biggest * LEAST - first) * 32768.0
    second = jnp.floor(rest)
    third = jnp.floor((rest - second) * 32768.0)
    wide_s[pl.ds(0, piv), :] = jnp.where(lane == 0, first, jnp.where(lane == 1, second, jnp.where(lane == 2, third, 0.0)))
    for p in range(n_pair):
        out_s[p, pl.ds(0, own * 8), :] = rounded16(out_f[pl.ds(p * own * 8, own * 8), :])
        out_s[p, pl.ds(own * 8, 32), :] = rounded16(wide_s[pl.ds(p * own, 32), :])
    outs = [to_pair(d, out_s.at[pairs[d]], out_r.at[me_p], out_send, out_recv) for d in ORDER]
    for copy in outs:
        copy.start()
    out_own = pltpu.make_async_copy(out_s.at[me_p], out_r.at[me_p], local_sem.at[9])
    out_own.start()

    inflows, linear = first_inflow()

    for copy in inflows:
        copy.wait_recv()
    for p in range(n_pair):
        face[pl.ds(p * own, own), :] = inflow_r[p]

    def late_copy(p, source):
        return pltpu.make_async_remote_copy(
            src_ref=late_p.at[p], dst_ref=late_r.at[source], send_sem=late_send.at[p],
            recv_sem=late_recv.at[source], device_id=(me_b, p), device_id_type=MESH)

    @pl.when(grp == 0)
    def _():
        sec[:, :128] += cour_col * jnp.where(half == 0, face[:, :128], face[:, 128:])
        for t, piece in enumerate(final_rows(0, jnp.zeros((piv, 128), F32))):
            late_s[:, pl.ds(t * 128, 128)] = jnp.where(t < live_rows, piece, 0.0)
        for p in range(n_pair):
            late_p[p] = late_s[pl.ds(p * own, own), :]
        for p in range(n_pair):
            @pl.when(me_p != p)
            def _():
                late_copy(p, me_p).start()

            @pl.when(me_p == p)
            def _():
                late_r[min(p, 1)] = late_p[p]

    terms = mixed(face[...])
    for t in range(2):
        terms_s[pl.ds(t, piv, stride=8), :] = terms[:, t * 128:(t + 1) * 128]

    digit = lax.broadcasted_iota(jnp.int32, (own, 128), 1)
    digit_size = jnp.where(
        digit == 0, 1.0, jnp.where(digit == 1, 1.0 / 32768.0, jnp.where(digit == 2, 1.0 / 32768.0 ** 2, 0.0))
    ) * (1.0 / (LEAST * 32767.0))
    out_own.wait()
    for copy in outs:
        copy.wait_recv()
    for p in range(n_pair):
        digits = out_r[p, pl.ds(own * 8, 32), :].astype(jnp.int32).astype(F32)[:own]
        scale = jnp.sum(digits * digit_size, axis=1, keepdims=True)
        tile = out_r[p, pl.ds(0, own * 8), :].astype(jnp.int32).astype(F32).reshape(own, 8, 128) * scale[:, :, None]
        main[:, pl.ds((p // 2) * 8, 8), pl.ds((p % 2) * 128, 128)] = tile

    for q in range(2):
        @pl.when(me_p != q)
        def _():
            late_copy(0, q).wait_recv()
    for t, add in enumerate((add_0, add_1)):
        for q in range(2):
            add[:, pl.ds(q * 128, 128)] = late_r[q, :, pl.ds(t * 128, 128)]
    for t in range(2):
        cols = slice(t * 128, (t + 1) * 128)
        top = linear[:, cols] + terms_s[pl.ds(me_p * own * 8 + t, own, stride=8), :]
        add_0[:, cols] += 0.5 * own_cour * top

    for copy in (ring_out + main_in + pick_out + inflows + outs):
        copy.wait_send()

    @pl.when(grp == 0)
    def _():
        for p in range(n_pair):
            @pl.when(me_p != p)
            def _():
                late_copy(p, me_p).wait_send()


def shards(n_pair, density, agg, share, target, frag, rate, cour, block_rows, upstream, face_map):
    own, height, width = density.shape
    piv = agg.shape[0]
    vmem = pl.BlockSpec(memory_space=pltpu.VMEM)
    hbm = pl.BlockSpec(memory_space=pltpu.HBM)
    dma = pltpu.SemaphoreType.DMA
    weight_rows = (BANDS + 2) * piv + 16
    main, add_0, add_1 = pl.pallas_call(
        functools.partial(step_kernel, n_pair, own, piv, height, width),
        out_shape=(
            pltpu.VMEM(density.shape, F32),
            pltpu.VMEM((own, width), F32),
            pltpu.VMEM((own, width), F32),
        ),
        in_specs=[hbm] * 10,
        out_specs=(vmem, vmem, vmem),
        scratch_shapes=[
            pltpu.VMEM((piv, piv), F32),
            pltpu.VMEM((piv, piv), F32),
            pltpu.VMEM((piv, piv), jnp.int32),
            pltpu.VMEM((piv, piv), F32),
            pltpu.VMEM((1, piv), F32),
            pltpu.VMEM((1, piv), F32),
            pltpu.SMEM(block_rows.shape, jnp.int32),
            pltpu.SMEM(upstream.shape, jnp.int32),
            pltpu.VMEM(face_map.shape, jnp.int32),
            pltpu.VMEM((2, own, height, 128), F32),
            pltpu.VMEM((n_pair, own * 8 + 48, 128), I16),
            pltpu.VMEM((n_pair, own * 8 + 48, 128), I16),
            pltpu.VMEM((piv * 8, 128), F32),
            pltpu.VMEM((piv, 1024), F32),
            pltpu.VMEM((piv, 1024), F32),
            pltpu.VMEM((piv * 8, 128), F32),
            pltpu.VMEM((n_pair, own * 8 + 32, 128), I16),
            pltpu.VMEM((n_pair, own * 8 + 32, 128), I16),
            pltpu.VMEM((weight_rows, piv), BF16),
            pltpu.VMEM((weight_rows, 256), F32),
            pltpu.VMEM((RING, 48, width), I16),
            pltpu.VMEM((4, 80, width), I16),
            pltpu.VMEM((4, 80, width), I16),
            pltpu.VMEM((48, width), F32),
            pltpu.VMEM((48, 128), F32),
            pltpu.VMEM((2, piv, 128), F32),
            pltpu.VMEM((own, width), F32),
            pltpu.VMEM((n_pair, own, width), F32),
            pltpu.VMEM((piv, width), F32),
            pltpu.VMEM((piv * 8, 128), F32),
            pltpu.VMEM((piv, 256), F32),
            pltpu.VMEM((n_pair, own, 256), F32),
            pltpu.VMEM((2, own, 256), F32),
            pltpu.VMEM((piv, 128), F32),
            pltpu.VMEM((piv + 16, 128), F32),
            dma((13,)),
            dma((n_pair,)), dma((n_pair,)),
            dma((n_pair,)), dma((n_pair,)),
            dma((n_pair,)), dma((2,)),
            dma((RING,)), dma((RING,)),
            dma((4,)), dma((4,)),
            dma((n_pair,)), dma((n_pair,)),
        ],
        compiler_params=pltpu.CompilerParams(
            collective_id=0, has_side_effects=True, vmem_limit_bytes=56 * 1024 * 1024),
    )(density, agg, share, target, frag, rate.reshape(1, piv), cour.reshape(1, piv), block_rows, upstream, face_map)
    row = lax.broadcasted_iota(jnp.int32, main.shape, 1)
    return main + jnp.where(row == 0, add_0[:, None, :], jnp.where(row == 1, add_1[:, None, :], 0.0))


def solution(mesh):
    in_specs = (P("pair", "blk", None), P(), P(), P(), P(), P(), P(), P(), P(), P("blk", None))
    out_specs = P("pair", "blk", None)
    return jax.shard_map(
        functools.partial(shards, mesh.shape["pair"]),
        mesh=mesh, in_specs=in_specs, out_specs=out_specs, check_vma=False)
```

```python
import functools

import jax
import jax.numpy as jnp
from jax import lax
from jax.experimental import pallas as pl
from jax.experimental.pallas import tpu as pltpu
from jax.sharding import PartitionSpec as P

MESH = pl.DeviceIdType.MESH
BANDS = 5
F32 = jnp.float32
BF16 = jnp.bfloat16
I16 = jnp.int16
RING, CORES = 4, 2
ORDER = (4, 3, 5, 2, 6, 1, 7)
MIDDLE = 1.025
STEP = 1.95 / 65534.0
LEAST = 32768.0 / 65536.0


def permuted(face, one_hot):
    total = None
    for _ in range(3):
        part = face.astype(BF16)
        face = face - part.astype(F32)
        moved = jnp.dot(part, one_hot, preferred_element_type=F32)
        total = moved if total is None else total + moved
    return total


def rounded16(x):
    return jnp.round(x).astype(jnp.int32).astype(I16)


def step_kernel(
    n_pair, own, piv, height, width,
    density, agg_h, share_h, target_h, frag_h, rate_h, cour_h, rows_h, up_h, map_h,
    main, add_0, add_1,
    agg, share, target, frag, rate, cour, rows_sm, up_sm, face_map, dens_v, enc, got, v0, sec, res, out_f, out_s, out_r, wb, y_s,
    ring, picked, picked_r, stage,
    halo_f, row_f, row_c, halo_c, inflow_s, inflow_r, face, row_s, edge, wide_s,
    local_sem, main_send, main_recv, inflow_send, inflow_recv,
    ring_send, ring_recv, pick_send, pick_recv,
    out_send, out_recv,
):
    me_b, me_p = lax.axis_index("blk"), lax.axis_index("pair")
    grp = me_p // 2
    z_hi, y, core = me_b // (RING * CORES), (me_b // CORES) % RING, me_b % CORES
    pairs = [(me_p + d) % n_pair for d in range(n_pair)]

    def block_at(dz, dy, dc):
        return ((z_hi + dz) % 2) * (RING * CORES) + ((y + dy) % RING) * CORES + (core + dc) % CORES

    ring_mates = [block_at(0, d, 0) for d in range(RING)]
    pick_mates = [block_at(q // 2, 0, q % 2) for q in range(4)]

    barrier = pltpu.get_barrier_semaphore()
    for p in pairs[1:]:
        pl.semaphore_signal(barrier, inc=1, device_id=(me_b, p), device_id_type=MESH)
    for b in ring_mates[1:] + pick_mates[1:]:
        pl.semaphore_signal(barrier, inc=1, device_id=(b, me_p), device_id_type=MESH)

    loads = [pltpu.make_async_copy(density.at[:, :, pl.ds(t * 128, 128)], dens_v.at[t], local_sem.at[t])
             for t in range(2)]
    for load in loads:
        load.start()
    scalars = [pltpu.make_async_copy(rows_h, rows_sm, local_sem.at[11]),
               pltpu.make_async_copy(up_h, up_sm, local_sem.at[12])]
    map_load = pltpu.make_async_copy(map_h, face_map, local_sem.at[8])
    for load in scalars + [map_load]:
        load.start()
    tables = [pltpu.make_async_copy(src, dst, local_sem.at[2 + n]) for n, (src, dst) in enumerate(
        ((agg_h, agg), (share_h, share), (target_h, target), (frag_h, frag),
         (rate_h, rate), (cour_h, cour)))]
    for load in tables:
        load.start()

    def to_pair(d, src, dst, send, recv):
        return pltpu.make_async_remote_copy(
            src_ref=src, dst_ref=dst, send_sem=send.at[d], recv_sem=recv.at[d],
            device_id=(me_b, pairs[d]), device_id_type=MESH)

    def to_block(b, d, src, dst, send, recv):
        return pltpu.make_async_remote_copy(
            src_ref=src, dst_ref=dst, send_sem=send.at[d], recv_sem=recv.at[d],
            device_id=(b, me_p), device_id_type=MESH)

    def ring_slot(b):
        return (b // CORES) % RING

    halo_f[...] = jnp.zeros(halo_f.shape, F32)
    row_f[...] = jnp.zeros(row_f.shape, F32)
    stage[...] = jnp.zeros(stage.shape, F32)
    for load in scalars:
        load.wait()
    live_rows = rows_sm[me_b]
    map_load.wait()
    stage[pl.ds(44, 1), :] = face_map[...].astype(F32)
    for load in loads:
        load.wait()
    dens_rows = dens_v.reshape(2 * own * height, 128)
    for n in range(2):
        for t in range(2):
            here = jnp.maximum(live_rows - 1 - n, 0) + t * own * height
            stage[pl.ds(24 * n, own), pl.ds(t * 128, 128)] = (
                dens_rows[pl.ds(here, own, stride=height), :] - MIDDLE) * (1.0 / STEP)
    ring[y] = rounded16(stage[...])
    pl.semaphore_wait(barrier, len(pairs) + len(ring_mates) + len(pick_mates) - 3)
    ring_out = [to_block(ring_mates[d], d, ring.at[y], ring.at[y], ring_send, ring_recv) for d in range(1, RING)]
    for copy in ring_out:
        copy.start()

    for t in range(2):
        row_f[pl.ds(t * own, own), :] = dens_rows[pl.ds(t * own * height, own, stride=height), :]
    row_16 = rounded16((row_f[...] - MIDDLE) * (1.0 / STEP))
    main_in = []
    for d in ORDER + (0,):
        p = pairs[d]
        tile = dens_v[p % 2, :, pl.ds(pl.multiple_of((p // 2) * 8, 8), 8), :].reshape(own * 8, 128)
        for n in range(2):
            under = jnp.maximum((p // 2) * 8 - 1 - n, 0) + (p % 2) * own * height
            halo_f[pl.ds(n * own, own), :] = dens_rows[pl.ds(under, own, stride=height), :]
        goal = enc.at[d] if d else got.at[me_p]
        goal[pl.ds(0, own * 8), :] = rounded16((tile - MIDDLE) * (1.0 / STEP))
        goal[pl.ds(own * 8, 48), :] = rounded16((halo_f[...] - MIDDLE) * (1.0 / STEP))
        goal[pl.ds(own * 8 + 48, 48), :] = row_16
        if d:
            main_in.append(to_pair(d, enc.at[d], got.at[me_p], main_send, main_recv))
            main_in[-1].start()

    for copy in ring_out:
        copy.wait_recv()
    for q in range(4):
        feeder = up_sm[pick_mates[q]]
        goal = picked.at[q] if q else picked_r.at[0]
        goal[pl.ds(0, 48), :] = ring[ring_slot(feeder)]
        goal[pl.ds(48, 32), :] = ring[ring_slot(up_sm[feeder]), pl.ds(0, 32), :]
    pick_out = [to_block(pick_mates[q], q, picked.at[q], picked_r.at[q], pick_send, pick_recv) for q in range(1, 4)]
    for copy in pick_out:
        copy.start()

    for load in tables:
        load.wait()
    row_id = lax.broadcasted_iota(jnp.int32, (piv, piv), 0)
    col_id = lax.broadcasted_iota(jnp.int32, (piv, piv), 1)
    kern = agg[...]
    part = share[...]
    low = (0.5 * kern * part).astype(BF16).astype(F32)
    high = (0.5 * kern * (1.0 - part)).astype(BF16).astype(F32)
    offset = (target[...] - jnp.maximum(row_id, col_id)).astype(F32)
    triangles = ((low, high, offset, col_id <= row_id), (low.T, high.T, offset.T, col_id < row_id))
    for d in range(BANDS):
        pair = [jnp.where(keep, jnp.where(off == d, lo, jnp.where(off == d - 1, hi, 0.0)), 0.0)
                for lo, hi, off, keep in triangles]
        wb[pl.ds(d * piv, piv), :] = (pair[0] + pair[1]).astype(BF16)
    pair = [jnp.where(keep & (off == -1), lo, 0.0)[piv - 8:] for lo, hi, off, keep in triangles]
    last = pltpu.roll(pair[0] + pair[1], 7, 0)
    rate_row = rate[...]
    cour_row = cour[...]
    base = BANDS * piv
    wb[pl.ds(base, piv), :] = kern.astype(BF16)
    wb[pl.ds(base + 2 * piv, 16), :] = jnp.concatenate([last, jnp.zeros_like(last)], axis=0).astype(BF16)
    smaller = (row_id < col_id).astype(F32)
    wb[pl.ds(base + piv, piv), :] = (frag[...] * rate_row * smaller).astype(BF16)
    diag = row_id == col_id
    rate_col = jnp.sum(jnp.where(diag, rate_row, 0.0), axis=1, keepdims=True)
    cour_col = jnp.sum(jnp.where(diag, cour_row, 0.0), axis=1, keepdims=True)
    own_diag = (lax.broadcasted_iota(jnp.int32, (own, piv), 0) + me_p * own
                == lax.broadcasted_iota(jnp.int32, (own, piv), 1))
    own_cour = jnp.sum(jnp.where(own_diag, cour_row, 0.0), axis=1, keepdims=True)
    own_rate = jnp.sum(jnp.where(own_diag, rate_row, 0.0), axis=1, keepdims=True)
    one_hot = (lax.broadcasted_iota(jnp.int32, (width, width), 0) == face_map[...]).astype(F32).astype(BF16)

    def mixed(v):
        y_s[:, :v.shape[1]] = jnp.dot(wb[...], v.astype(BF16), preferred_element_type=F32)
        vb = v.astype(BF16).astype(F32)
        cols = slice(0, v.shape[1])
        y_s[pl.ds(base + 2 * piv - 8, 8), cols] += y_s[pl.ds(base + 2 * piv, 8), cols] * vb[piv - 1:]
        births = None
        for d in reversed(range(BANDS)):
            here = vb * y_s[pl.ds(d * piv, piv), cols]
            births = here if births is None else here + pltpu.roll(births, 1, 0)
        return births - v * y_s[pl.ds(base, piv), cols] + y_s[pl.ds(base + piv, piv), cols]

    def change(v, prev):
        return v + (mixed(v) - rate_col * v - cour_col * (v - prev))

    def start_row(s):
        return v0[pl.ds(s, piv, stride=8), :]

    def pick_slot(b):
        return ((b // (RING * CORES) + z_hi) % 2) * 2 + (b + core) % CORES

    def first_inflow():
        for copy in pick_out:
            copy.wait_recv()
        feeder = up_sm[me_b]
        stage[...] = picked_r[pick_slot(feeder), pl.ds(0, 48), :].astype(jnp.int32).astype(F32)
        inflow = permuted(stage[pl.ds(0, 24), :], one_hot)[:own] * STEP + MIDDLE
        inflow_s[...] = inflow
        inflows = [to_pair(d, inflow_s, inflow_r.at[me_p], inflow_send, inflow_recv) for d in ORDER]
        for copy in inflows:
            copy.start()
        inflow_r[me_p] = inflow

        feeder_hot = (lax.broadcasted_iota(jnp.int32, (width, width), 0).astype(F32) == stage[pl.ds(44, 1), :])
        fed = picked_r[pick_slot(up_sm[feeder]), pl.ds(48, 32), :].astype(jnp.int32).astype(F32)
        fed = permuted(fed, feeder_hot.astype(F32).astype(BF16))
        prev = jnp.where(rows_sm[feeder] == 1, fed[:24], stage[pl.ds(24, 24), :])
        prev = permuted(prev, one_hot)[:own] * STEP + MIDDLE
        return inflows, inflow - own_cour * (inflow - prev) - own_rate * inflow

    for copy in main_in:
        copy.wait_recv()
    for p in range(n_pair):
        v0[pl.ds(p * own * 8, own * 8), :] = (
            got[p, pl.ds(0, own * 8), :].astype(jnp.int32).astype(F32) * STEP + MIDDLE)
        halo_f[...] = got[p, pl.ds(own * 8, 48), :].astype(jnp.int32).astype(F32) * STEP + MIDDLE
        row_f[...] = got[p, pl.ds(own * 8 + 48, 48), :].astype(jnp.int32).astype(F32) * STEP + MIDDLE
        for t in range(2):
            row_c[pl.ds(p * own, own), pl.ds(t * 128, 128)] = row_f[pl.ds(t * own, own), :]
        for n in range(2):
            halo_c[n, pl.ds(p * own, own), :] = jnp.where(grp > 0, halo_f[pl.ds(n * own, own), :], 0.0)

    for it in reversed(range(4)):
        s = 2 * it
        before = halo_c[0] if it == 0 else start_row(s - 1)
        first, second = start_row(s), start_row(s + 1)
        now = change(jnp.concatenate([first, second], axis=1), jnp.concatenate([before, first], axis=1))
        for t in range(2):
            row = grp * 8 + s + t
            piece = jnp.where(row < live_rows, now[:, t * 128:(t + 1) * 128], 0.0)
            sec[:, pl.ds((s + t) * 128, 128)] = piece
    edge[...] = change(halo_c[0], halo_c[1])

    def final_rows(it, before):
        v = sec[:, pl.ds(it * 256, 256)]
        now = change(v, jnp.concatenate([before, v[:, :128]], axis=1))
        return [0.5 * start_row(2 * it + t) + 0.5 * now[:, t * 128:(t + 1) * 128] for t in range(2)]

    biggest = None
    for it in reversed(range(4)):
        if it == 0:
            before = edge[...]
        else:
            before = sec[:, pl.ds((2 * it - 1) * 128, 128)]
        for t, piece in enumerate(final_rows(it, before)):
            row = grp * 8 + 2 * it + t
            piece = jnp.where((row < live_rows) & (row >= 1), piece, 0.0)
            res[:, pl.ds((2 * it + t) * 128, 128)] = piece
            size = jnp.abs(piece)
            biggest = size if biggest is None else jnp.maximum(biggest, size)

    inflows, linear = first_inflow()
    biggest = jnp.max(biggest, axis=1, keepdims=True)
    finer = jnp.where(biggest > 0.0, 32767.0 / biggest, 0.0)
    for s in range(8):
        out_f[pl.ds(s, piv, stride=8), :] = res[:, pl.ds(s * 128, 128)] * finer
    lane = lax.broadcasted_iota(jnp.int32, (piv, 128), 1)
    wide_s[pl.ds(piv, 16), :] = jnp.zeros((16, 128), F32)
    first = jnp.floor(biggest * LEAST)
    rest = (biggest * LEAST - first) * 32768.0
    second = jnp.floor(rest)
    third = jnp.floor((rest - second) * 32768.0)
    wide_s[pl.ds(0, piv), :] = jnp.where(lane == 0, first, jnp.where(lane == 1, second, jnp.where(lane == 2, third, 0.0)))
    for p in range(n_pair):
        out_s[p, pl.ds(0, own * 8), :] = rounded16(out_f[pl.ds(p * own * 8, own * 8), :])
        out_s[p, pl.ds(own * 8, 32), :] = rounded16(wide_s[pl.ds(p * own, 32), :])
    outs = [to_pair(d, out_s.at[pairs[d]], out_r.at[me_p], out_send, out_recv) for d in ORDER]
    for copy in outs:
        copy.start()
    out_own = pltpu.make_async_copy(out_s.at[me_p], out_r.at[me_p], local_sem.at[9])
    out_own.start()


    for copy in inflows:
        copy.wait_recv()
    for p in range(n_pair):
        face[pl.ds(p * own, own), :] = inflow_r[p]

    inflow_all = face[...]
    start = row_c[...]
    moved = change(start, inflow_all)
    row_0 = 0.5 * start + 0.5 * (moved + (mixed(moved) - rate_col * moved - cour_col * moved))
    row_0 = row_0 + 0.5 * cour_col * mixed(inflow_all)
    for t in range(2):
        row_s[pl.ds(t, piv, stride=8), :] = row_0[:, t * 128:(t + 1) * 128]
    for t in range(2):
        cols = slice(t * 128, (t + 1) * 128)
        mine = row_s[pl.ds(me_p * own * 8 + t, own, stride=8), :]
        add_0[:, cols] = mine + 0.5 * own_cour * linear[:, cols]
        add_1[:, cols] = jnp.where(live_rows > 1, 0.5 * own_cour * own_cour * inflow_s[:, cols], 0.0)

    digit = lax.broadcasted_iota(jnp.int32, (own, 128), 1)
    digit_size = jnp.where(
        digit == 0, 1.0, jnp.where(digit == 1, 1.0 / 32768.0, jnp.where(digit == 2, 1.0 / 32768.0 ** 2, 0.0))
    ) * (1.0 / (LEAST * 32767.0))
    out_own.wait()
    for copy in outs:
        copy.wait_recv()
    for p in range(n_pair):
        digits = out_r[p, pl.ds(own * 8, 32), :].astype(jnp.int32).astype(F32)[:own]
        scale = jnp.sum(digits * digit_size, axis=1, keepdims=True)
        tile = out_r[p, pl.ds(0, own * 8), :].astype(jnp.int32).astype(F32).reshape(own, 8, 128) * scale[:, :, None]
        main[:, pl.ds((p // 2) * 8, 8), pl.ds((p % 2) * 128, 128)] = tile

    for copy in (ring_out + main_in + pick_out + inflows + outs):
        copy.wait_send()


def shards(n_pair, density, agg, share, target, frag, rate, cour, block_rows, upstream, face_map):
    own, height, width = density.shape
    piv = agg.shape[0]
    vmem = pl.BlockSpec(memory_space=pltpu.VMEM)
    hbm = pl.BlockSpec(memory_space=pltpu.HBM)
    dma = pltpu.SemaphoreType.DMA
    weight_rows = (BANDS + 2) * piv + 16
    main, add_0, add_1 = pl.pallas_call(
        functools.partial(step_kernel, n_pair, own, piv, height, width),
        out_shape=(
            pltpu.VMEM(density.shape, F32),
            pltpu.VMEM((own, width), F32),
            pltpu.VMEM((own, width), F32),
        ),
        in_specs=[hbm] * 10,
        out_specs=(vmem, vmem, vmem),
        scratch_shapes=[
            pltpu.VMEM((piv, piv), F32),
            pltpu.VMEM((piv, piv), F32),
            pltpu.VMEM((piv, piv), jnp.int32),
            pltpu.VMEM((piv, piv), F32),
            pltpu.VMEM((1, piv), F32),
            pltpu.VMEM((1, piv), F32),
            pltpu.SMEM(block_rows.shape, jnp.int32),
            pltpu.SMEM(upstream.shape, jnp.int32),
            pltpu.VMEM(face_map.shape, jnp.int32),
            pltpu.VMEM((2, own, height, 128), F32),
            pltpu.VMEM((n_pair, own * 8 + 96, 128), I16),
            pltpu.VMEM((n_pair, own * 8 + 96, 128), I16),
            pltpu.VMEM((piv * 8, 128), F32),
            pltpu.VMEM((piv, 1024), F32),
            pltpu.VMEM((piv, 1024), F32),
            pltpu.VMEM((piv * 8, 128), F32),
            pltpu.VMEM((n_pair, own * 8 + 32, 128), I16),
            pltpu.VMEM((n_pair, own * 8 + 32, 128), I16),
            pltpu.VMEM((weight_rows, piv), BF16),
            pltpu.VMEM((weight_rows, 256), F32),
            pltpu.VMEM((RING, 48, width), I16),
            pltpu.VMEM((4, 80, width), I16),
            pltpu.VMEM((4, 80, width), I16),
            pltpu.VMEM((48, width), F32),
            pltpu.VMEM((48, 128), F32),
            pltpu.VMEM((48, 128), F32),
            pltpu.VMEM((piv, width), F32),
            pltpu.VMEM((2, piv, 128), F32),
            pltpu.VMEM((own, width), F32),
            pltpu.VMEM((n_pair, own, width), F32),
            pltpu.VMEM((piv, width), F32),
            pltpu.VMEM((piv * 8, 128), F32),
            pltpu.VMEM((piv, 128), F32),
            pltpu.VMEM((piv + 16, 128), F32),
            dma((13,)),
            dma((n_pair,)), dma((n_pair,)),
            dma((n_pair,)), dma((n_pair,)),
            dma((RING,)), dma((RING,)),
            dma((4,)), dma((4,)),
            dma((n_pair,)), dma((n_pair,)),
        ],
        compiler_params=pltpu.CompilerParams(
            collective_id=0, has_side_effects=True, vmem_limit_bytes=56 * 1024 * 1024),
    )(density, agg, share, target, frag, rate.reshape(1, piv), cour.reshape(1, piv), block_rows, upstream, face_map)
    row = lax.broadcasted_iota(jnp.int32, main.shape, 1)
    return main + jnp.where(row == 0, add_0[:, None, :], jnp.where(row == 1, add_1[:, None, :], 0.0))


def solution(mesh):
    in_specs = (P("pair", "blk", None), P(), P(), P(), P(), P(), P(), P(), P(), P("blk", None))
    out_specs = P("pair", "blk", None)
    return jax.shard_map(
        functools.partial(shards, mesh.shape["pair"]),
        mesh=mesh, in_specs=in_specs, out_specs=out_specs, check_vma=False)
```

```python
import functools

import jax
import jax.numpy as jnp
from jax import lax
from jax.experimental import pallas as pl
from jax.experimental.pallas import tpu as pltpu
from jax.sharding import PartitionSpec as P

MESH = pl.DeviceIdType.MESH
BANDS = 5
F32 = jnp.float32
BF16 = jnp.bfloat16
I16 = jnp.int16
RING, CORES = 4, 2
ORDER = (4, 3, 5, 2, 6, 1, 7)
MIDDLE = 1.025
STEP = 1.95 / 65534.0
LEAST = 32768.0 / 65536.0


def permuted(face, one_hot):
    total = None
    for _ in range(3):
        part = face.astype(BF16)
        face = face - part.astype(F32)
        moved = jnp.dot(part, one_hot, preferred_element_type=F32)
        total = moved if total is None else total + moved
    return total


def rounded16(x):
    return jnp.round(x).astype(jnp.int32).astype(I16)


def step_kernel(
    n_pair, own, piv, height, width,
    density, agg_h, share_h, target_h, frag_h, rate_h, cour_h, rows_h, up_h, map_h,
    main, add_0, add_1,
    agg, share, target, frag, rate, cour, rows_sm, up_sm, face_map, dens_v, enc, got, v0, sec, res, out_f, out_s, out_r, wb, y_s,
    ring, picked, picked_r, stage,
    side, row_c, halo_c, inflow_f, inflow_s, inflow_r, face, row_s, edge, wide_s,
    local_sem, main_send, main_recv, inflow_send, inflow_recv,
    ring_send, ring_recv, pick_send, pick_recv,
    out_send, out_recv,
):
    me_b, me_p = lax.axis_index("blk"), lax.axis_index("pair")
    grp = me_p // 2
    z_hi, y, core = me_b // (RING * CORES), (me_b // CORES) % RING, me_b % CORES
    pairs = [(me_p + d) % n_pair for d in range(n_pair)]

    def block_at(dz, dy, dc):
        return ((z_hi + dz) % 2) * (RING * CORES) + ((y + dy) % RING) * CORES + (core + dc) % CORES

    ring_mates = [block_at(0, d, 0) for d in range(RING)]
    pick_mates = [block_at(q // 2, 0, q % 2) for q in range(4)]

    barrier = pltpu.get_barrier_semaphore()
    for p in pairs[1:]:
        pl.semaphore_signal(barrier, inc=1, device_id=(me_b, p), device_id_type=MESH)
    for b in ring_mates[1:] + pick_mates[1:]:
        pl.semaphore_signal(barrier, inc=1, device_id=(b, me_p), device_id_type=MESH)

    loads = [pltpu.make_async_copy(density.at[:, :, pl.ds(t * 128, 128)], dens_v.at[t], local_sem.at[t])
             for t in range(2)]
    for load in loads:
        load.start()
    scalars = [pltpu.make_async_copy(rows_h, rows_sm, local_sem.at[11]),
               pltpu.make_async_copy(up_h, up_sm, local_sem.at[12])]
    map_load = pltpu.make_async_copy(map_h, face_map, local_sem.at[8])
    for load in scalars + [map_load]:
        load.start()
    tables = [pltpu.make_async_copy(src, dst, local_sem.at[2 + n]) for n, (src, dst) in enumerate(
        ((agg_h, agg), (share_h, share), (target_h, target), (frag_h, frag),
         (rate_h, rate), (cour_h, cour)))]
    for load in tables:
        load.start()

    def to_pair(d, src, dst, send, recv):
        return pltpu.make_async_remote_copy(
            src_ref=src, dst_ref=dst, send_sem=send.at[d], recv_sem=recv.at[d],
            device_id=(me_b, pairs[d]), device_id_type=MESH)

    def to_block(b, d, src, dst, send, recv):
        return pltpu.make_async_remote_copy(
            src_ref=src, dst_ref=dst, send_sem=send.at[d], recv_sem=recv.at[d],
            device_id=(b, me_p), device_id_type=MESH)

    def ring_slot(b):
        return (b // CORES) % RING

    inflow_f[...] = jnp.zeros(inflow_f.shape, F32)
    stage[...] = jnp.zeros(stage.shape, F32)
    for load in scalars:
        load.wait()
    live_rows = rows_sm[me_b]
    map_load.wait()
    stage[pl.ds(44, 1), :] = face_map[...].astype(F32)
    for load in loads:
        load.wait()
    dens_rows = dens_v.reshape(2 * own * height, 128)
    for n in range(2):
        for t in range(2):
            here = jnp.maximum(live_rows - 1 - n, 0) + t * own * height
            stage[pl.ds(24 * n, own), pl.ds(t * 128, 128)] = (
                dens_rows[pl.ds(here, own, stride=height), :] - MIDDLE) * (1.0 / STEP)
    ring[y] = rounded16(stage[...])
    pl.semaphore_wait(barrier, len(pairs) + len(ring_mates) + len(pick_mates) - 3)
    ring_out = [to_block(ring_mates[d], d, ring.at[y], ring.at[y], ring_send, ring_recv) for d in range(1, RING)]
    for copy in ring_out:
        copy.start()

    for t in range(2):
        side[pl.ds((2 + t) * own, own), :] = dens_rows[pl.ds(t * own * height, own, stride=height), :]
    main_in = []
    for d in ORDER + (0,):
        p = pairs[d]
        tile = dens_v[p % 2, :, pl.ds(pl.multiple_of((p // 2) * 8, 8), 8), :].reshape(own * 8, 128)
        for n in range(2):
            under = jnp.maximum((p // 2) * 8 - 1 - n, 0) + (p % 2) * own * height
            side[pl.ds(n * own, own), :] = dens_rows[pl.ds(under, own, stride=height), :]
        goal = enc.at[d] if d else got.at[me_p]
        goal[pl.ds(0, own * 8), :] = rounded16((tile - MIDDLE) * (1.0 / STEP))
        goal[pl.ds(own * 8, own * 4), :] = rounded16((side[...] - MIDDLE) * (1.0 / STEP))
        if d:
            main_in.append(to_pair(d, enc.at[d], got.at[me_p], main_send, main_recv))
            main_in[-1].start()

    for copy in ring_out:
        copy.wait_recv()
    for q in range(4):
        feeder = up_sm[pick_mates[q]]
        goal = picked.at[q] if q else picked_r.at[0]
        goal[pl.ds(0, 48), :] = ring[ring_slot(feeder)]
        goal[pl.ds(48, 32), :] = ring[ring_slot(up_sm[feeder]), pl.ds(0, 32), :]
    pick_out = [to_block(pick_mates[q], q, picked.at[q], picked_r.at[q], pick_send, pick_recv) for q in range(1, 4)]
    for copy in pick_out:
        copy.start()

    for load in tables:
        load.wait()
    row_id = lax.broadcasted_iota(jnp.int32, (piv, piv), 0)
    col_id = lax.broadcasted_iota(jnp.int32, (piv, piv), 1)
    kern = agg[...]
    part = share[...]
    low = (0.5 * kern * part).astype(BF16).astype(F32)
    high = (0.5 * kern * (1.0 - part)).astype(BF16).astype(F32)
    offset = (target[...] - jnp.maximum(row_id, col_id)).astype(F32)
    triangles = ((low, high, offset, col_id <= row_id), (low.T, high.T, offset.T, col_id < row_id))
    for d in range(BANDS):
        pair = [jnp.where(keep, jnp.where(off == d, lo, jnp.where(off == d - 1, hi, 0.0)), 0.0)
                for lo, hi, off, keep in triangles]
        wb[pl.ds(d * piv, piv), :] = (pair[0] + pair[1]).astype(BF16)
    pair = [jnp.where(keep & (off == -1), lo, 0.0)[piv - 8:] for lo, hi, off, keep in triangles]
    last = pltpu.roll(pair[0] + pair[1], 7, 0)
    rate_row = rate[...]
    cour_row = cour[...]
    base = BANDS * piv
    wb[pl.ds(base, piv), :] = kern.astype(BF16)
    wb[pl.ds(base + 2 * piv, 16), :] = jnp.concatenate([last, jnp.zeros_like(last)], axis=0).astype(BF16)
    smaller = (row_id < col_id).astype(F32)
    wb[pl.ds(base + piv, piv), :] = (frag[...] * rate_row * smaller).astype(BF16)
    diag = row_id == col_id
    rate_col = jnp.sum(jnp.where(diag, rate_row, 0.0), axis=1, keepdims=True)
    cour_col = jnp.sum(jnp.where(diag, cour_row, 0.0), axis=1, keepdims=True)
    own_diag = (lax.broadcasted_iota(jnp.int32, (own, piv), 0) + me_p * own
                == lax.broadcasted_iota(jnp.int32, (own, piv), 1))
    own_cour = jnp.sum(jnp.where(own_diag, cour_row, 0.0), axis=1, keepdims=True)
    own_rate = jnp.sum(jnp.where(own_diag, rate_row, 0.0), axis=1, keepdims=True)
    one_hot = (lax.broadcasted_iota(jnp.int32, (width, width), 0) == face_map[...]).astype(F32).astype(BF16)

    def mixed(v):
        y_s[:, :v.shape[1]] = jnp.dot(wb[...], v.astype(BF16), preferred_element_type=F32)
        vb = v.astype(BF16).astype(F32)
        cols = slice(0, v.shape[1])
        y_s[pl.ds(base + 2 * piv - 8, 8), cols] += y_s[pl.ds(base + 2 * piv, 8), cols] * vb[piv - 1:]
        births = None
        for d in reversed(range(BANDS)):
            here = vb * y_s[pl.ds(d * piv, piv), cols]
            births = here if births is None else here + pltpu.roll(births, 1, 0)
        return births - v * y_s[pl.ds(base, piv), cols] + y_s[pl.ds(base + piv, piv), cols]

    def change(v, prev):
        return v + (mixed(v) - rate_col * v - cour_col * (v - prev))

    def start_row(s):
        return v0[pl.ds(s, piv, stride=8), :]

    def pick_slot(b):
        return ((b // (RING * CORES) + z_hi) % 2) * 2 + (b + core) % CORES

    def first_inflow():
        for copy in pick_out:
            copy.wait_recv()
        feeder = up_sm[me_b]
        stage[...] = picked_r[pick_slot(feeder), pl.ds(0, 48), :].astype(jnp.int32).astype(F32)
        steps = permuted(stage[pl.ds(0, 24), :], one_hot)[:own]
        for t in range(2):
            inflow_f[pl.ds(t * own, own), :] = steps[:, t * 128:(t + 1) * 128]
        inflow_s[...] = rounded16(inflow_f[...])
        inflows = [to_pair(d, inflow_s, inflow_r.at[me_p], inflow_send, inflow_recv) for d in ORDER]
        for copy in inflows:
            copy.start()
        inflow_r[me_p] = inflow_s[...]
        inflow = steps * STEP + MIDDLE

        feeder_hot = (lax.broadcasted_iota(jnp.int32, (width, width), 0).astype(F32) == stage[pl.ds(44, 1), :])
        fed = picked_r[pick_slot(up_sm[feeder]), pl.ds(48, 32), :].astype(jnp.int32).astype(F32)
        fed = permuted(fed, feeder_hot.astype(F32).astype(BF16))
        prev = jnp.where(rows_sm[feeder] == 1, fed[:24], stage[pl.ds(24, 24), :])
        prev = permuted(prev, one_hot)[:own] * STEP + MIDDLE
        return inflows, inflow, inflow - own_cour * (inflow - prev) - own_rate * inflow

    for copy in main_in:
        copy.wait_recv()
    for p in range(n_pair):
        v0[pl.ds(p * own * 8, own * 8), :] = (
            got[p, pl.ds(0, own * 8), :].astype(jnp.int32).astype(F32) * STEP + MIDDLE)
        side[...] = got[p, pl.ds(own * 8, own * 4), :].astype(jnp.int32).astype(F32) * STEP + MIDDLE
        for t in range(2):
            row_c[pl.ds(p * own, own), pl.ds(t * 128, 128)] = side[pl.ds((2 + t) * own, own), :]
        for n in range(2):
            halo_c[n, pl.ds(p * own, own), :] = jnp.where(grp > 0, side[pl.ds(n * own, own), :], 0.0)

    for it in reversed(range(4)):
        s = 2 * it
        before = halo_c[0] if it == 0 else start_row(s - 1)
        first, second = start_row(s), start_row(s + 1)
        now = change(jnp.concatenate([first, second], axis=1), jnp.concatenate([before, first], axis=1))
        for t in range(2):
            row = grp * 8 + s + t
            piece = jnp.where(row < live_rows, now[:, t * 128:(t + 1) * 128], 0.0)
            sec[:, pl.ds((s + t) * 128, 128)] = piece
    edge[...] = change(halo_c[0], halo_c[1])

    def final_rows(it, before):
        v = sec[:, pl.ds(it * 256, 256)]
        now = change(v, jnp.concatenate([before, v[:, :128]], axis=1))
        return [0.5 * start_row(2 * it + t) + 0.5 * now[:, t * 128:(t + 1) * 128] for t in range(2)]

    biggest = None
    for it in reversed(range(4)):
        if it == 0:
            before = edge[...]
        else:
            before = sec[:, pl.ds((2 * it - 1) * 128, 128)]
        for t, piece in enumerate(final_rows(it, before)):
            row = grp * 8 + 2 * it + t
            piece = jnp.where((row < live_rows) & (row >= 1), piece, 0.0)
            res[:, pl.ds((2 * it + t) * 128, 128)] = piece
            size = jnp.abs(piece)
            biggest = size if biggest is None else jnp.maximum(biggest, size)

    inflows, inflow, linear = first_inflow()
    biggest = jnp.max(biggest, axis=1, keepdims=True)
    finer = jnp.where(biggest > 0.0, 32767.0 / biggest, 0.0)
    for s in range(8):
        out_f[pl.ds(s, piv, stride=8), :] = res[:, pl.ds(s * 128, 128)] * finer
    lane = lax.broadcasted_iota(jnp.int32, (piv, 128), 1)
    wide_s[pl.ds(piv, 16), :] = jnp.zeros((16, 128), F32)
    first = jnp.floor(biggest * LEAST)
    rest = (biggest * LEAST - first) * 32768.0
    second = jnp.floor(rest)
    third = jnp.floor((rest - second) * 32768.0)
    wide_s[pl.ds(0, piv), :] = jnp.where(lane == 0, first, jnp.where(lane == 1, second, jnp.where(lane == 2, third, 0.0)))
    for p in range(n_pair):
        out_s[p, pl.ds(0, own * 8), :] = rounded16(out_f[pl.ds(p * own * 8, own * 8), :])
        out_s[p, pl.ds(own * 8, 32), :] = rounded16(wide_s[pl.ds(p * own, 32), :])
    outs = [to_pair(d, out_s.at[pairs[d]], out_r.at[me_p], out_send, out_recv) for d in ORDER]
    for copy in outs:
        copy.start()
    out_own = pltpu.make_async_copy(out_s.at[me_p], out_r.at[me_p], local_sem.at[9])
    out_own.start()


    for copy in inflows:
        copy.wait_recv()
    for p in range(n_pair):
        inflow_f[...] = inflow_r[p].astype(jnp.int32).astype(F32) * STEP + MIDDLE
        for t in range(2):
            face[pl.ds(p * own, own), pl.ds(t * 128, 128)] = inflow_f[pl.ds(t * own, own), :]

    inflow_all = face[...]
    start = row_c[...]
    moved = change(start, inflow_all)
    row_0 = 0.5 * start + 0.5 * (moved + (mixed(moved) - rate_col * moved - cour_col * moved))
    row_0 = row_0 + 0.5 * cour_col * mixed(inflow_all)
    for t in range(2):
        row_s[pl.ds(t, piv, stride=8), :] = row_0[:, t * 128:(t + 1) * 128]
    for t in range(2):
        cols = slice(t * 128, (t + 1) * 128)
        mine = row_s[pl.ds(me_p * own * 8 + t, own, stride=8), :]
        add_0[:, cols] = mine + 0.5 * own_cour * linear[:, cols]
        add_1[:, cols] = jnp.where(live_rows > 1, 0.5 * own_cour * own_cour * inflow[:, cols], 0.0)

    digit = lax.broadcasted_iota(jnp.int32, (own, 128), 1)
    digit_size = jnp.where(
        digit == 0, 1.0, jnp.where(digit == 1, 1.0 / 32768.0, jnp.where(digit == 2, 1.0 / 32768.0 ** 2, 0.0))
    ) * (1.0 / (LEAST * 32767.0))
    out_own.wait()
    for copy in outs:
        copy.wait_recv()
    for p in range(n_pair):
        digits = out_r[p, pl.ds(own * 8, 32), :].astype(jnp.int32).astype(F32)[:own]
        scale = jnp.sum(digits * digit_size, axis=1, keepdims=True)
        tile = out_r[p, pl.ds(0, own * 8), :].astype(jnp.int32).astype(F32).reshape(own, 8, 128) * scale[:, :, None]
        main[:, pl.ds((p // 2) * 8, 8), pl.ds((p % 2) * 128, 128)] = tile

    for copy in (ring_out + main_in + pick_out + inflows + outs):
        copy.wait_send()


def shards(n_pair, density, agg, share, target, frag, rate, cour, block_rows, upstream, face_map):
    own, height, width = density.shape
    piv = agg.shape[0]
    vmem = pl.BlockSpec(memory_space=pltpu.VMEM)
    hbm = pl.BlockSpec(memory_space=pltpu.HBM)
    dma = pltpu.SemaphoreType.DMA
    weight_rows = (BANDS + 2) * piv + 16
    main, add_0, add_1 = pl.pallas_call(
        functools.partial(step_kernel, n_pair, own, piv, height, width),
        out_shape=(
            pltpu.VMEM(density.shape, F32),
            pltpu.VMEM((own, width), F32),
            pltpu.VMEM((own, width), F32),
        ),
        in_specs=[hbm] * 10,
        out_specs=(vmem, vmem, vmem),
        scratch_shapes=[
            pltpu.VMEM((piv, piv), F32),
            pltpu.VMEM((piv, piv), F32),
            pltpu.VMEM((piv, piv), jnp.int32),
            pltpu.VMEM((piv, piv), F32),
            pltpu.VMEM((1, piv), F32),
            pltpu.VMEM((1, piv), F32),
            pltpu.SMEM(block_rows.shape, jnp.int32),
            pltpu.SMEM(upstream.shape, jnp.int32),
            pltpu.VMEM(face_map.shape, jnp.int32),
            pltpu.VMEM((2, own, height, 128), F32),
            pltpu.VMEM((n_pair, own * 12, 128), I16),
            pltpu.VMEM((n_pair, own * 12, 128), I16),
            pltpu.VMEM((piv * 8, 128), F32),
            pltpu.VMEM((piv, 1024), F32),
            pltpu.VMEM((piv, 1024), F32),
            pltpu.VMEM((piv * 8, 128), F32),
            pltpu.VMEM((n_pair, own * 8 + 32, 128), I16),
            pltpu.VMEM((n_pair, own * 8 + 32, 128), I16),
            pltpu.VMEM((weight_rows, piv), BF16),
            pltpu.VMEM((weight_rows, 256), F32),
            pltpu.VMEM((RING, 48, width), I16),
            pltpu.VMEM((4, 80, width), I16),
            pltpu.VMEM((4, 80, width), I16),
            pltpu.VMEM((48, width), F32),
            pltpu.VMEM((own * 4, 128), F32),
            pltpu.VMEM((piv, width), F32),
            pltpu.VMEM((2, piv, 128), F32),
            pltpu.VMEM((48, 128), F32),
            pltpu.VMEM((48, 128), I16),
            pltpu.VMEM((n_pair, 48, 128), I16),
            pltpu.VMEM((piv, width), F32),
            pltpu.VMEM((piv * 8, 128), F32),
            pltpu.VMEM((piv, 128), F32),
            pltpu.VMEM((piv + 16, 128), F32),
            dma((13,)),
            dma((n_pair,)), dma((n_pair,)),
            dma((n_pair,)), dma((n_pair,)),
            dma((RING,)), dma((RING,)),
            dma((4,)), dma((4,)),
            dma((n_pair,)), dma((n_pair,)),
        ],
        compiler_params=pltpu.CompilerParams(
            collective_id=0, has_side_effects=True, vmem_limit_bytes=56 * 1024 * 1024),
    )(density, agg, share, target, frag, rate.reshape(1, piv), cour.reshape(1, piv), block_rows, upstream, face_map)
    row = lax.broadcasted_iota(jnp.int32, main.shape, 1)
    return main + jnp.where(row == 0, add_0[:, None, :], jnp.where(row == 1, add_1[:, None, :], 0.0))


def solution(mesh):
    in_specs = (P("pair", "blk", None), P(), P(), P(), P(), P(), P(), P(), P(), P("blk", None))
    out_specs = P("pair", "blk", None)
    return jax.shard_map(
        functools.partial(shards, mesh.shape["pair"]),
        mesh=mesh, in_specs=in_specs, out_specs=out_specs, check_vma=False)
```

```python
import functools

import jax
import jax.numpy as jnp
from jax import lax
from jax.experimental import pallas as pl
from jax.experimental.pallas import tpu as pltpu
from jax.sharding import PartitionSpec as P

MESH = pl.DeviceIdType.MESH
BANDS = 5
F32 = jnp.float32
BF16 = jnp.bfloat16
I16 = jnp.int16
RING, CORES = 4, 2
ORDER = (1, 7, 2, 6, 3, 5, 4)
MIDDLE = 1.025
STEP = 1.95 / 65534.0
LEAST = 32768.0 / 65536.0


def permuted(face, one_hot):
    total = None
    for _ in range(3):
        part = face.astype(BF16)
        face = face - part.astype(F32)
        moved = jnp.dot(part, one_hot, preferred_element_type=F32)
        total = moved if total is None else total + moved
    return total


def rounded16(x):
    return jnp.round(x).astype(jnp.int32).astype(I16)


def step_kernel(
    n_pair, own, piv, height, width,
    density, agg_h, share_h, target_h, frag_h, rate_h, cour_h, rows_h, up_h, map_h,
    main, add_0, add_1,
    agg, share, target, frag, rate, cour, rows_sm, up_sm, face_map, dens_v, enc, got, v0, sec, res, out_f, out_s, out_r, wb, y_s,
    ring, picked, picked_r, stage,
    side, row_c, halo_c, inflow_f, inflow_s, inflow_r, face, row_s, edge, wide_s,
    local_sem, main_send, main_recv, inflow_send, inflow_recv,
    ring_send, ring_recv, pick_send, pick_recv,
    out_send, out_recv,
):
    me_b, me_p = lax.axis_index("blk"), lax.axis_index("pair")
    grp = me_p // 2
    z_hi, y, core = me_b // (RING * CORES), (me_b // CORES) % RING, me_b % CORES
    pairs = [(me_p + d) % n_pair for d in range(n_pair)]

    def block_at(dz, dy, dc):
        return ((z_hi + dz) % 2) * (RING * CORES) + ((y + dy) % RING) * CORES + (core + dc) % CORES

    ring_mates = [block_at(0, d, 0) for d in range(RING)]
    pick_mates = [block_at(q // 2, 0, q % 2) for q in range(4)]

    barrier = pltpu.get_barrier_semaphore()
    for p in pairs[1:]:
        pl.semaphore_signal(barrier, inc=1, device_id=(me_b, p), device_id_type=MESH)
    for b in ring_mates[1:] + pick_mates[1:]:
        pl.semaphore_signal(barrier, inc=1, device_id=(b, me_p), device_id_type=MESH)

    loads = [pltpu.make_async_copy(density.at[:, :, pl.ds(t * 128, 128)], dens_v.at[t], local_sem.at[t])
             for t in range(2)]
    for load in loads:
        load.start()
    scalars = [pltpu.make_async_copy(rows_h, rows_sm, local_sem.at[11]),
               pltpu.make_async_copy(up_h, up_sm, local_sem.at[12])]
    map_load = pltpu.make_async_copy(map_h, face_map, local_sem.at[8])
    for load in scalars + [map_load]:
        load.start()
    tables = [pltpu.make_async_copy(src, dst, local_sem.at[2 + n]) for n, (src, dst) in enumerate(
        ((agg_h, agg), (share_h, share), (target_h, target), (frag_h, frag),
         (rate_h, rate), (cour_h, cour)))]
    for load in tables:
        load.start()

    def to_pair(d, src, dst, send, recv):
        return pltpu.make_async_remote_copy(
            src_ref=src, dst_ref=dst, send_sem=send.at[d], recv_sem=recv.at[d],
            device_id=(me_b, pairs[d]), device_id_type=MESH)

    def to_block(b, d, src, dst, send, recv):
        return pltpu.make_async_remote_copy(
            src_ref=src, dst_ref=dst, send_sem=send.at[d], recv_sem=recv.at[d],
            device_id=(b, me_p), device_id_type=MESH)

    def ring_slot(b):
        return (b // CORES) % RING

    inflow_f[...] = jnp.zeros(inflow_f.shape, F32)
    stage[...] = jnp.zeros(stage.shape, F32)
    for load in scalars:
        load.wait()
    live_rows = rows_sm[me_b]
    map_load.wait()
    stage[pl.ds(44, 1), :] = face_map[...].astype(F32)
    for load in loads:
        load.wait()
    dens_rows = dens_v.reshape(2 * own * height, 128)
    for n in range(2):
        for t in range(2):
            here = jnp.maximum(live_rows - 1 - n, 0) + t * own * height
            stage[pl.ds(24 * n, own), pl.ds(t * 128, 128)] = (
                dens_rows[pl.ds(here, own, stride=height), :] - MIDDLE) * (1.0 / STEP)
    ring[y] = rounded16(stage[...])
    pl.semaphore_wait(barrier, len(pairs) + len(ring_mates) + len(pick_mates) - 3)
    ring_out = [to_block(ring_mates[d], d, ring.at[y], ring.at[y], ring_send, ring_recv) for d in range(1, RING)]
    for copy in ring_out:
        copy.start()

    for t in range(2):
        side[pl.ds((2 + t) * own, own), :] = dens_rows[pl.ds(t * own * height, own, stride=height), :]
    main_in = []
    for d in ORDER + (0,):
        p = pairs[d]
        tile = dens_v[p % 2, :, pl.ds(pl.multiple_of((p // 2) * 8, 8), 8), :].reshape(own * 8, 128)
        for n in range(2):
            under = jnp.maximum((p // 2) * 8 - 1 - n, 0) + (p % 2) * own * height
            side[pl.ds(n * own, own), :] = dens_rows[pl.ds(under, own, stride=height), :]
        goal = enc.at[d] if d else got.at[me_p]
        goal[pl.ds(0, own * 8), :] = rounded16((tile - MIDDLE) * (1.0 / STEP))
        goal[pl.ds(own * 8, own * 4), :] = rounded16((side[...] - MIDDLE) * (1.0 / STEP))
        if d:
            main_in.append(to_pair(d, enc.at[d], got.at[me_p], main_send, main_recv))
            main_in[-1].start()

    for copy in ring_out:
        copy.wait_recv()
    for q in range(4):
        feeder = up_sm[pick_mates[q]]
        goal = picked.at[q] if q else picked_r.at[0]
        goal[pl.ds(0, 48), :] = ring[ring_slot(feeder)]
        goal[pl.ds(48, 32), :] = ring[ring_slot(up_sm[feeder]), pl.ds(0, 32), :]
    pick_out = [to_block(pick_mates[q], q, picked.at[q], picked_r.at[q], pick_send, pick_recv) for q in range(1, 4)]
    for copy in pick_out:
        copy.start()

    for load in tables:
        load.wait()
    row_id = lax.broadcasted_iota(jnp.int32, (piv, piv), 0)
    col_id = lax.broadcasted_iota(jnp.int32, (piv, piv), 1)
    kern = agg[...]
    part = share[...]
    low = (0.5 * kern * part).astype(BF16).astype(F32)
    high = (0.5 * kern * (1.0 - part)).astype(BF16).astype(F32)
    offset = (target[...] - jnp.maximum(row_id, col_id)).astype(F32)
    triangles = ((low, high, offset, col_id <= row_id), (low.T, high.T, offset.T, col_id < row_id))
    for d in range(BANDS):
        pair = [jnp.where(keep, jnp.where(off == d, lo, jnp.where(off == d - 1, hi, 0.0)), 0.0)
                for lo, hi, off, keep in triangles]
        wb[pl.ds(d * piv, piv), :] = (pair[0] + pair[1]).astype(BF16)
    pair = [jnp.where(keep & (off == -1), lo, 0.0)[piv - 8:] for lo, hi, off, keep in triangles]
    last = pltpu.roll(pair[0] + pair[1], 7, 0)
    rate_row = rate[...]
    cour_row = cour[...]
    base = BANDS * piv
    wb[pl.ds(base, piv), :] = kern.astype(BF16)
    wb[pl.ds(base + 2 * piv, 16), :] = jnp.concatenate([last, jnp.zeros_like(last)], axis=0).astype(BF16)
    smaller = (row_id < col_id).astype(F32)
    wb[pl.ds(base + piv, piv), :] = (frag[...] * rate_row * smaller).astype(BF16)
    diag = row_id == col_id
    rate_col = jnp.sum(jnp.where(diag, rate_row, 0.0), axis=1, keepdims=True)
    cour_col = jnp.sum(jnp.where(diag, cour_row, 0.0), axis=1, keepdims=True)
    own_diag = (lax.broadcasted_iota(jnp.int32, (own, piv), 0) + me_p * own
                == lax.broadcasted_iota(jnp.int32, (own, piv), 1))
    own_cour = jnp.sum(jnp.where(own_diag, cour_row, 0.0), axis=1, keepdims=True)
    own_rate = jnp.sum(jnp.where(own_diag, rate_row, 0.0), axis=1, keepdims=True)
    one_hot = (lax.broadcasted_iota(jnp.int32, (width, width), 0) == face_map[...]).astype(F32).astype(BF16)

    def mixed(v):
        y_s[:, :v.shape[1]] = jnp.dot(wb[...], v.astype(BF16), preferred_element_type=F32)
        vb = v.astype(BF16).astype(F32)
        cols = slice(0, v.shape[1])
        y_s[pl.ds(base + 2 * piv - 8, 8), cols] += y_s[pl.ds(base + 2 * piv, 8), cols] * vb[piv - 1:]
        births = None
        for d in reversed(range(BANDS)):
            here = vb * y_s[pl.ds(d * piv, piv), cols]
            births = here if births is None else here + pltpu.roll(births, 1, 0)
        return births - v * y_s[pl.ds(base, piv), cols] + y_s[pl.ds(base + piv, piv), cols]

    def change(v, prev):
        return v + (mixed(v) - rate_col * v - cour_col * (v - prev))

    def start_row(s):
        return v0[pl.ds(s, piv, stride=8), :]

    def pick_slot(b):
        return ((b // (RING * CORES) + z_hi) % 2) * 2 + (b + core) % CORES

    def first_inflow():
        for copy in pick_out:
            copy.wait_recv()
        feeder = up_sm[me_b]
        stage[...] = picked_r[pick_slot(feeder), pl.ds(0, 48), :].astype(jnp.int32).astype(F32)
        steps = permuted(stage[pl.ds(0, 24), :], one_hot)[:own]
        for t in range(2):
            inflow_f[pl.ds(t * own, own), :] = steps[:, t * 128:(t + 1) * 128]
        inflow_s[...] = rounded16(inflow_f[...])
        inflows = [to_pair(d, inflow_s, inflow_r.at[me_p], inflow_send, inflow_recv) for d in ORDER]
        for copy in inflows:
            copy.start()
        inflow_r[me_p] = inflow_s[...]
        inflow = steps * STEP + MIDDLE

        feeder_hot = (lax.broadcasted_iota(jnp.int32, (width, width), 0).astype(F32) == stage[pl.ds(44, 1), :])
        fed = picked_r[pick_slot(up_sm[feeder]), pl.ds(48, 32), :].astype(jnp.int32).astype(F32)
        fed = permuted(fed, feeder_hot.astype(F32).astype(BF16))
        prev = jnp.where(rows_sm[feeder] == 1, fed[:24], stage[pl.ds(24, 24), :])
        prev = permuted(prev, one_hot)[:own] * STEP + MIDDLE
        return inflows, inflow, inflow - own_cour * (inflow - prev) - own_rate * inflow

    for copy in main_in:
        copy.wait_recv()
    for p in range(n_pair):
        v0[pl.ds(p * own * 8, own * 8), :] = (
            got[p, pl.ds(0, own * 8), :].astype(jnp.int32).astype(F32) * STEP + MIDDLE)
        side[...] = got[p, pl.ds(own * 8, own * 4), :].astype(jnp.int32).astype(F32) * STEP + MIDDLE
        for t in range(2):
            row_c[pl.ds(p * own, own), pl.ds(t * 128, 128)] = side[pl.ds((2 + t) * own, own), :]
        for n in range(2):
            halo_c[n, pl.ds(p * own, own), :] = jnp.where(grp > 0, side[pl.ds(n * own, own), :], 0.0)

    for it in reversed(range(4)):
        s = 2 * it
        before = halo_c[0] if it == 0 else start_row(s - 1)
        first, second = start_row(s), start_row(s + 1)
        now = change(jnp.concatenate([first, second], axis=1), jnp.concatenate([before, first], axis=1))
        for t in range(2):
            row = grp * 8 + s + t
            piece = jnp.where(row < live_rows, now[:, t * 128:(t + 1) * 128], 0.0)
            sec[:, pl.ds((s + t) * 128, 128)] = piece
    edge[...] = change(halo_c[0], halo_c[1])

    def final_rows(it, before):
        v = sec[:, pl.ds(it * 256, 256)]
        now = change(v, jnp.concatenate([before, v[:, :128]], axis=1))
        return [0.5 * start_row(2 * it + t) + 0.5 * now[:, t * 128:(t + 1) * 128] for t in range(2)]

    biggest = None
    for it in reversed(range(4)):
        if it == 0:
            before = edge[...]
        else:
            before = sec[:, pl.ds((2 * it - 1) * 128, 128)]
        for t, piece in enumerate(final_rows(it, before)):
            row = grp * 8 + 2 * it + t
            piece = jnp.where((row < live_rows) & (row >= 1), piece, 0.0)
            res[:, pl.ds((2 * it + t) * 128, 128)] = piece
            size = jnp.abs(piece)
            biggest = size if biggest is None else jnp.maximum(biggest, size)

    inflows, inflow, linear = first_inflow()
    biggest = jnp.max(biggest, axis=1, keepdims=True)
    finer = jnp.where(biggest > 0.0, 32767.0 / biggest, 0.0)
    for s in range(8):
        out_f[pl.ds(s, piv, stride=8), :] = res[:, pl.ds(s * 128, 128)] * finer
    lane = lax.broadcasted_iota(jnp.int32, (piv, 128), 1)
    wide_s[pl.ds(piv, 16), :] = jnp.zeros((16, 128), F32)
    first = jnp.floor(biggest * LEAST)
    rest = (biggest * LEAST - first) * 32768.0
    second = jnp.floor(rest)
    third = jnp.floor((rest - second) * 32768.0)
    wide_s[pl.ds(0, piv), :] = jnp.where(lane == 0, first, jnp.where(lane == 1, second, jnp.where(lane == 2, third, 0.0)))
    for p in range(n_pair):
        out_s[p, pl.ds(0, own * 8), :] = rounded16(out_f[pl.ds(p * own * 8, own * 8), :])
        out_s[p, pl.ds(own * 8, 32), :] = rounded16(wide_s[pl.ds(p * own, 32), :])
    outs = [to_pair(d, out_s.at[pairs[d]], out_r.at[me_p], out_send, out_recv) for d in ORDER]
    for copy in outs:
        copy.start()
    out_own = pltpu.make_async_copy(out_s.at[me_p], out_r.at[me_p], local_sem.at[9])
    out_own.start()


    for copy in inflows:
        copy.wait_recv()
    for p in range(n_pair):
        inflow_f[...] = inflow_r[p].astype(jnp.int32).astype(F32) * STEP + MIDDLE
        for t in range(2):
            face[pl.ds(p * own, own), pl.ds(t * 128, 128)] = inflow_f[pl.ds(t * own, own), :]

    inflow_all = face[...]
    start = row_c[...]
    moved = change(start, inflow_all)
    row_0 = 0.5 * start + 0.5 * (moved + (mixed(moved) - rate_col * moved - cour_col * moved))
    row_0 = row_0 + 0.5 * cour_col * mixed(inflow_all)
    for t in range(2):
        row_s[pl.ds(t, piv, stride=8), :] = row_0[:, t * 128:(t + 1) * 128]
    for t in range(2):
        cols = slice(t * 128, (t + 1) * 128)
        mine = row_s[pl.ds(me_p * own * 8 + t, own, stride=8), :]
        add_0[:, cols] = mine + 0.5 * own_cour * linear[:, cols]
        add_1[:, cols] = jnp.where(live_rows > 1, 0.5 * own_cour * own_cour * inflow[:, cols], 0.0)

    digit = lax.broadcasted_iota(jnp.int32, (own, 128), 1)
    digit_size = jnp.where(
        digit == 0, 1.0, jnp.where(digit == 1, 1.0 / 32768.0, jnp.where(digit == 2, 1.0 / 32768.0 ** 2, 0.0))
    ) * (1.0 / (LEAST * 32767.0))
    out_own.wait()
    for copy in outs:
        copy.wait_recv()
    for p in range(n_pair):
        digits = out_r[p, pl.ds(own * 8, 32), :].astype(jnp.int32).astype(F32)[:own]
        scale = jnp.sum(digits * digit_size, axis=1, keepdims=True)
        tile = out_r[p, pl.ds(0, own * 8), :].astype(jnp.int32).astype(F32).reshape(own, 8, 128) * scale[:, :, None]
        main[:, pl.ds((p // 2) * 8, 8), pl.ds((p % 2) * 128, 128)] = tile

    for copy in (ring_out + main_in + pick_out + inflows + outs):
        copy.wait_send()


def shards(n_pair, density, agg, share, target, frag, rate, cour, block_rows, upstream, face_map):
    own, height, width = density.shape
    piv = agg.shape[0]
    vmem = pl.BlockSpec(memory_space=pltpu.VMEM)
    hbm = pl.BlockSpec(memory_space=pltpu.HBM)
    dma = pltpu.SemaphoreType.DMA
    weight_rows = (BANDS + 2) * piv + 16
    main, add_0, add_1 = pl.pallas_call(
        functools.partial(step_kernel, n_pair, own, piv, height, width),
        out_shape=(
            pltpu.VMEM(density.shape, F32),
            pltpu.VMEM((own, width), F32),
            pltpu.VMEM((own, width), F32),
        ),
        in_specs=[hbm] * 10,
        out_specs=(vmem, vmem, vmem),
        scratch_shapes=[
            pltpu.VMEM((piv, piv), F32),
            pltpu.VMEM((piv, piv), F32),
            pltpu.VMEM((piv, piv), jnp.int32),
            pltpu.VMEM((piv, piv), F32),
            pltpu.VMEM((1, piv), F32),
            pltpu.VMEM((1, piv), F32),
            pltpu.SMEM(block_rows.shape, jnp.int32),
            pltpu.SMEM(upstream.shape, jnp.int32),
            pltpu.VMEM(face_map.shape, jnp.int32),
            pltpu.VMEM((2, own, height, 128), F32),
            pltpu.VMEM((n_pair, own * 12, 128), I16),
            pltpu.VMEM((n_pair, own * 12, 128), I16),
            pltpu.VMEM((piv * 8, 128), F32),
            pltpu.VMEM((piv, 1024), F32),
            pltpu.VMEM((piv, 1024), F32),
            pltpu.VMEM((piv * 8, 128), F32),
            pltpu.VMEM((n_pair, own * 8 + 32, 128), I16),
            pltpu.VMEM((n_pair, own * 8 + 32, 128), I16),
            pltpu.VMEM((weight_rows, piv), BF16),
            pltpu.VMEM((weight_rows, 256), F32),
            pltpu.VMEM((RING, 48, width), I16),
            pltpu.VMEM((4, 80, width), I16),
            pltpu.VMEM((4, 80, width), I16),
            pltpu.VMEM((48, width), F32),
            pltpu.VMEM((own * 4, 128), F32),
            pltpu.VMEM((piv, width), F32),
            pltpu.VMEM((2, piv, 128), F32),
            pltpu.VMEM((48, 128), F32),
            pltpu.VMEM((48, 128), I16),
            pltpu.VMEM((n_pair, 48, 128), I16),
            pltpu.VMEM((piv, width), F32),
            pltpu.VMEM((piv * 8, 128), F32),
            pltpu.VMEM((piv, 128), F32),
            pltpu.VMEM((piv + 16, 128), F32),
            dma((13,)),
            dma((n_pair,)), dma((n_pair,)),
            dma((n_pair,)), dma((n_pair,)),
            dma((RING,)), dma((RING,)),
            dma((4,)), dma((4,)),
            dma((n_pair,)), dma((n_pair,)),
        ],
        compiler_params=pltpu.CompilerParams(
            collective_id=0, has_side_effects=True, vmem_limit_bytes=56 * 1024 * 1024),
    )(density, agg, share, target, frag, rate.reshape(1, piv), cour.reshape(1, piv), block_rows, upstream, face_map)
    row = lax.broadcasted_iota(jnp.int32, main.shape, 1)
    return main + jnp.where(row == 0, add_0[:, None, :], jnp.where(row == 1, add_1[:, None, :], 0.0))


def solution(mesh):
    in_specs = (P("pair", "blk", None), P(), P(), P(), P(), P(), P(), P(), P(), P("blk", None))
    out_specs = P("pair", "blk", None)
    return jax.shard_map(
        functools.partial(shards, mesh.shape["pair"]),
        mesh=mesh, in_specs=in_specs, out_specs=out_specs, check_vma=False)
```

```python
import functools

import jax
import jax.numpy as jnp
from jax import lax
from jax.experimental import pallas as pl
from jax.experimental.pallas import tpu as pltpu
from jax.sharding import PartitionSpec as P

MESH = pl.DeviceIdType.MESH
BANDS = 5
F32 = jnp.float32
BF16 = jnp.bfloat16
I16 = jnp.int16
RING, CORES = 4, 2
ORDER = (1, 7, 2, 6, 3, 5, 4)
MIDDLE = 1.025
STEP = 1.95 / 65534.0
LEAST = 32768.0 / 65536.0


def permuted(face, one_hot):
    total = None
    for _ in range(3):
        part = face.astype(BF16)
        face = face - part.astype(F32)
        moved = jnp.dot(part, one_hot, preferred_element_type=F32)
        total = moved if total is None else total + moved
    return total


def rounded16(x):
    return jnp.round(x).astype(jnp.int32).astype(I16)


def step_kernel(
    n_pair, own, piv, height, width,
    density, agg_h, share_h, target_h, frag_h, rate_h, cour_h, rows_h, up_h, map_h,
    main, add_0, add_1,
    agg, share, target, frag, rate, cour, rows_sm, up_sm, face_map, dens_v, enc, got, v0, sec, res, out_f, out_s, out_r, wb, y_s,
    ring, picked, picked_r, stage,
    side, row_c, halo_c, inflow_f, inflow_s, inflow_r, face, row_s, edge, wide_s,
    local_sem, main_send, main_recv, inflow_send, inflow_recv,
    ring_send, ring_recv, pick_send, pick_recv,
    out_send, out_recv,
):
    me_b, me_p = lax.axis_index("blk"), lax.axis_index("pair")
    grp = me_p // 2
    z_hi, y, core = me_b // (RING * CORES), (me_b // CORES) % RING, me_b % CORES
    pairs = [(me_p + d) % n_pair for d in range(n_pair)]

    def block_at(dz, dy, dc):
        return ((z_hi + dz) % 2) * (RING * CORES) + ((y + dy) % RING) * CORES + (core + dc) % CORES

    ring_mates = [block_at(0, d, 0) for d in range(RING)]
    pick_mates = [block_at(q // 2, 0, q % 2) for q in range(4)]

    barrier = pltpu.get_barrier_semaphore()
    for p in pairs[1:]:
        pl.semaphore_signal(barrier, inc=1, device_id=(me_b, p), device_id_type=MESH)
    for b in ring_mates[1:] + pick_mates[1:]:
        pl.semaphore_signal(barrier, inc=1, device_id=(b, me_p), device_id_type=MESH)

    loads = [pltpu.make_async_copy(density.at[:, :, pl.ds(t * 128, 128)], dens_v.at[t], local_sem.at[t])
             for t in range(2)]
    for load in loads:
        load.start()
    scalars = [pltpu.make_async_copy(rows_h, rows_sm, local_sem.at[11]),
               pltpu.make_async_copy(up_h, up_sm, local_sem.at[12])]
    map_load = pltpu.make_async_copy(map_h, face_map, local_sem.at[8])
    for load in scalars + [map_load]:
        load.start()
    tables = [pltpu.make_async_copy(src, dst, local_sem.at[2 + n]) for n, (src, dst) in enumerate(
        ((agg_h, agg), (share_h, share), (target_h, target), (frag_h, frag),
         (rate_h, rate), (cour_h, cour)))]
    for load in tables:
        load.start()

    def to_pair(d, src, dst, send, recv):
        return pltpu.make_async_remote_copy(
            src_ref=src, dst_ref=dst, send_sem=send.at[d], recv_sem=recv.at[d],
            device_id=(me_b, pairs[d]), device_id_type=MESH)

    def to_block(b, d, src, dst, send, recv):
        return pltpu.make_async_remote_copy(
            src_ref=src, dst_ref=dst, send_sem=send.at[d], recv_sem=recv.at[d],
            device_id=(b, me_p), device_id_type=MESH)

    def ring_slot(b):
        return (b // CORES) % RING

    inflow_f[...] = jnp.zeros(inflow_f.shape, F32)
    stage[...] = jnp.zeros(stage.shape, F32)
    for load in scalars:
        load.wait()
    live_rows = rows_sm[me_b]
    map_load.wait()
    stage[pl.ds(44, 1), :] = face_map[...].astype(F32)
    for load in loads:
        load.wait()
    dens_rows = dens_v.reshape(2 * own * height, 128)
    for n in range(2):
        for t in range(2):
            here = jnp.maximum(live_rows - 1 - n, 0) + t * own * height
            stage[pl.ds(24 * n, own), pl.ds(t * 128, 128)] = (
                dens_rows[pl.ds(here, own, stride=height), :] - MIDDLE) * (1.0 / STEP)
    ring[y] = rounded16(stage[...])
    pl.semaphore_wait(barrier, len(pairs) + len(ring_mates) + len(pick_mates) - 3)
    ring_out = [to_block(ring_mates[d], d, ring.at[y], ring.at[y], ring_send, ring_recv) for d in range(1, RING)]
    for copy in ring_out:
        copy.start()

    for t in range(2):
        side[pl.ds((2 + t) * own, own), :] = dens_rows[pl.ds(t * own * height, own, stride=height), :]
    main_in = []
    for d in ORDER + (0,):
        p = pairs[d]
        tile = dens_v[p % 2, :, pl.ds(pl.multiple_of((p // 2) * 8, 8), 8), :].reshape(own * 8, 128)
        for n in range(2):
            under = jnp.maximum((p // 2) * 8 - 1 - n, 0) + (p % 2) * own * height
            side[pl.ds(n * own, own), :] = dens_rows[pl.ds(under, own, stride=height), :]
        goal = enc.at[d] if d else got.at[me_p]
        goal[pl.ds(0, own * 8), :] = rounded16((tile - MIDDLE) * (1.0 / STEP))
        goal[pl.ds(own * 8, own * 4), :] = rounded16((side[...] - MIDDLE) * (1.0 / STEP))
        if d:
            main_in.append(to_pair(d, enc.at[d], got.at[me_p], main_send, main_recv))
            main_in[-1].start()

    for copy in ring_out:
        copy.wait_recv()
    for q in range(4):
        feeder = up_sm[pick_mates[q]]
        goal = picked.at[q] if q else picked_r.at[0]
        goal[pl.ds(0, 48), :] = ring[ring_slot(feeder)]
        goal[pl.ds(48, 32), :] = ring[ring_slot(up_sm[feeder]), pl.ds(0, 32), :]
    pick_out = [to_block(pick_mates[q], q, picked.at[q], picked_r.at[q], pick_send, pick_recv) for q in range(1, 4)]
    for copy in pick_out:
        copy.start()

    for load in tables:
        load.wait()
    row_id = lax.broadcasted_iota(jnp.int32, (piv, piv), 0)
    col_id = lax.broadcasted_iota(jnp.int32, (piv, piv), 1)
    kern = agg[...]
    part = share[...]
    low = (0.5 * kern * part).astype(BF16).astype(F32)
    high = (0.5 * kern * (1.0 - part)).astype(BF16).astype(F32)
    offset = (target[...] - jnp.maximum(row_id, col_id)).astype(F32)
    triangles = ((low, high, offset, col_id <= row_id), (low.T, high.T, offset.T, col_id < row_id))
    for d in range(BANDS):
        pair = [jnp.where(keep, jnp.where(off == d, lo, jnp.where(off == d - 1, hi, 0.0)), 0.0)
                for lo, hi, off, keep in triangles]
        wb[pl.ds(d * piv, piv), :] = (pair[0] + pair[1]).astype(BF16)
    pair = [jnp.where(keep & (off == -1), lo, 0.0)[piv - 8:] for lo, hi, off, keep in triangles]
    last = pltpu.roll(pair[0] + pair[1], 7, 0)
    rate_row = rate[...]
    cour_row = cour[...]
    base = BANDS * piv
    wb[pl.ds(base, piv), :] = kern.astype(BF16)
    wb[pl.ds(base + 2 * piv, 16), :] = jnp.concatenate([last, jnp.zeros_like(last)], axis=0).astype(BF16)
    smaller = (row_id < col_id).astype(F32)
    wb[pl.ds(base + piv, piv), :] = (frag[...] * rate_row * smaller).astype(BF16)
    diag = row_id == col_id
    rate_col = jnp.sum(jnp.where(diag, rate_row, 0.0), axis=1, keepdims=True)
    cour_col = jnp.sum(jnp.where(diag, cour_row, 0.0), axis=1, keepdims=True)
    own_diag = (lax.broadcasted_iota(jnp.int32, (own, piv), 0) + me_p * own
                == lax.broadcasted_iota(jnp.int32, (own, piv), 1))
    own_cour = jnp.sum(jnp.where(own_diag, cour_row, 0.0), axis=1, keepdims=True)
    own_rate = jnp.sum(jnp.where(own_diag, rate_row, 0.0), axis=1, keepdims=True)
    one_hot = (lax.broadcasted_iota(jnp.int32, (width, width), 0) == face_map[...]).astype(F32).astype(BF16)

    def mixed(v):
        y_s[:, :v.shape[1]] = jnp.dot(wb[...], v.astype(BF16), preferred_element_type=F32)
        vb = v.astype(BF16).astype(F32)
        cols = slice(0, v.shape[1])
        y_s[pl.ds(base + 2 * piv - 8, 8), cols] += y_s[pl.ds(base + 2 * piv, 8), cols] * vb[piv - 1:]
        births = None
        for d in reversed(range(BANDS)):
            here = vb * y_s[pl.ds(d * piv, piv), cols]
            births = here if births is None else here + pltpu.roll(births, 1, 0)
        return births - v * y_s[pl.ds(base, piv), cols] + y_s[pl.ds(base + piv, piv), cols]

    def change(v, prev):
        return v + (mixed(v) - rate_col * v - cour_col * (v - prev))

    def start_row(s):
        return v0[pl.ds(s, piv, stride=8), :]

    def pick_slot(b):
        return ((b // (RING * CORES) + z_hi) % 2) * 2 + (b + core) % CORES

    def first_inflow():
        for copy in pick_out:
            copy.wait_recv()
        feeder = up_sm[me_b]
        stage[...] = picked_r[pick_slot(feeder), pl.ds(0, 48), :].astype(jnp.int32).astype(F32)
        steps = permuted(stage[pl.ds(0, 24), :], one_hot)[:own]
        for t in range(2):
            inflow_f[pl.ds(t * own, own), :] = steps[:, t * 128:(t + 1) * 128]
        inflow_s[...] = rounded16(inflow_f[...])
        inflows = [to_pair(d, inflow_s, inflow_r.at[me_p], inflow_send, inflow_recv) for d in ORDER]
        for copy in inflows:
            copy.start()
        inflow_r[me_p] = inflow_s[...]
        return inflows, steps * STEP + MIDDLE

    def linear_part(inflow):
        feeder = up_sm[me_b]
        feeder_hot = (lax.broadcasted_iota(jnp.int32, (width, width), 0).astype(F32) == stage[pl.ds(44, 1), :])
        fed = picked_r[pick_slot(up_sm[feeder]), pl.ds(48, 32), :].astype(jnp.int32).astype(F32)
        fed = permuted(fed, feeder_hot.astype(F32).astype(BF16))
        prev = jnp.where(rows_sm[feeder] == 1, fed[:24], stage[pl.ds(24, 24), :])
        prev = permuted(prev, one_hot)[:own] * STEP + MIDDLE
        return inflow - own_cour * (inflow - prev) - own_rate * inflow

    for copy in main_in:
        copy.wait_recv()
    for p in range(n_pair):
        v0[pl.ds(p * own * 8, own * 8), :] = (
            got[p, pl.ds(0, own * 8), :].astype(jnp.int32).astype(F32) * STEP + MIDDLE)
        side[...] = got[p, pl.ds(own * 8, own * 4), :].astype(jnp.int32).astype(F32) * STEP + MIDDLE
        for t in range(2):
            row_c[pl.ds(p * own, own), pl.ds(t * 128, 128)] = side[pl.ds((2 + t) * own, own), :]
        for n in range(2):
            halo_c[n, pl.ds(p * own, own), :] = jnp.where(grp > 0, side[pl.ds(n * own, own), :], 0.0)

    for it in reversed(range(4)):
        s = 2 * it
        before = halo_c[0] if it == 0 else start_row(s - 1)
        first, second = start_row(s), start_row(s + 1)
        now = change(jnp.concatenate([first, second], axis=1), jnp.concatenate([before, first], axis=1))
        for t in range(2):
            row = grp * 8 + s + t
            piece = jnp.where(row < live_rows, now[:, t * 128:(t + 1) * 128], 0.0)
            sec[:, pl.ds((s + t) * 128, 128)] = piece
    edge[...] = change(halo_c[0], halo_c[1])

    def final_rows(it, before):
        v = sec[:, pl.ds(it * 256, 256)]
        now = change(v, jnp.concatenate([before, v[:, :128]], axis=1))
        return [0.5 * start_row(2 * it + t) + 0.5 * now[:, t * 128:(t + 1) * 128] for t in range(2)]

    biggest = None
    for it in reversed(range(4)):
        if it == 0:
            before = edge[...]
        else:
            before = sec[:, pl.ds((2 * it - 1) * 128, 128)]
        for t, piece in enumerate(final_rows(it, before)):
            row = grp * 8 + 2 * it + t
            piece = jnp.where((row < live_rows) & (row >= 1), piece, 0.0)
            res[:, pl.ds((2 * it + t) * 128, 128)] = piece
            size = jnp.abs(piece)
            biggest = size if biggest is None else jnp.maximum(biggest, size)

    inflows, inflow = first_inflow()
    biggest = jnp.max(biggest, axis=1, keepdims=True)
    finer = jnp.where(biggest > 0.0, 32767.0 / biggest, 0.0)
    for s in range(8):
        out_f[pl.ds(s, piv, stride=8), :] = res[:, pl.ds(s * 128, 128)] * finer
    lane = lax.broadcasted_iota(jnp.int32, (piv, 128), 1)
    wide_s[pl.ds(piv, 16), :] = jnp.zeros((16, 128), F32)
    first = jnp.floor(biggest * LEAST)
    rest = (biggest * LEAST - first) * 32768.0
    second = jnp.floor(rest)
    third = jnp.floor((rest - second) * 32768.0)
    wide_s[pl.ds(0, piv), :] = jnp.where(lane == 0, first, jnp.where(lane == 1, second, jnp.where(lane == 2, third, 0.0)))
    for p in range(n_pair):
        out_s[p, pl.ds(0, own * 8), :] = rounded16(out_f[pl.ds(p * own * 8, own * 8), :])
        out_s[p, pl.ds(own * 8, 32), :] = rounded16(wide_s[pl.ds(p * own, 32), :])
    outs = [to_pair(d, out_s.at[pairs[d]], out_r.at[me_p], out_send, out_recv) for d in ORDER]
    for copy in outs:
        copy.start()
    out_own = pltpu.make_async_copy(out_s.at[me_p], out_r.at[me_p], local_sem.at[9])
    out_own.start()
    linear = linear_part(inflow)


    for copy in inflows:
        copy.wait_recv()
    for p in range(n_pair):
        inflow_f[...] = inflow_r[p].astype(jnp.int32).astype(F32) * STEP + MIDDLE
        for t in range(2):
            face[pl.ds(p * own, own), pl.ds(t * 128, 128)] = inflow_f[pl.ds(t * own, own), :]

    inflow_all = face[...]
    start = row_c[...]
    moved = change(start, inflow_all)
    row_0 = 0.5 * start + 0.5 * (moved + (mixed(moved) - rate_col * moved - cour_col * moved))
    row_0 = row_0 + 0.5 * cour_col * mixed(inflow_all)
    for t in range(2):
        row_s[pl.ds(t, piv, stride=8), :] = row_0[:, t * 128:(t + 1) * 128]
    for t in range(2):
        cols = slice(t * 128, (t + 1) * 128)
        mine = row_s[pl.ds(me_p * own * 8 + t, own, stride=8), :]
        add_0[:, cols] = mine + 0.5 * own_cour * linear[:, cols]
        add_1[:, cols] = jnp.where(live_rows > 1, 0.5 * own_cour * own_cour * inflow[:, cols], 0.0)

    digit = lax.broadcasted_iota(jnp.int32, (own, 128), 1)
    digit_size = jnp.where(
        digit == 0, 1.0, jnp.where(digit == 1, 1.0 / 32768.0, jnp.where(digit == 2, 1.0 / 32768.0 ** 2, 0.0))
    ) * (1.0 / (LEAST * 32767.0))
    out_own.wait()
    for copy in outs:
        copy.wait_recv()
    for p in range(n_pair):
        digits = out_r[p, pl.ds(own * 8, 32), :].astype(jnp.int32).astype(F32)[:own]
        scale = jnp.sum(digits * digit_size, axis=1, keepdims=True)
        tile = out_r[p, pl.ds(0, own * 8), :].astype(jnp.int32).astype(F32).reshape(own, 8, 128) * scale[:, :, None]
        main[:, pl.ds((p // 2) * 8, 8), pl.ds((p % 2) * 128, 128)] = tile

    for copy in (ring_out + main_in + pick_out + inflows + outs):
        copy.wait_send()


def shards(n_pair, density, agg, share, target, frag, rate, cour, block_rows, upstream, face_map):
    own, height, width = density.shape
    piv = agg.shape[0]
    vmem = pl.BlockSpec(memory_space=pltpu.VMEM)
    hbm = pl.BlockSpec(memory_space=pltpu.HBM)
    dma = pltpu.SemaphoreType.DMA
    weight_rows = (BANDS + 2) * piv + 16
    main, add_0, add_1 = pl.pallas_call(
        functools.partial(step_kernel, n_pair, own, piv, height, width),
        out_shape=(
            pltpu.VMEM(density.shape, F32),
            pltpu.VMEM((own, width), F32),
            pltpu.VMEM((own, width), F32),
        ),
        in_specs=[hbm] * 10,
        out_specs=(vmem, vmem, vmem),
        scratch_shapes=[
            pltpu.VMEM((piv, piv), F32),
            pltpu.VMEM((piv, piv), F32),
            pltpu.VMEM((piv, piv), jnp.int32),
            pltpu.VMEM((piv, piv), F32),
            pltpu.VMEM((1, piv), F32),
            pltpu.VMEM((1, piv), F32),
            pltpu.SMEM(block_rows.shape, jnp.int32),
            pltpu.SMEM(upstream.shape, jnp.int32),
            pltpu.VMEM(face_map.shape, jnp.int32),
            pltpu.VMEM((2, own, height, 128), F32),
            pltpu.VMEM((n_pair, own * 12, 128), I16),
            pltpu.VMEM((n_pair, own * 12, 128), I16),
            pltpu.VMEM((piv * 8, 128), F32),
            pltpu.VMEM((piv, 1024), F32),
            pltpu.VMEM((piv, 1024), F32),
            pltpu.VMEM((piv * 8, 128), F32),
            pltpu.VMEM((n_pair, own * 8 + 32, 128), I16),
            pltpu.VMEM((n_pair, own * 8 + 32, 128), I16),
            pltpu.VMEM((weight_rows, piv), BF16),
            pltpu.VMEM((weight_rows, 256), F32),
            pltpu.VMEM((RING, 48, width), I16),
            pltpu.VMEM((4, 80, width), I16),
            pltpu.VMEM((4, 80, width), I16),
            pltpu.VMEM((48, width), F32),
            pltpu.VMEM((own * 4, 128), F32),
            pltpu.VMEM((piv, width), F32),
            pltpu.VMEM((2, piv, 128), F32),
            pltpu.VMEM((48, 128), F32),
            pltpu.VMEM((48, 128), I16),
            pltpu.VMEM((n_pair, 48, 128), I16),
            pltpu.VMEM((piv, width), F32),
            pltpu.VMEM((piv * 8, 128), F32),
            pltpu.VMEM((piv, 128), F32),
            pltpu.VMEM((piv + 16, 128), F32),
            dma((13,)),
            dma((n_pair,)), dma((n_pair,)),
            dma((n_pair,)), dma((n_pair,)),
            dma((RING,)), dma((RING,)),
            dma((4,)), dma((4,)),
            dma((n_pair,)), dma((n_pair,)),
        ],
        compiler_params=pltpu.CompilerParams(
            collective_id=0, has_side_effects=True, vmem_limit_bytes=56 * 1024 * 1024),
    )(density, agg, share, target, frag, rate.reshape(1, piv), cour.reshape(1, piv), block_rows, upstream, face_map)
    row = lax.broadcasted_iota(jnp.int32, main.shape, 1)
    return main + jnp.where(row == 0, add_0[:, None, :], jnp.where(row == 1, add_1[:, None, :], 0.0))


def solution(mesh):
    in_specs = (P("pair", "blk", None), P(), P(), P(), P(), P(), P(), P(), P(), P("blk", None))
    out_specs = P("pair", "blk", None)
    return jax.shard_map(
        functools.partial(shards, mesh.shape["pair"]),
        mesh=mesh, in_specs=in_specs, out_specs=out_specs, check_vma=False)
```
